32 devices in a mesh: stream: 4 (over y, core), span: 8 (over z, x).
Axes of the slice: x: 2, y: 2, z: 4, core: 2. Of those that a mesh axis runs over, the one named last changes fastest.
Arguments:
- velocity_modes: bfloat16 [8, 64, 10, 3, 128], P('stream', 'span'), may hold values from -6 to 6
- cell_weight: float32 [8, 64, 10], P('stream', 'span'), may hold values from 0.001 to 0.01
Outputs:
- convection: float32 [128, 128, 128], replicated
The draws below stay inside these ranges and needn't reach their ends.
All inputs are finite; a program needn't handle non-finite values.
Results may differ from the reference program's by a relative error of at most 0.0085.
Values may be sent and summed in bfloat16 or wider, within the bound.
No kernel may reach another device: no remote copies, remote signals or barrier semaphores. Data moves between devices by JAX's collectives and lax.ppermute only.
A program may use at most 64 MiB of HBM per device.

```python
import math
import jax
import jax.numpy as jnp
from jax import lax

M = 128
NZ = 10
NX = 8
NY = 64


def levels(own_key, extent, pieces, least, largest):
    loudness = 1.0
    for position, parts in pieces:
        heights = jax.random.uniform(jax.random.fold_in(jax.random.fold_in(own_key, 6), position), (parts,), jnp.float32, least / len(pieces), largest / len(pieces))
        loudness = loudness * jnp.repeat(jnp.exp(heights), extent[position] // parts).reshape((-1,) + (1,) * (len(extent) - 1 - position))
    return loudness


def scatter_about(stream_key, dims, deviation, most, split=(), dtype=jnp.bfloat16):
    result = deviation * jax.random.normal(stream_key, dims, jnp.float32)
    if split:
        result = result * levels(stream_key, dims, split, -0.22, 0.18)
    return jnp.clip(result, -most, most).astype(dtype)


def setup_inputs(seed: int = 0) -> dict:
    key_list = jax.random.split(jax.random.key(seed), 3)
    velocity_modes = scatter_about(key_list[0], (NX, NY, NZ, 3, M), 1.0, 6.0, ((0, 4), (1, 8)))
    cell_weight = jnp.clip(jnp.exp(math.log(0.01) - 2.30258502 * jax.random.uniform(key_list[1], (NX, NY, NZ), jnp.float32) ** levels(key_list[1], (NX, NY, NZ), ((0, 4), (1, 8)), -0.2, 0.2)), 0.001, 0.01)
    return {"velocity_modes": velocity_modes, "cell_weight": cell_weight}


def gradient(padded):
    core_x = padded[:, 2:-2]
    deriv_x = (8.0 * (core_x[3:-1] - core_x[1:-3]) - (core_x[4:] - core_x[:-4])) / 12.0
    core_y = padded[2:-2]
    deriv_y = (8.0 * (core_y[:, 3:-1] - core_y[:, 1:-3]) - (core_y[:, 4:] - core_y[:, :-4])) / 12.0
    center = padded[2:-2, 2:-2]
    vertical = jnp.pad(center, ((0, 0), (0, 0), (1, 1), (0, 0), (0, 0)))
    deriv_z = 0.5 * (vertical[:, :, 2:] - vertical[:, :, :-2])
    return jnp.stack([deriv_x, deriv_y, deriv_z])


def reference(velocity_modes, cell_weight):
    phi_full = velocity_modes.astype(jnp.float32)
    padded = jnp.pad(phi_full, ((2, 2), (2, 2), (0, 0), (0, 0), (0, 0)))
    grads = gradient(padded)
    width = phi_full.shape[-1]
    plane = NY * NZ

    def add_slice(slice_index, running):
        phi_x = lax.dynamic_index_in_dim(phi_full, slice_index, 0, False).reshape(plane, 3, width)
        grad_x = lax.dynamic_index_in_dim(grads, slice_index, 1, False).reshape(3, plane, 3, width)
        weight_x = lax.dynamic_index_in_dim(cell_weight, slice_index, 0, False).reshape(plane)
        quad = jnp.einsum("cbi,acbk->acik", phi_x, grad_x, precision=lax.Precision.HIGHEST)
        quad = quad * weight_x[None, :, None, None]
        quad = lax.optimization_barrier(quad.astype(jnp.bfloat16)).astype(jnp.float32)
        return running + jnp.einsum("caj,acik->ijk", phi_x, quad, precision=lax.Precision.HIGHEST)

    zeros = jnp.zeros((width, width, width), jnp.float32)
    return lax.fori_loop(0, NX, add_slice, zeros)
```

```python
import jax
import jax.numpy as jnp
from jax import lax
from jax.sharding import PartitionSpec as P


def with_halo(cells, axis, dim, width):
    count = lax.axis_size(axis)
    ends = count - 1
    head = lax.slice_in_dim(cells, 0, width, axis=dim)
    tail = lax.slice_in_dim(cells, cells.shape[dim] - width, cells.shape[dim], axis=dim)
    return jnp.concatenate(
        [
            lax.ppermute(tail, axis, [(i, i + 1) for i in range(ends)]),
            cells,
            lax.ppermute(head, axis, [(i + 1, i) for i in range(ends)]),
        ],
        axis=dim,
    )


def gradient(padded):
    core_x = padded[:, 2:-2]
    deriv_x = (8.0 * (core_x[3:-1] - core_x[1:-3]) - (core_x[4:] - core_x[:-4])) / 12.0
    core_y = padded[2:-2]
    deriv_y = (8.0 * (core_y[:, 3:-1] - core_y[:, 1:-3]) - (core_y[:, 4:] - core_y[:, :-4])) / 12.0
    center = padded[2:-2, 2:-2]
    vertical = jnp.pad(center, ((0, 0), (0, 0), (1, 1), (0, 0), (0, 0)))
    deriv_z = 0.5 * (vertical[:, :, 2:] - vertical[:, :, :-2])
    return jnp.stack([deriv_x, deriv_y, deriv_z])


def shards(velocity_modes, cell_weight):
    streams = lax.axis_size("stream")
    me = lax.axis_index("stream")
    width = velocity_modes.shape[-1]
    wide = with_halo(velocity_modes, "span", 1, 2)
    block = lax.all_gather(wide, "stream", axis=0, tiled=True)
    weight = lax.all_gather(cell_weight, "stream", axis=0, tiled=True)
    padded = jnp.pad(block.astype(jnp.float32), ((2, 2), (0, 0), (0, 0), (0, 0), (0, 0)))
    center = block[:, 2:-2]
    cells = center.shape[0] * center.shape[1] * center.shape[2]
    grads = gradient(padded).reshape(3, cells, 3, width)
    phi = center.reshape(cells, 3, width)
    weighted = phi.astype(jnp.float32) * weight.reshape(cells, 1, 1)
    share = width // streams
    own = lax.dynamic_slice_in_dim(weighted, me * share, share, 2)
    turn = min(8, share)

    def one_block(step, result):
        mine = lax.dynamic_slice_in_dim(own, step * turn, turn, 2)
        quad = sum(
            mine[None, :, b, :, None] * grads[:, :, b, None, :] for b in range(3)
        ).astype(jnp.bfloat16)
        terms = jnp.einsum("caj,acik->ijk", phi, quad, preferred_element_type=jnp.float32)
        return lax.dynamic_update_slice_in_dim(
            result, terms.astype(jnp.bfloat16), step * turn, 0
        )

    result = jnp.zeros((share, width, width), jnp.bfloat16)
    result = lax.fori_loop(0, share // turn, one_block, result)
    rows = result.reshape(share * width, width)
    mine = lax.psum_scatter(rows, "span", scatter_dimension=0, tiled=True)
    whole = lax.all_gather(mine, ("stream", "span"), axis=0, tiled=True)
    return whole.astype(jnp.float32).reshape(width, width, width)


def solution(mesh):
    placed = (P("stream", "span", None, None, None), P("stream", "span", None))
    return jax.shard_map(shards, mesh=mesh, in_specs=placed, out_specs=P(), check_vma=False)
```

```python
import jax
import jax.numpy as jnp
from jax import lax
from jax.sharding import PartitionSpec as P


def with_halo(cells, axis, dim, width):
    count = lax.axis_size(axis)
    ends = count - 1
    head = lax.slice_in_dim(cells, 0, width, axis=dim)
    tail = lax.slice_in_dim(cells, cells.shape[dim] - width, cells.shape[dim], axis=dim)
    return jnp.concatenate(
        [
            lax.ppermute(tail, axis, [(i, i + 1) for i in range(ends)]),
            cells,
            lax.ppermute(head, axis, [(i + 1, i) for i in range(ends)]),
        ],
        axis=dim,
    )


def gradient(padded):
    core_x = padded[:, 2:-2]
    deriv_x = (8.0 * (core_x[3:-1] - core_x[1:-3]) - (core_x[4:] - core_x[:-4])) / 12.0
    core_y = padded[2:-2]
    deriv_y = (8.0 * (core_y[:, 3:-1] - core_y[:, 1:-3]) - (core_y[:, 4:] - core_y[:, :-4])) / 12.0
    center = padded[2:-2, 2:-2]
    vertical = jnp.pad(center, ((0, 0), (0, 0), (1, 1), (0, 0), (0, 0)))
    deriv_z = 0.5 * (vertical[:, :, 2:] - vertical[:, :, :-2])
    return jnp.stack([deriv_x, deriv_y, deriv_z])


def shards(velocity_modes, cell_weight):
    streams = lax.axis_size("stream")
    me = lax.axis_index("stream")
    width = velocity_modes.shape[-1]
    wide = with_halo(velocity_modes, "span", 1, 2)
    block = lax.all_gather(wide, "stream", axis=0, tiled=True)
    weight = lax.all_gather(cell_weight, "stream", axis=0, tiled=True)
    padded = jnp.pad(block.astype(jnp.float32), ((2, 2), (0, 0), (0, 0), (0, 0), (0, 0)))
    center = block[:, 2:-2]
    cells = center.shape[0] * center.shape[1] * center.shape[2]
    grads = gradient(padded).reshape(3, cells, 3, width)
    phi = center.reshape(cells, 3, width)
    weighted = phi.astype(jnp.float32) * weight.reshape(cells, 1, 1)
    share = width // streams
    own = lax.dynamic_slice_in_dim(weighted, me * share, share, 2)
    turn = min(8, share)

    def one_block(step, result):
        mine = lax.dynamic_slice_in_dim(own, step * turn, turn, 2)
        quad = sum(
            mine[None, :, b, :, None] * grads[:, :, b, None, :] for b in range(3)
        ).astype(jnp.bfloat16)
        terms = jnp.einsum("caj,acik->ijk", phi, quad, preferred_element_type=jnp.float32)
        return lax.dynamic_update_slice_in_dim(
            result, terms.astype(jnp.bfloat16), step * turn, 0
        )

    result = jnp.zeros((share, width, width), jnp.bfloat16)
    result = lax.fori_loop(0, share // turn, one_block, result)
    rows = result.reshape(share * width, width)
    spans = lax.axis_size("span")
    pieces = lax.all_to_all(rows.reshape(spans, -1, width), "span", 0, 0)
    mine = jnp.sum(pieces.astype(jnp.float32), axis=0).astype(jnp.bfloat16)
    slab = lax.all_gather(mine, "span", axis=0, tiled=True)
    whole = lax.all_gather(slab, "stream", axis=0, tiled=True)
    return whole.astype(jnp.float32).reshape(width, width, width)


def solution(mesh):
    placed = (P("stream", "span", None, None, None), P("stream", "span", None))
    return jax.shard_map(shards, mesh=mesh, in_specs=placed, out_specs=P(), check_vma=False)
```

```python
import functools

import jax
import jax.numpy as jnp
from jax import lax
from jax.experimental import pallas as pl
from jax.experimental.pallas import tpu as pltpu
from jax.sharding import Mesh, PartitionSpec as P

STREAM = ("row", "core")
SPAN = ("deck", "side")
PLANE = ("row", "core", "side")
LANES = 128


def shift_pairs(axis, by):
    count = lax.axis_size(axis)
    return [(i, i + by) for i in range(count) if 0 <= i + by < count]


def rotate(value, axis, by=1):
    count = lax.axis_size(axis)
    return lax.ppermute(value, axis, [(i, (i + by) % count) for i in range(count)])


def terms_kernel(sizes, place_ref, cells_ref, weight_ref, out_ref, grad, own, phi, quad, total):
    layers, height, across, share, chunk = sizes
    width = LANES
    shift = lax.rem(width - place_ref[0] * share, width)

    def one_layer(x, _):
        def cell(layer, z, b, first=2):
            return cells_ref[layer, z, b, first : first + across, :]

        before = [(jnp.maximum(x - s, 0), (x >= s).astype(jnp.float32)) for s in (1, 2)]
        after = [
            (jnp.minimum(x + s, layers - 1), (x < layers - s).astype(jnp.float32)) for s in (1, 2)
        ]
        for z in range(height):
            at = pl.ds(pl.multiple_of((x * height + z) * across, across), across)
            weight = weight_ref[x, z]
            for b in range(3):
                here = cell(x, z, b)
                near = cell(after[0][0], z, b) * after[0][1] - cell(before[0][0], z, b) * before[0][1]
                far = cell(after[1][0], z, b) * after[1][1] - cell(before[1][0], z, b) * before[1][1]
                grad[0, b, at, :] = (8.0 * near - far) * (1.0 / 12.0)
                near = cell(x, z, b, 3) - cell(x, z, b, 1)
                far = cell(x, z, b, 4) - cell(x, z, b, 0)
                grad[1, b, at, :] = (8.0 * near - far) * (1.0 / 12.0)
                if z == 0:
                    grad[2, b, at, :] = 0.5 * cell(x, z + 1, b)
                elif z == height - 1:
                    grad[2, b, at, :] = -0.5 * cell(x, z - 1, b)
                else:
                    grad[2, b, at, :] = 0.5 * (cell(x, z + 1, b) - cell(x, z - 1, b))
                own[b, at, :] = pltpu.roll(here * weight, shift, 1)
                phi[b, at, :] = here
        return 0

    lax.fori_loop(0, layers, one_layer, 0)
    total[...] = jnp.zeros_like(total)
    rows = 16

    def one_chunk(turn, _):
        start = pl.multiple_of(turn * chunk, chunk)
        turned = jnp.concatenate(
            [phi[a, pl.ds(start, chunk), :].T.astype(jnp.bfloat16) for a in range(3)], axis=1
        )
        for pair in range(share // 2):
            for r in range(chunk // rows):
                at = pl.ds(pl.multiple_of(start + r * rows, rows), rows)
                mine = [own[b, at, :] for b in range(3)]
                for half in range(2):
                    lane = 2 * pair + half
                    spread = [
                        jnp.broadcast_to(mine[b][:, lane : lane + 1], (rows, width))
                        for b in range(3)
                    ]
                    for a in range(3):
                        value = spread[0] * grad[a, 0, at, :]
                        value = value + spread[1] * grad[a, 1, at, :]
                        value = value + spread[2] * grad[a, 2, at, :]
                        quad[
                            a * chunk + r * rows : a * chunk + (r + 1) * rows,
                            half * width : (half + 1) * width,
                        ] = value.astype(jnp.bfloat16)
            total[pair] += jnp.dot(turned, quad[...], preferred_element_type=jnp.float32)
        return 0

    lax.fori_loop(0, layers * height * across // chunk, one_chunk, 0)
    for pair in range(share // 2):
        for half in range(2):
            i = 2 * pair + half
            out_ref[i * width : (i + 1) * width, :] = total[
                pair, :, half * width : (half + 1) * width
            ].astype(jnp.bfloat16)


def plane_terms(place, cells, weight, share):
    layers, height, _, padded, width = cells.shape
    across = padded - 4
    count = layers * height * across
    chunk = next(c for c in (256, 128, 64, 32, 16) if count % c == 0)
    kernel = functools.partial(terms_kernel, (layers, height, across, share, chunk))
    flops = 2 * share * width * width * count * 3
    return pl.pallas_call(
        kernel,
        out_shape=jax.ShapeDtypeStruct((share * width, width), jnp.bfloat16),
        in_specs=[
            pl.BlockSpec(memory_space=pltpu.SMEM),
            pl.BlockSpec(memory_space=pltpu.VMEM),
            pl.BlockSpec(memory_space=pltpu.VMEM),
        ],
        out_specs=pl.BlockSpec(memory_space=pltpu.VMEM),
        scratch_shapes=[
            pltpu.VMEM((3, 3, count, width), jnp.float32),
            pltpu.VMEM((3, count, width), jnp.float32),
            pltpu.VMEM((3, count, width), jnp.float32),
            pltpu.VMEM((3 * chunk, 2 * width), jnp.bfloat16),
            pltpu.VMEM((share // 2, width, 2 * width), jnp.float32),
        ],
        compiler_params=pltpu.CompilerParams(vmem_limit_bytes=56 * 2**20),
        cost_estimate=pl.CostEstimate(flops=flops, bytes_accessed=2**22, transcendentals=0),
    )(place, cells, weight)


def pack(velocity, weight):
    x, y, z, comps, width = velocity.shape
    rows = velocity.transpose(0, 2, 3, 1, 4).reshape(x * z * comps * y, width)
    columns = weight.transpose(1, 0, 2).reshape(y, x * z)
    parts = []
    for _ in range(3):
        part = columns.astype(jnp.bfloat16)
        columns = columns - part.astype(jnp.float32)
        parts.append(part)
    tile = jnp.concatenate(parts, axis=1)
    tile = jnp.pad(tile, ((0, 0), (0, width - tile.shape[1])))
    return jnp.concatenate([rows, tile], axis=0)


def unpack(packed, shape):
    x, y, z, comps, width = shape
    streams = packed.shape[0] // 2
    cells = x * z * comps * y
    block = packed[:, :cells].reshape(streams, 2, x, z, comps, y, width)
    block = block.transpose(0, 2, 3, 4, 1, 5, 6).reshape(streams * x, z, comps, 2 * y, width)
    tile = packed[:, cells:, : 3 * x * z].astype(jnp.float32).reshape(streams, 2, y, 3, x, z)
    weight = tile.sum(axis=3).transpose(0, 3, 4, 1, 2).reshape(streams * x, z, 2 * y)
    return block, weight


def spread_all(piece):
    rows = lax.axis_size("row")
    half = piece.shape[0] // 2
    got = {(0, 0): piece}
    got[(0, 1)] = rotate(piece, "side")
    for r in range(1, rows):
        got[(r, 0)] = rotate(piece, "row", r)
    for r in range(1, rows):
        got[(r, 1)] = (
            rotate(got[(0, 1)][:half], "row", r),
            rotate(got[(r, 0)][half:], "side"),
        )
    out = {}
    for (r, s), value in got.items():
        out[(r, 0, s)] = value
        out[(r, 1, s)] = jax.tree.map(lambda v: rotate(v, "core"), value)
    return out


def shards(velocity_modes, cell_weight):
    shape = velocity_modes.shape
    width = shape[-1]
    rows, decks = lax.axis_size("row"), lax.axis_size("deck")
    members = rows * 4
    share = width // members
    row, core, side = (lax.axis_index(a) for a in PLANE)
    place = (row * 2 + core) * 2 + side

    packed = lax.all_gather(pack(velocity_modes, cell_weight), PLANE, axis=0, tiled=False)
    block, weight = unpack(packed, shape)
    below = lax.ppermute(block[..., -2:, :], "deck", shift_pairs("deck", 1))
    above = lax.ppermute(block[..., :2, :], "deck", shift_pairs("deck", -1))
    cells = jnp.concatenate([below, block, above], axis=3).astype(jnp.float32)
    spread_weight = jnp.broadcast_to(weight[..., None], weight.shape + (width,))
    terms = plane_terms(place.reshape(1).astype(jnp.int32), cells, spread_weight, share)

    parts = lax.all_to_all(terms.reshape(decks, -1, width), "deck", 0, 0)
    mine = jnp.sum(parts.astype(jnp.float32), axis=0).astype(jnp.bfloat16)
    piece = lax.all_gather(mine, "deck", axis=0, tiled=True)

    result = jnp.zeros((members * share * width, width), jnp.float32)
    for (r, c, s), value in spread_all(piece).items():
        source = (lax.rem(row - r + rows, rows) * 2 + lax.rem(core + c, 2)) * 2 + lax.rem(side + s, 2)
        start = source * share * width
        for part in value if isinstance(value, tuple) else (value,):
            result = lax.dynamic_update_slice(result, part.astype(jnp.float32), (start, 0))
            start = start + part.shape[0]
    return result.reshape(width, width, width)


def solution(mesh):
    streams, spans = (mesh.shape[name] for name in ("stream", "span"))
    split = Mesh(mesh.devices.reshape(streams // 2, 2, spans // 2, 2), STREAM + SPAN)
    placed = (P(STREAM, SPAN, None, None, None), P(STREAM, SPAN, None))
    return jax.shard_map(shards, mesh=split, in_specs=placed, out_specs=P(), check_vma=False)
```

```python
import functools

import jax
import jax.numpy as jnp
from jax import lax
from jax.experimental import pallas as pl
from jax.experimental.pallas import tpu as pltpu
from jax.sharding import Mesh, PartitionSpec as P

STREAM = ("row", "core")
SPAN = ("deck", "side")
DIAGONAL = ("row", "side")
WEIGHT_PARTS = 3
VMEM_LIMIT = 56 * 2**20


def rotate(value, axis, by=1):
    count = lax.axis_size(axis)
    return lax.ppermute(value, axis, [(i, (i + by) % count) for i in range(count)])


def terms_kernel(sizes, place_ref, *refs):
    layers, height, across, width, share, members = sizes
    pieces, out_ref = refs[:members], refs[members]
    field, grad, own, tall, turned, quad, total = refs[members + 1 :]
    cells = layers * height * across
    slab = 2 * cells
    depth = quad.shape[1]
    streams = members // 2
    shift = place_ref[0]

    for n, piece in enumerate(pieces):
        field[place_ref[1 + n]] = piece[...].astype(jnp.float32)

    index = lax.broadcasted_iota(jnp.int32, (across, width), 0)

    def column(b):
        return slice(b * width, (b + 1) * width)

    def one_stream(s, _):
        def layer_at(layer, side):
            at = s * layers + layer
            inside = ((at >= 0) & (at < streams * layers)).astype(jnp.float32)
            at = jnp.clip(at, 0, streams * layers - 1)
            return lax.div(at, layers) * 2 + side, lax.rem(at, layers), inside

        for side in range(2):
            member = 2 * s + side
            tile = field[member, cells + 2 * layers * height :, 0:width]
            weights = tile
            for part in range(1, WEIGHT_PARTS):
                weights = weights + pltpu.roll(tile, width - part * layers * height, 1)
            for layer in range(layers):
                beside = {step: layer_at(layer + step, side) for step in (-2, -1, 1, 2)}
                for z in range(height):
                    line = layer * height + z
                    row = line * across
                    rows = slice(row, row + across)
                    at = pl.ds(pl.multiple_of(member * cells + row, across), across)
                    weight = jnp.broadcast_to(weights[:, line : line + 1], (across, width))
                    first = cells + 2 * line
                    base = first // across * across
                    for b in range(3):
                        here = field[member, rows, column(b)]
                        along = {}
                        for step, (m, l, inside) in beside.items():
                            start = pl.multiple_of((l * height + z) * across, across)
                            along[step] = field[m, pl.ds(start, across), column(b)] * inside
                        value = 8.0 * (along[1] - along[-1]) - (along[2] - along[-2])
                        grad[0, at, column(b)] = value * (1.0 / 12.0)

                        outer = field[member, base : base + across, column(b)]
                        if side == 0:
                            prev = pltpu.roll(outer, (across - 2 - (first - base)) % across, 0)
                            after = field[member + 1, rows, column(b)]
                        else:
                            prev = field[member - 1, rows, column(b)]
                            after = pltpu.roll(outer, (across - (first - base)) % across, 0)
                        near = pltpu.roll(jnp.where(index < 1, after, here), across - 1, 0)
                        near = near - pltpu.roll(jnp.where(index >= across - 1, prev, here), 1, 0)
                        far = pltpu.roll(jnp.where(index < 2, after, here), across - 2, 0)
                        far = far - pltpu.roll(jnp.where(index >= across - 2, prev, here), 2, 0)
                        grad[1, at, column(b)] = (8.0 * near - far) * (1.0 / 12.0)

                        value = jnp.zeros_like(here)
                        if z < height - 1:
                            value = field[member, row + across : row + 2 * across, column(b)]
                        if z > 0:
                            value = value - field[member, row - across : row, column(b)]
                        grad[2, at, column(b)] = 0.5 * value
                        own[at, column(b)] = pltpu.roll(here * weight, shift, 1)
            for a in range(3):
                start = a * slab + side * cells
                tall[start : start + cells, :] = field[member, :cells, column(a)]
        if depth > 3 * slab:
            tall[3 * slab :, :] = jnp.zeros((depth - 3 * slab, width), jnp.float32)
        turned[s] = tall[...].T.astype(jnp.bfloat16)
        return 0

    lax.fori_loop(0, streams, one_stream, 0)
    total[...] = jnp.zeros_like(total)
    if depth > 3 * slab:
        quad[:, 3 * slab :, :] = jnp.zeros((2, depth - 3 * slab, 2 * width), jnp.bfloat16)
    rows = 16

    def one_slab(s, _):
        for pair in range(share // 2):
            for r in range(slab // rows):
                at = pl.ds(pl.multiple_of(s * slab + r * rows, rows), rows)
                mine = [own[at, column(b)] for b in range(3)]
                for half in range(2):
                    lane = 2 * pair + half
                    spread = [
                        jnp.broadcast_to(mine[b][:, lane : lane + 1], (rows, width))
                        for b in range(3)
                    ]
                    for a in range(3):
                        value = spread[0] * grad[a, at, column(0)]
                        value = value + spread[1] * grad[a, at, column(1)]
                        value = value + spread[2] * grad[a, at, column(2)]
                        start = a * slab + r * rows
                        quad[pair % 2, start : start + rows, column(half)] = value.astype(
                            jnp.bfloat16
                        )
            total[pair] += jnp.dot(
                turned[s], quad[pair % 2], preferred_element_type=jnp.float32
            )
        return 0

    lax.fori_loop(0, streams, one_slab, 0)
    for pair in range(share // 2):
        for half in range(2):
            start = (2 * pair + half) * width
            out_ref[start : start + width, :] = total[pair, :, column(half)].astype(jnp.bfloat16)


def plane_terms(place, pieces, shape, share):
    layers, across, height, comps, width = shape
    members = len(pieces)
    cells = layers * height * across
    count = members * cells
    depth = pl.cdiv(3 * 2 * cells, 256) * 256
    sizes = (layers, height, across, width, share, members)
    vmem = pl.BlockSpec(memory_space=pltpu.VMEM)
    return pl.pallas_call(
        functools.partial(terms_kernel, sizes),
        out_shape=jax.ShapeDtypeStruct((share * width, width), jnp.bfloat16),
        in_specs=[pl.BlockSpec(memory_space=pltpu.SMEM)] + [vmem] * members,
        out_specs=vmem,
        scratch_shapes=[
            pltpu.VMEM((members,) + pieces[0].shape, jnp.float32),
            pltpu.VMEM((3, count, comps * width), jnp.float32),
            pltpu.VMEM((count, comps * width), jnp.float32),
            pltpu.VMEM((depth, width), jnp.float32),
            pltpu.VMEM((members // 2, width, depth), jnp.bfloat16),
            pltpu.VMEM((2, depth, 2 * width), jnp.bfloat16),
            pltpu.VMEM((share // 2, width, 2 * width), jnp.float32),
        ],
        compiler_params=pltpu.CompilerParams(vmem_limit_bytes=VMEM_LIMIT),
        cost_estimate=pl.CostEstimate(
            flops=2 * share * width * width * count * 3, bytes_accessed=2**22, transcendentals=0
        ),
    )(place, *pieces)


def place_kernel(pieces, given, start_ref, *refs):
    out_ref, wide, sems = refs[pieces + given :]
    copies = []
    done = 0
    for n, piece in enumerate(refs[:pieces]):
        rows = piece.shape[0]
        here = wide.at[done : done + rows]
        here[...] = piece[...].astype(jnp.float32)
        to = pl.ds(pl.multiple_of(start_ref[n], rows), rows)
        copies.append(pltpu.make_async_copy(here, out_ref.at[to], sems.at[n]))
        copies[-1].start()
        done += rows
    for copy in copies:
        copy.wait()


def put(result, total_rows, pieces, starts):
    width = pieces[0].shape[1]
    given = [] if result is None else [result]
    rows = sum(piece.shape[0] for piece in pieces)
    vmem, anywhere = (pl.BlockSpec(memory_space=m) for m in (pltpu.VMEM, pl.ANY))
    return pl.pallas_call(
        functools.partial(place_kernel, len(pieces), len(given)),
        out_shape=jax.ShapeDtypeStruct((total_rows, width), jnp.float32),
        in_specs=[pl.BlockSpec(memory_space=pltpu.SMEM)]
        + [vmem] * len(pieces)
        + [anywhere] * len(given),
        out_specs=anywhere,
        scratch_shapes=[
            pltpu.VMEM((rows, width), jnp.float32),
            pltpu.SemaphoreType.DMA((len(pieces),)),
        ],
        input_output_aliases={1 + len(pieces): 0} if given else {},
        compiler_params=pltpu.CompilerParams(vmem_limit_bytes=VMEM_LIMIT),
        cost_estimate=pl.CostEstimate(
            flops=0, bytes_accessed=6 * rows * width, transcendentals=0
        ),
    )(jnp.stack(starts).astype(jnp.int32), *pieces, *given)


def pack(velocity, weight):
    x, y, z, comps, width = velocity.shape
    side = lax.axis_index("side")
    decks = lax.axis_size("deck")
    edge = jnp.where(side == 1, velocity[:, y - 2 :], velocity[:, :2])
    joints = [(2 * d + 1, 2 * d + 2) for d in range(decks - 1)]
    outer = lax.ppermute(edge, SPAN, joints + [(j, i) for i, j in joints])
    columns = weight.transpose(1, 0, 2).reshape(y, x * z)
    parts = []
    for _ in range(WEIGHT_PARTS):
        part = lax.reduce_precision(columns, 8, 7)
        columns = columns - part
        parts.append(part.astype(jnp.bfloat16))
    tile = jnp.concatenate(parts, axis=1)
    tile = jnp.pad(tile, ((0, 0), (0, comps * width - tile.shape[1])))
    rows = [v.transpose(0, 2, 1, 3, 4).reshape(-1, comps * width) for v in (velocity, outer)]
    return jnp.concatenate(rows + [tile], axis=0)


def spread_small(piece):
    rows = lax.axis_size("row")
    got = {(0, 0): piece, (0, 1): rotate(piece, "side")}
    for r in range(1, rows):
        got[(r, 0)] = rotate(piece, "row", r)
        pairs = [
            (2 * i + s, 2 * ((i + r) % rows) + 1 - s) for i in range(rows) for s in range(2)
        ]
        got[(r, 1)] = lax.ppermute(piece, DIAGONAL, pairs)
    out = {}
    for (r, s), value in got.items():
        out[(r, 0, s)] = value
        out[(r, 1, s)] = rotate(value, "core")
    return out


def spread_all(piece):
    rows = lax.axis_size("row")
    half = piece.shape[0] // 2
    got = {(0, 0): (piece,), (0, 1): (rotate(piece, "side"),)}
    for r in range(1, rows):
        got[(r, 0)] = (rotate(piece, "row", r),)
    for r in range(1, rows):
        got[(r, 1)] = (
            rotate(got[(0, 1)][0][:half], "row", r),
            rotate(got[(r, 0)][0][half:], "side"),
        )
    out = {}
    for (r, s), value in got.items():
        out[(r, 0, s)] = value
        out[(r, 1, s)] = tuple(rotate(v, "core") for v in value)
    return out


def shards(velocity_modes, cell_weight):
    shape = velocity_modes.shape
    width = shape[-1]
    rows, decks = lax.axis_size("row"), lax.axis_size("deck")
    members = rows * 4
    share = width // members
    row, core, side = (lax.axis_index(a) for a in ("row", "core", "side"))

    def member(r, c, s):
        return (lax.rem(row - r + rows, rows) * 2 + lax.rem(core + c, 2)) * 2 + lax.rem(side + s, 2)

    pieces = spread_small(pack(velocity_modes, cell_weight))
    shift = lax.rem(width - member(0, 0, 0) * share, width)
    place = jnp.stack([shift] + [member(*offsets) for offsets in pieces]).astype(jnp.int32)
    terms = plane_terms(place, list(pieces.values()), shape, share)

    parts = lax.all_to_all(terms.reshape(decks, -1, width), "deck", 0, 0)
    mine = jnp.sum(parts.astype(jnp.float32), axis=0).astype(jnp.bfloat16)
    piece = lax.all_gather(mine, "deck", axis=0, tiled=True)

    result = None
    block = share * width
    got = spread_all(piece)
    for s, r in sorted({(s, r) for r, _, s in got}):
        values, starts = [], []
        for c in range(2):
            start = member(r, c, s) * block
            for value in got[(r, c, s)]:
                values.append(value)
                starts.append(start)
                start = start + value.shape[0]
        result = put(result, members * block, values, starts)
    return result.reshape(width, width, width)


def solution(mesh):
    streams, spans = (mesh.shape[name] for name in ("stream", "span"))
    split = Mesh(mesh.devices.reshape(streams // 2, 2, spans // 2, 2), STREAM + SPAN)
    placed = (P(STREAM, SPAN, None, None, None), P(STREAM, SPAN, None))
    return jax.shard_map(shards, mesh=split, in_specs=placed, out_specs=P(), check_vma=False)
```

```python
import functools

import jax
import jax.numpy as jnp
from jax import lax
from jax.experimental import pallas as pl
from jax.experimental.pallas import tpu as pltpu
from jax.sharding import Mesh, PartitionSpec as P

STREAM = ("row", "core")
SPAN = ("deck", "side")
DIAGONAL = ("row", "side")
WEIGHT_PARTS = 3
VMEM_LIMIT = 56 * 2**20
LANES = 128
CHUNKS = 2
TURNED = (((1,), (1,)), ((), ()))


def rotate(value, axis, by=1):
    count = lax.axis_size(axis)
    return lax.ppermute(value, axis, [(i, (i + by) % count) for i in range(count)])


def transposed(value):
    rows = value.shape[1]
    row, column = (lax.broadcasted_iota(jnp.int32, (rows, rows), d) for d in range(2))
    eye = (row == column).astype(jnp.bfloat16)
    return lax.dot_general(eye, value, TURNED, preferred_element_type=jnp.float32)


def terms_kernel(sizes, place_ref, *refs):
    layers, height, across, width, share, members, outs = sizes
    pieces, out_refs = refs[:members], refs[members : members + outs]
    field, flat, grad, phi, phi_wide, grad_turned, own, quad = refs[members + outs :]
    cells = layers * height * across
    count = members * cells
    streams = members // 2
    span = grad.shape[1]
    together = span // (2 * cells)

    for n, piece in enumerate(pieces):
        field[place_ref[2 + n]] = piece[...].astype(jnp.float32)

    index = lax.broadcasted_iota(jnp.int32, (across, width), 0)

    def column(b):
        return slice(b * width, (b + 1) * width)

    def one_stream(s, group):
        def layer_at(layer, side):
            at = s * layers + layer
            inside = ((at >= 0) & (at < streams * layers)).astype(jnp.float32)
            at = jnp.clip(at, 0, streams * layers - 1)
            return lax.div(at, layers) * 2 + side, lax.rem(at, layers), inside

        for side in range(2):
            member = 2 * s + side
            tile = field[member, cells + 2 * layers * height :, 0:width]
            weights = tile
            for part in range(1, WEIGHT_PARTS):
                weights = weights + pltpu.roll(tile, width - part * layers * height, 1)
            for layer in range(layers):
                beside = {step: layer_at(layer + step, side) for step in (-2, -1, 1, 2)}
                for z in range(height):
                    line = layer * height + z
                    row = line * across
                    rows = slice(row, row + across)
                    at = (s - group * together) * 2 + side
                    at = pl.ds(pl.multiple_of(at * cells + row, across), across)
                    weight = jnp.broadcast_to(weights[:, line : line + 1], (across, width))
                    twelfth, half = weight * (1.0 / 12.0), weight * 0.5
                    first = cells + 2 * line
                    base = first // across * across
                    for b in range(3):
                        here = field[member, rows, column(b)]
                        along = {}
                        for step, (m, l, inside) in beside.items():
                            start = pl.multiple_of((l * height + z) * across, across)
                            along[step] = field[m, pl.ds(start, across), column(b)] * inside
                        value = 8.0 * (along[1] - along[-1]) - (along[2] - along[-2])
                        grad[0, at, column(b)] = value * twelfth

                        outer = field[member, base : base + across, column(b)]
                        if side == 0:
                            prev = pltpu.roll(outer, (across - 2 - (first - base)) % across, 0)
                            after = field[member + 1, rows, column(b)]
                        else:
                            prev = field[member - 1, rows, column(b)]
                            after = pltpu.roll(outer, (across - (first - base)) % across, 0)
                        near = pltpu.roll(jnp.where(index < 1, after, here), across - 1, 0)
                        near = near - pltpu.roll(jnp.where(index >= across - 1, prev, here), 1, 0)
                        far = pltpu.roll(jnp.where(index < 2, after, here), across - 2, 0)
                        far = far - pltpu.roll(jnp.where(index >= across - 2, prev, here), 2, 0)
                        grad[1, at, column(b)] = (8.0 * near - far) * twelfth

                        value = jnp.zeros_like(here)
                        if z < height - 1:
                            value = field[member, row + across : row + 2 * across, column(b)]
                        if z > 0:
                            value = value - field[member, row - across : row, column(b)]
                        grad[2, at, column(b)] = value * half
                        flat[at, column(b)] = here
        return group

    def one_group(group, _):
        lax.fori_loop(group * together, (group + 1) * together, one_stream, group)
        start = pl.multiple_of(group * span, LANES)
        lanes = pl.ds(start, span)
        for b in range(3):
            value = transposed(flat[:, column(b)].astype(jnp.bfloat16))
            phi_wide[b, :, lanes] = value
            phi[:, pl.ds(pl.multiple_of(b * count + start, LANES), span)] = value.astype(jnp.bfloat16)
            for a in range(3):
                value = transposed(grad[a, :, column(b)].astype(jnp.bfloat16))
                grad_turned[a, b, :, lanes] = value.astype(jnp.bfloat16)
        return 0

    lax.fori_loop(0, streams // together, one_group, 0)

    rows = 16
    for i in range(share):
        mode = place_ref[0] + lax.rem(i + place_ref[1], share)
        for b in range(3):
            row = phi_wide[b, pl.ds(mode, 1), :]
            own[b, i] = jnp.broadcast_to(row, (rows, count)).astype(jnp.bfloat16)

    for pair in range(share // 2):
        for a in range(3):
            for start in range(0, count, LANES):
                lanes = slice(start, start + LANES)
                spread = [[own[b, 2 * pair + h, :, lanes] for b in range(3)] for h in range(2)]
                for k in range(0, width, rows):
                    slope = [grad_turned[a, b, k : k + rows, lanes] for b in range(3)]
                    for h in range(2):
                        value = spread[h][0] * slope[0]
                        value = value + spread[h][1] * slope[1]
                        value = value + spread[h][2] * slope[2]
                        quad[
                            pair % 2,
                            h * width + k : h * width + k + rows,
                            a * count + start : a * count + start + LANES,
                        ] = value
        total = lax.dot_general(
            phi[...], quad[pair % 2], TURNED, preferred_element_type=jnp.float32
        )
        for h in range(2):
            start = (2 * pair + h) * width
            out_ref = out_refs[start * outs // (share * width)]
            start = start % (share * width // outs)
            out_ref[start : start + width, :] = total[:, column(h)].astype(out_ref.dtype)


def plane_terms(place, pieces, shape, share, outs):
    layers, across, height, comps, width = shape
    members = len(pieces)
    cells = layers * height * across
    count = members * cells
    span = next(n * 2 * cells for n in (1, 2, 4, members // 2) if n * 2 * cells % LANES == 0)
    sizes = (layers, height, across, width, share, members, outs)
    vmem = pl.BlockSpec(memory_space=pltpu.VMEM)
    dtypes = [jnp.float32 if outs > 1 and n == 0 else jnp.bfloat16 for n in range(outs)]
    return pl.pallas_call(
        functools.partial(terms_kernel, sizes),
        out_shape=[jax.ShapeDtypeStruct((share * width // outs, width), t) for t in dtypes],
        in_specs=[pl.BlockSpec(memory_space=pltpu.SMEM)] + [vmem] * members,
        out_specs=[vmem] * outs,
        scratch_shapes=[
            pltpu.VMEM((members,) + pieces[0].shape, jnp.float32),
            pltpu.VMEM((span, comps * width), jnp.float32),
            pltpu.VMEM((3, span, comps * width), jnp.float32),
            pltpu.VMEM((width, 3 * count), jnp.bfloat16),
            pltpu.VMEM((3, width, count), jnp.float32),
            pltpu.VMEM((3, 3, width, count), jnp.bfloat16),
            pltpu.VMEM((3, share, 16, count), jnp.bfloat16),
            pltpu.VMEM((min(2, share // 2), 2 * width, 3 * count), jnp.bfloat16),
        ],
        compiler_params=pltpu.CompilerParams(vmem_limit_bytes=VMEM_LIMIT),
        cost_estimate=pl.CostEstimate(
            flops=2 * share * width * width * count * 3, bytes_accessed=2**22, transcendentals=0
        ),
    )(place, *pieces)


def place_kernel(runs, pieces, given, start_ref, *refs):
    out_ref, wide, sems = refs[pieces + given :]
    copies = []
    done = 0
    for n, (piece, first, rows) in enumerate(runs):
        here = wide.at[done : done + rows]
        here[...] = refs[piece][first : first + rows, :].astype(jnp.float32)
        to = pl.ds(pl.multiple_of(start_ref[n], rows), rows)
        copies.append(pltpu.make_async_copy(here, out_ref.at[to], sems.at[n]))
        copies[-1].start()
        done += rows
    for copy in copies:
        copy.wait()


def put(result, total_rows, values, starts):
    pieces = list({id(value): value for value, _, _ in values}.values())
    place = {id(piece): n for n, piece in enumerate(pieces)}
    runs = [(place[id(value)], first, rows) for value, first, rows in values]
    width = pieces[0].shape[1]
    given = [] if result is None else [result]
    rows = sum(run[2] for run in runs)
    vmem, anywhere = (pl.BlockSpec(memory_space=m) for m in (pltpu.VMEM, pl.ANY))
    return pl.pallas_call(
        functools.partial(place_kernel, runs, len(pieces), len(given)),
        out_shape=jax.ShapeDtypeStruct((total_rows, width), jnp.float32),
        in_specs=[pl.BlockSpec(memory_space=pltpu.SMEM)]
        + [vmem] * len(pieces)
        + [anywhere] * len(given),
        out_specs=anywhere,
        scratch_shapes=[
            pltpu.VMEM((rows, width), jnp.float32),
            pltpu.SemaphoreType.DMA((len(runs),)),
        ],
        input_output_aliases={1 + len(pieces): 0} if given else {},
        compiler_params=pltpu.CompilerParams(vmem_limit_bytes=VMEM_LIMIT),
        cost_estimate=pl.CostEstimate(
            flops=0, bytes_accessed=6 * rows * width, transcendentals=0
        ),
    )(jnp.stack(starts).astype(jnp.int32), *pieces, *given)


def pack(velocity, weight):
    x, y, z, comps, width = velocity.shape
    side = lax.axis_index("side")
    decks = lax.axis_size("deck")
    edge = jnp.where(side == 1, velocity[:, y - 2 :], velocity[:, :2])
    joints = [(2 * d + 1, 2 * d + 2) for d in range(decks - 1)]
    outer = lax.ppermute(edge, SPAN, joints + [(j, i) for i, j in joints])
    columns = weight.transpose(1, 0, 2).reshape(y, x * z)
    parts = []
    for _ in range(WEIGHT_PARTS):
        part = lax.reduce_precision(columns, 8, 7)
        columns = columns - part
        parts.append(part.astype(jnp.bfloat16))
    tile = jnp.concatenate(parts, axis=1)
    tile = jnp.pad(tile, ((0, 0), (0, comps * width - tile.shape[1])))
    rows = [v.transpose(0, 2, 1, 3, 4).reshape(-1, comps * width) for v in (velocity, outer)]
    return jnp.concatenate(rows + [tile], axis=0)


def spread_small(piece):
    rows = lax.axis_size("row")
    got = {(0, 0): piece, (0, 1): rotate(piece, "side")}
    for r in range(1, rows):
        got[(r, 0)] = rotate(piece, "row", r)
        pairs = [
            (2 * i + s, 2 * ((i + r) % rows) + 1 - s) for i in range(rows) for s in range(2)
        ]
        got[(r, 1)] = lax.ppermute(piece, DIAGONAL, pairs)
    out = {}
    for (r, s), value in got.items():
        out[(r, 0, s)] = value
        out[(r, 1, s)] = rotate(value, "core")
    return out


def sum_over_decks(terms, decks):
    if len(terms) > 1:
        parts = [terms[0]] + [rotate(terms[r], "deck", r) for r in range(1, decks)]
    else:
        width = terms[0].shape[1]
        parts = list(lax.all_to_all(terms[0].reshape(decks, -1, width), "deck", 0, 0))
    return sum(part.astype(jnp.float32) for part in parts).astype(jnp.bfloat16)


def shards(velocity_modes, cell_weight):
    shape = velocity_modes.shape
    width = shape[-1]
    rows, decks = lax.axis_size("row"), lax.axis_size("deck")
    members = rows * 4
    share = width // members
    part = share // CHUNKS
    row, core, side, deck = (lax.axis_index(a) for a in ("row", "core", "side", "deck"))
    outs = decks if part % (2 * decks) == 0 else 1

    def member(r, c, s):
        return (lax.rem(row - r + rows, rows) * 2 + lax.rem(core + c, 2)) * 2 + lax.rem(side + s, 2)

    pieces = spread_small(pack(velocity_modes, cell_weight))
    sources = [member(*offsets) for offsets in pieces]
    first = deck * (part // decks) if outs > 1 else jnp.zeros_like(deck)
    terms = []
    for n in range(CHUNKS):
        start = member(0, 0, 0) * share + n * part
        place = jnp.stack([start, first] + sources).astype(jnp.int32)
        terms.append(plane_terms(place, list(pieces.values()), shape, part, outs))

    block = part * width
    line = block // decks
    result = None

    def put_all(result, n, chosen):
        values, starts = [], []
        for (r, c, s), value in chosen:
            start = (member(r, c, s) * CHUNKS + n) * block
            for d in range(decks):
                values.append((value, d * line, line))
                starts.append(start + lax.rem(deck - d + decks, decks) * line)
        return put(result, members * share * width, values, starts)

    waiting = []
    for n in range(CHUNKS):
        mine = sum_over_decks(terms[n], decks)
        piece = jnp.concatenate([mine] + [rotate(mine, "deck", r) for r in range(1, decks)], axis=0)
        across = rotate(piece, "side")
        along = [rotate(piece, "row", r) for r in range(1, rows)]
        near = [((0, 0, 0), piece), ((0, 0, 1), across)]
        near += [((r, 0, 0), v) for r, v in enumerate(along, 1)]
        if n == 0:
            diagonal = [rotate(across, "row", r) for r in range(1, rows)]
        else:
            along, result = lax.optimization_barrier((along, put_all(result, *waiting.pop(0))))
            diagonal = [rotate(v, "side") for v in along]
        near_core = [((r, 1, s), rotate(v, "core")) for (r, _, s), v in near]
        waiting.append((n, near + near_core))
        far = [((r, 0, 1), v) for r, v in enumerate(diagonal, 1)]
        if n == CHUNKS - 1:
            for group in waiting:
                result = put_all(result, *group)
            waiting = []
            far_values, result = lax.optimization_barrier(([v for _, v in far], result))
            far = [(o, v) for (o, _), v in zip(far, far_values)]
        far_core = [((r, 1, s), rotate(v, "core")) for (r, _, s), v in far]
        waiting.append((n, far + far_core))
    for group in waiting:
        result = put_all(result, *group)
    return result.reshape(width, width, width)


def solution(mesh):
    streams, spans = (mesh.shape[name] for name in ("stream", "span"))
    split = Mesh(mesh.devices.reshape(streams // 2, 2, spans // 2, 2), STREAM + SPAN)
    placed = (P(STREAM, SPAN, None, None, None), P(STREAM, SPAN, None))
    return jax.shard_map(shards, mesh=split, in_specs=placed, out_specs=P(), check_vma=False)
```

```python
import functools
import math

import jax
import jax.numpy as jnp
from jax import lax
from jax.experimental import pallas as pl
from jax.experimental.pallas import tpu as pltpu
from jax.sharding import Mesh, PartitionSpec as P

STREAM = ("row", "core")
SPAN = ("deck", "side")
DIAGONAL = ("row", "side")
WEIGHT_PARTS = 3
LANES = 128
TILE = 16
CHUNKS = 2
TURNED = (((1,), (1,)), ((), ()))


def rotate(value, axis, by=1):
    count = lax.axis_size(axis)
    return lax.ppermute(value, axis, [(i, (i + by) % count) for i in range(count)])


def member(where, rows, offsets):
    r, c, s = offsets
    row = lax.rem(where[0] - r + rows, rows)
    return (row * 2 + lax.rem(where[1] + c, 2)) * 2 + lax.rem(where[2] + s, 2)


def grant(shapes, slack=6 * 2**20):
    total = slack
    for shape, dtype in shapes:
        *outer, rows, columns = shape
        size = jnp.dtype(dtype).itemsize
        rows, columns = pl.cdiv(rows, TILE) * TILE, pl.cdiv(columns, LANES) * LANES
        total += math.prod(outer) * rows * columns * size
    return total


def terms_kernel(sizes, offsets, where_ref, *refs):
    layers, height, across, width, share, chunk, rows, decks, outs = sizes
    members = len(offsets)
    blocks, edges = refs[:members], refs[members : 2 * members]
    out_refs = refs[2 * members : 2 * members + outs]
    field, edge, source, turned, phi, own, even, odd, total = refs[2 * members + outs :]
    slab = layers * height * across
    count = members * slab
    span = source.shape[2]
    group_layers = span // (2 * height * across)

    for n in range(members):
        at = member(where_ref, rows, offsets[n])
        field[at] = blocks[n][...].astype(jnp.float32)
        edge[at] = edges[n][...].astype(jnp.float32)

    index = lax.broadcasted_iota(jnp.int32, (across, width), 0)
    line_rows = 2 * height
    weight_row = edge.shape[2] - across

    def one_layer(x, first_layer):
        stream, layer = lax.div(x, layers), lax.rem(x, layers)

        def layer_at(step, side):
            at = x + step
            inside = ((at >= 0) & (at < members // 2 * layers)).astype(jnp.float32)
            at = jnp.clip(at, 0, members // 2 * layers - 1)
            return lax.div(at, layers) * 2 + side, lax.rem(at, layers), inside

        for side in range(2):
            here_at = 2 * stream + side
            tile = edge[here_at, layer, weight_row:, 0:width]
            weights = tile
            for part in range(1, WEIGHT_PARTS):
                weights = weights + pltpu.roll(tile, width - part * height, 1)
            beside = {step: layer_at(step, side) for step in (-2, -1, 1, 2)}
            for z in range(height):
                at = ((x - first_layer) * 2 + side) * height + z
                at = pl.ds(pl.multiple_of(at * across, across), across)
                weight = jnp.broadcast_to(weights[:, z : z + 1], (across, width))
                twelfth, half = weight * (1.0 / 12.0), weight * 0.5
                base = 2 * z // across * across
                for b in range(3):
                    here = field[here_at, layer, z, b]
                    source[0, b, at, :] = here
                    along = {
                        step: field[m, l, z, b] * inside for step, (m, l, inside) in beside.items()
                    }
                    value = 8.0 * (along[1] - along[-1]) - (along[2] - along[-2])
                    source[1, b, at, :] = value * twelfth

                    outer = edge[here_at, layer, base : base + across, b * width : (b + 1) * width]
                    beyond = field[here_at + 1 - 2 * side, layer, z, b]
                    if side == 0:
                        prev = pltpu.roll(outer, (across - 2 - (2 * z - base)) % across, 0)
                        after = beyond
                    else:
                        prev = beyond
                        after = pltpu.roll(outer, (across - (2 * z - base)) % across, 0)
                    near = pltpu.roll(jnp.where(index < 1, after, here), across - 1, 0)
                    near = near - pltpu.roll(jnp.where(index >= across - 1, prev, here), 1, 0)
                    far = pltpu.roll(jnp.where(index < 2, after, here), across - 2, 0)
                    far = far - pltpu.roll(jnp.where(index >= across - 2, prev, here), 2, 0)
                    source[2, b, at, :] = (8.0 * near - far) * twelfth

                    value = jnp.zeros_like(here)
                    if z < height - 1:
                        value = field[here_at, layer, z + 1, b]
                    if z > 0:
                        value = value - field[here_at, layer, z - 1, b]
                    source[3, b, at, :] = value * half
        return first_layer

    tall = width + share * TILE
    row, column = (lax.broadcasted_iota(jnp.int32, (tall, width), d) for d in range(2))
    mode = lax.div(row - width, TILE) + (
        where_ref[3] * (share // decks) if outs > 1 else 0
    )
    mode = jnp.where(mode >= share, mode - share, mode)
    mode = mode + (member(where_ref, rows, (0, 0, 0)) * CHUNKS + chunk) * share
    pick = (column == jnp.where(row < width, row, mode)).astype(jnp.bfloat16)
    eye = pick[:width]

    def one_group(group, _):
        first_layer = group * group_layers
        lax.fori_loop(first_layer, first_layer + group_layers, one_layer, first_layer)
        lanes = pl.ds(pl.multiple_of(group * span, LANES), span)

        def turn_phi(b, _):
            value = source[0, b].astype(jnp.bfloat16)
            value = lax.dot_general(pick, value, TURNED, preferred_element_type=jnp.float32)
            value = value.astype(jnp.bfloat16)
            phi[b, :, lanes] = value[:width]
            own[b, :, lanes] = value[width:]
            return 0

        def turn_slope(unit, _):
            a, b = lax.div(unit, 3), lax.rem(unit, 3)
            value = source[1 + a, b].astype(jnp.bfloat16)
            value = lax.dot_general(eye, value, TURNED, preferred_element_type=jnp.float32)
            turned[a, b, :, lanes] = value.astype(jnp.bfloat16)
            return 0

        lax.fori_loop(0, 3, turn_phi, 0)
        lax.fori_loop(0, 9, turn_slope, 0)
        return 0

    lax.fori_loop(0, count // span, one_group, 0)

    def build(unit, quad):
        pair, a = lax.div(unit, 3), lax.rem(unit, 3)
        for start in range(0, count, LANES):
            lanes = slice(start, start + LANES)
            spread = [
                [
                    own[b, pl.ds(pl.multiple_of((2 * pair + h) * TILE, TILE), TILE), lanes]
                    for b in range(3)
                ]
                for h in range(2)
            ]
            for k in range(0, width, TILE):
                slope = [turned[a, b, k : k + TILE, lanes] for b in range(3)]
                for h in range(2):
                    value = spread[h][0] * slope[0]
                    value = value + spread[h][1] * slope[1]
                    value = value + spread[h][2] * slope[2]
                    quad[h * width + k : h * width + k + TILE, lanes] = value

    def contract(unit, quad):
        pair, a = lax.div(unit, 3), lax.rem(unit, 3)
        total[pair] += lax.dot_general(
            phi[a], quad[...], TURNED, preferred_element_type=jnp.float32
        )

    units = share // 2 * 3
    total[...] = jnp.zeros_like(total)
    odd[...] = jnp.zeros_like(odd)

    def two_units(turn, _):
        contract(jnp.maximum(2 * turn - 1, 0), odd)
        build(2 * turn, even)
        contract(2 * turn, even)
        build(2 * turn + 1, odd)
        return 0

    lax.fori_loop(0, units // 2, two_units, 0)
    if units % 2:
        contract(units - 2, odd)
        build(units - 1, even)
        contract(units - 1, even)
    else:
        contract(units - 1, odd)
    for pair in range(share // 2):
        for h in range(2):
            start = (2 * pair + h) * width
            out_ref = out_refs[start * outs // (share * width)]
            start = start % (share * width // outs)
            out_ref[start : start + width, :] = total[pair, :, h * width : (h + 1) * width].astype(
                out_ref.dtype
            )


def plane_terms(where, blocks, edges, offsets, chunk, share, rows, decks, outs):
    layers, height, comps, across, width = blocks[0].shape
    members = len(blocks)
    slab = layers * height * across
    count = members * slab
    span = next(n * 2 * slab for n in (1, 2, 4, members // 2) if n * 2 * slab % LANES == 0)
    sizes = (layers, height, across, width, share, chunk, rows, decks, outs)
    vmem = pl.BlockSpec(memory_space=pltpu.VMEM)
    dtypes = [jnp.float32 if outs > 1 and n == 0 else jnp.bfloat16 for n in range(outs)]
    results = [((share * width // outs, width), t) for t in dtypes]
    scratch = [
        ((members,) + blocks[0].shape, jnp.float32),
        ((members,) + edges[0].shape, jnp.float32),
        ((4, comps, span, width), jnp.float32),
        ((3, comps, width, count), jnp.bfloat16),
        ((3, width, count), jnp.bfloat16),
        ((3, share * TILE, count), jnp.bfloat16),
        ((2 * width, count), jnp.bfloat16),
        ((2 * width, count), jnp.bfloat16),
        ((share // 2, width, 2 * width), jnp.float32),
    ]
    inputs = [(v.shape, v.dtype) for v in blocks + edges]
    return pl.pallas_call(
        functools.partial(terms_kernel, sizes, offsets),
        out_shape=[jax.ShapeDtypeStruct(*result) for result in results],
        in_specs=[pl.BlockSpec(memory_space=pltpu.SMEM)] + [vmem] * (2 * members),
        out_specs=[vmem] * outs,
        scratch_shapes=[pltpu.VMEM(*shape) for shape in scratch],
        compiler_params=pltpu.CompilerParams(vmem_limit_bytes=grant(results + scratch + inputs)),
        cost_estimate=pl.CostEstimate(
            flops=2 * share * width * width * count * 3, bytes_accessed=2**22, transcendentals=0
        ),
    )(where, *blocks, *edges)


def place_kernel(plan, pieces, given, where_ref, *refs):
    rows, decks, line, block, runs = plan
    out_ref, wide, sems = refs[pieces + given :]
    step = math.gcd(line, LANES)
    copies = []
    for n, (piece, offsets, chunk, d) in enumerate(runs):
        done = n * line

        def widen(k, _):
            at = pl.multiple_of(k * step, step)
            wide[pl.ds(done + at, step), :] = refs[piece][pl.ds(d * line + at, step), :].astype(
                jnp.float32
            )
            return 0

        lax.fori_loop(0, line // step, widen, 0)
        start = (member(where_ref, rows, offsets) * CHUNKS + chunk) * block
        start = start + lax.rem(where_ref[3] - d + decks, decks) * line
        to = pl.ds(pl.multiple_of(start, line), line)
        copies.append(
            pltpu.make_async_copy(wide.at[done : done + line], out_ref.at[to], sems.at[n])
        )
        copies[-1].start()
    for copy in copies:
        copy.wait()


def put(where, result, total_rows, rows, decks, chosen):
    values = [value for _, _, value in chosen]
    block, width = values[0].shape
    line = block // decks
    runs = [
        (n, offsets, chunk, d) for n, (chunk, offsets, _) in enumerate(chosen) for d in range(decks)
    ]
    given = [] if result is None else [result]
    vmem, anywhere = (pl.BlockSpec(memory_space=m) for m in (pltpu.VMEM, pl.ANY))
    wide = ((len(runs) * line, width), jnp.float32)
    return pl.pallas_call(
        functools.partial(place_kernel, (rows, decks, line, block, runs), len(values), len(given)),
        out_shape=jax.ShapeDtypeStruct((total_rows, width), jnp.float32),
        in_specs=[pl.BlockSpec(memory_space=pltpu.SMEM)]
        + [vmem] * len(values)
        + [anywhere] * len(given),
        out_specs=anywhere,
        scratch_shapes=[pltpu.VMEM(*wide), pltpu.SemaphoreType.DMA((len(runs),))],
        input_output_aliases={1 + len(values): 0} if given else {},
        compiler_params=pltpu.CompilerParams(
            vmem_limit_bytes=grant([wide] + [(v.shape, v.dtype) for v in values], 2**21)
        ),
        cost_estimate=pl.CostEstimate(
            flops=0, bytes_accessed=6 * wide[0][0] * width, transcendentals=0
        ),
    )(where, *values, *given)


def edge_piece(cells, weight):
    layers, height, comps, across, width = cells.shape
    decks = lax.axis_size("deck")
    outer = jnp.where(lax.axis_index("side") == 1, cells[..., across - 2 :, :], cells[..., :2, :])
    joints = [(2 * d + 1, 2 * d + 2) for d in range(decks - 1)]
    outer = lax.ppermute(outer, SPAN, joints + [(j, i) for i, j in joints])
    outer = outer.transpose(0, 1, 3, 2, 4).reshape(layers, 2 * height, comps * width)
    columns = weight.transpose(0, 1, 2)
    parts = []
    for _ in range(WEIGHT_PARTS):
        part = lax.reduce_precision(columns, 8, 7)
        columns = columns - part
        parts.append(part.astype(jnp.bfloat16))
    tile = jnp.concatenate(parts, axis=2)
    total = pl.cdiv(2 * height + across, TILE) * TILE
    outer = jnp.pad(outer, ((0, 0), (0, total - across - 2 * height), (0, 0)))
    tile = jnp.pad(tile, ((0, 0), (0, 0), (0, comps * width - tile.shape[2])))
    return jnp.concatenate([outer, tile], axis=1)


def spread_small(piece):
    rows = lax.axis_size("row")
    got = {(0, 0): piece, (0, 1): rotate(piece, "side")}
    for r in range(1, rows):
        got[(r, 0)] = rotate(piece, "row", r)
        pairs = [(2 * i + s, 2 * ((i + r) % rows) + 1 - s) for i in range(rows) for s in range(2)]
        got[(r, 1)] = lax.ppermute(piece, DIAGONAL, pairs)
    out = {}
    for (r, s), value in got.items():
        out[(r, 0, s)] = value
        out[(r, 1, s)] = rotate(value, "core")
    return out


def sum_over_decks(terms, decks):
    if len(terms) > 1:
        parts = [terms[0]] + [rotate(terms[r], "deck", r) for r in range(1, decks)]
    else:
        width = terms[0].shape[1]
        parts = list(lax.all_to_all(terms[0].reshape(decks, -1, width), "deck", 0, 0))
    return sum(part.astype(jnp.float32) for part in parts).astype(jnp.bfloat16)


def shards(velocity_modes, cell_weight):
    width = velocity_modes.shape[-1]
    rows, decks = lax.axis_size("row"), lax.axis_size("deck")
    members = rows * 4
    share = width // members // CHUNKS
    where = jnp.stack([lax.axis_index(a) for a in ("row", "core", "side", "deck")]).astype(jnp.int32)
    outs = decks if share % (2 * decks) == 0 else 1

    cells = velocity_modes.transpose(0, 2, 3, 1, 4)
    blocks = spread_small(cells)
    edges = spread_small(edge_piece(cells, cell_weight))
    offsets = list(blocks)
    blocks, edges = ([d[o] for o in offsets] for d in (blocks, edges))
    terms = [
        plane_terms(where, blocks, edges, offsets, n, share, rows, decks, outs)
        for n in range(CHUNKS)
    ]

    def put_all(result, chosen):
        return put(where, result, width * width, rows, decks, chosen)

    result = None
    waiting = []
    for n in range(CHUNKS):
        mine = sum_over_decks(terms[n], decks)
        piece = jnp.concatenate([mine] + [rotate(mine, "deck", r) for r in range(1, decks)], axis=0)
        across = rotate(piece, "side")
        along = [rotate(piece, "row", r) for r in range(1, rows)]
        near = [(n, (0, 0, 0), piece), (n, (0, 0, 1), across)]
        near += [(n, (r, 0, 0), v) for r, v in enumerate(along, 1)]
        if n == 0:
            diagonal = [rotate(across, "row", r) for r in range(1, rows)]
        else:
            result = put_all(result, waiting.pop(0))
            along, result = lax.optimization_barrier((along, result))
            diagonal = [rotate(v, "side") for v in along]
        near += [(n, (r, 1, s), rotate(v, "core")) for _, (r, _, s), v in near]
        waiting.append(near)
        if n == CHUNKS - 1:
            result = put_all(result, waiting.pop(0))
            diagonal, result = lax.optimization_barrier((diagonal, result))
        far = [(n, (r, 0, 1), v) for r, v in enumerate(diagonal, 1)]
        far_core = [(n, (r, 1, 1), rotate(v, "core")) for r, v in enumerate(diagonal, 1)]
        if n == CHUNKS - 1:
            waiting[-1] += far
            waiting.append(far_core)
        else:
            waiting.append(far + far_core)
    for chosen in waiting:
        result = put_all(result, chosen)
    return result.reshape(width, width, width)


def solution(mesh):
    streams, spans = (mesh.shape[name] for name in ("stream", "span"))
    split = Mesh(mesh.devices.reshape(streams // 2, 2, spans // 2, 2), STREAM + SPAN)
    placed = (P(STREAM, SPAN, None, None, None), P(STREAM, SPAN, None))
    return jax.shard_map(shards, mesh=split, in_specs=placed, out_specs=P(), check_vma=False)
```

```python
import functools
import math

import jax
import jax.numpy as jnp
from jax import lax
from jax.experimental import pallas as pl
from jax.experimental.pallas import tpu as pltpu
from jax.sharding import Mesh, PartitionSpec as P

STREAM = ("row", "core")
SPAN = ("deck", "side")
DIAGONAL = ("row", "side")
WEIGHT_PARTS = 3
LANES = 128
TILE = 16
CHUNKS = 2
TURNED = (((1,), (1,)), ((), ()))


def rotate(value, axis, by=1):
    count = lax.axis_size(axis)
    return lax.ppermute(value, axis, [(i, (i + by) % count) for i in range(count)])


def member(where, rows, offsets):
    r, c, s = offsets
    row = lax.rem(where[0] - r + rows, rows)
    return (row * 2 + lax.rem(where[1] + c, 2)) * 2 + lax.rem(where[2] + s, 2)


def grant(shapes, slack=6 * 2**20):
    total = slack
    for shape, dtype in shapes:
        *outer, rows, columns = shape
        size = jnp.dtype(dtype).itemsize
        rows, columns = pl.cdiv(rows, TILE) * TILE, pl.cdiv(columns, LANES) * LANES
        total += math.prod(outer) * rows * columns * size
    return total


def slopes_kernel(sizes, offsets, where_ref, *refs):
    layers, height, across, width, share, rows, decks, outs = sizes
    members = len(offsets)
    blocks, edges = refs[:members], refs[members : 2 * members]
    turned, phi, own, field, edge, source = refs[2 * members :]
    slab = layers * height * across
    count = members * slab
    span = source.shape[2]
    group_layers = span // (2 * height * across)

    for n in range(members):
        at = member(where_ref, rows, offsets[n])
        field[at] = blocks[n][...].astype(jnp.float32)
        edge[at] = edges[n][...].astype(jnp.float32)

    index = lax.broadcasted_iota(jnp.int32, (across, width), 0)
    line_rows = 2 * height
    weight_row = edge.shape[2] - across

    def one_layer(x, first_layer):
        stream, layer = lax.div(x, layers), lax.rem(x, layers)

        def layer_at(step, side):
            at = x + step
            inside = ((at >= 0) & (at < members // 2 * layers)).astype(jnp.float32)
            at = jnp.clip(at, 0, members // 2 * layers - 1)
            return lax.div(at, layers) * 2 + side, lax.rem(at, layers), inside

        for side in range(2):
            here_at = 2 * stream + side
            tile = edge[here_at, layer, weight_row:, 0:width]
            weights = tile
            for part in range(1, WEIGHT_PARTS):
                weights = weights + pltpu.roll(tile, width - part * height, 1)
            beside = {step: layer_at(step, side) for step in (-2, -1, 1, 2)}
            for z in range(height):
                at = ((x - first_layer) * 2 + side) * height + z
                at = pl.ds(pl.multiple_of(at * across, across), across)
                weight = jnp.broadcast_to(weights[:, z : z + 1], (across, width))
                twelfth, half = weight * (1.0 / 12.0), weight * 0.5
                base = 2 * z // across * across
                for b in range(3):
                    here = field[here_at, layer, z, b]
                    source[0, b, at, :] = here
                    along = {
                        step: field[m, l, z, b] * inside for step, (m, l, inside) in beside.items()
                    }
                    value = 8.0 * (along[1] - along[-1]) - (along[2] - along[-2])
                    source[1, b, at, :] = value * twelfth

                    outer = edge[here_at, layer, base : base + across, b * width : (b + 1) * width]
                    beyond = field[here_at + 1 - 2 * side, layer, z, b]
                    if side == 0:
                        prev = pltpu.roll(outer, (across - 2 - (2 * z - base)) % across, 0)
                        after = beyond
                    else:
                        prev = beyond
                        after = pltpu.roll(outer, (across - (2 * z - base)) % across, 0)
                    near = pltpu.roll(jnp.where(index < 1, after, here), across - 1, 0)
                    near = near - pltpu.roll(jnp.where(index >= across - 1, prev, here), 1, 0)
                    far = pltpu.roll(jnp.where(index < 2, after, here), across - 2, 0)
                    far = far - pltpu.roll(jnp.where(index >= across - 2, prev, here), 2, 0)
                    source[2, b, at, :] = (8.0 * near - far) * twelfth

                    value = jnp.zeros_like(here)
                    if z < height - 1:
                        value = field[here_at, layer, z + 1, b]
                    if z > 0:
                        value = value - field[here_at, layer, z - 1, b]
                    source[3, b, at, :] = value * half
        return first_layer

    row, column = (lax.broadcasted_iota(jnp.int32, (width, width), d) for d in range(2))
    eye = (row == column).astype(jnp.bfloat16)
    row, column = (
        lax.broadcasted_iota(jnp.int32, (CHUNKS * share * TILE, width), d) for d in range(2)
    )
    chunk = sum((row >= n * share * TILE).astype(jnp.int32) for n in range(1, CHUNKS))
    mode = lax.shift_right_logical(row, TILE.bit_length() - 1) - chunk * share
    mode = mode + (where_ref[3] * (share // decks) if outs > 1 else 0)
    mode = jnp.where(mode >= share, mode - share, mode)
    mode = mode + (member(where_ref, rows, (0, 0, 0)) * CHUNKS + chunk) * share
    pick = (column == mode).astype(jnp.bfloat16)

    def one_group(group, _):
        first_layer = group * group_layers
        lax.fori_loop(first_layer, first_layer + group_layers, one_layer, first_layer)
        lanes = pl.ds(pl.multiple_of(group * span, LANES), span)

        def pick_phi(b, _):
            value = source[0, b].astype(jnp.bfloat16)
            phi[b, lanes, :] = value
            value = lax.dot_general(pick, value, TURNED, preferred_element_type=jnp.float32)
            own[b, :, lanes] = value.astype(jnp.bfloat16)
            return 0

        def turn_slope(unit, _):
            a, b = lax.div(unit, 3), lax.rem(unit, 3)
            value = source[1 + a, b].astype(jnp.bfloat16)
            value = lax.dot_general(eye, value, TURNED, preferred_element_type=jnp.float32)
            turned[a, b, :, lanes] = value.astype(jnp.bfloat16)
            return 0

        lax.fori_loop(0, 3, pick_phi, 0)
        lax.fori_loop(0, 9, turn_slope, 0)
        return 0

    lax.fori_loop(0, count // span, one_group, 0)

def plane_slopes(where, blocks, edges, offsets, share, rows, decks, outs):
    layers, height, comps, across, width = blocks[0].shape
    members = len(blocks)
    slab = layers * height * across
    count = members * slab
    span = next(n * 2 * slab for n in (1, 2, 4, members // 2) if n * 2 * slab % LANES == 0)
    sizes = (layers, height, across, width, share, rows, decks, outs)
    vmem = pl.BlockSpec(memory_space=pltpu.VMEM)
    results = [
        ((3, comps, width, count), jnp.bfloat16),
        ((3, count, width), jnp.bfloat16),
        ((3, CHUNKS * share * TILE, count), jnp.bfloat16),
    ]
    scratch = [
        ((members,) + blocks[0].shape, jnp.float32),
        ((members,) + edges[0].shape, jnp.float32),
        ((4, comps, span, width), jnp.float32),
    ]
    inputs = [(v.shape, v.dtype) for v in blocks + edges]
    return pl.pallas_call(
        functools.partial(slopes_kernel, sizes, offsets),
        out_shape=[jax.ShapeDtypeStruct(*result) for result in results],
        in_specs=[pl.BlockSpec(memory_space=pltpu.SMEM)] + [vmem] * (2 * members),
        out_specs=[vmem] * len(results),
        scratch_shapes=[pltpu.VMEM(*shape) for shape in scratch],
        compiler_params=pltpu.CompilerParams(vmem_limit_bytes=grant(results + scratch + inputs)),
        cost_estimate=pl.CostEstimate(
            flops=2 * 12 * count * width * width, bytes_accessed=2**22, transcendentals=0
        ),
    )(where, *blocks, *edges)


def terms_kernel(share, chunk, turned, phi, own, *refs):
    *out_refs, even, odd, total = refs
    outs = len(out_refs)
    width, count = turned.shape[2:]

    first = chunk * share

    def build(unit, quad):
        pair, a = lax.div(unit, 3), lax.rem(unit, 3)
        for start in range(0, count, LANES):
            lanes = slice(start, start + LANES)
            spread = [
                [
                    own[b, pl.ds(pl.multiple_of((first + 2 * pair + h) * TILE, TILE), TILE), lanes]
                    for b in range(3)
                ]
                for h in range(2)
            ]
            for k in range(0, width, TILE):
                slope = [turned[a, b, k : k + TILE, lanes] for b in range(3)]
                for h in range(2):
                    value = spread[h][0] * slope[0]
                    value = value + spread[h][1] * slope[1]
                    value = value + spread[h][2] * slope[2]
                    quad[h * width + k : h * width + k + TILE, lanes] = value

    def contract(unit, quad):
        pair, a = lax.div(unit, 3), lax.rem(unit, 3)
        total[pair] += jnp.dot(quad[...], phi[a], preferred_element_type=jnp.float32)

    units = share // 2 * 3
    total[...] = jnp.zeros_like(total)
    odd[...] = jnp.zeros_like(odd)

    def two_units(turn, _):
        contract(jnp.maximum(2 * turn - 1, 0), odd)
        build(2 * turn, even)
        contract(2 * turn, even)
        build(2 * turn + 1, odd)
        return 0

    lax.fori_loop(0, units // 2, two_units, 0)
    if units % 2:
        contract(units - 2, odd)
        build(units - 1, even)
        contract(units - 1, even)
    else:
        contract(units - 1, odd)
    for pair in range(share // 2):
        for h in range(2):
            start = (2 * pair + h) * width
            out_ref = out_refs[start * outs // (share * width)]
            start = start % (share * width // outs)
            value = total[pair, h * width : (h + 1) * width, :].T
            out_ref[start : start + width, :] = value.astype(out_ref.dtype)


def plane_terms(turned, phi, own, chunk, share, outs):
    width, count = turned.shape[2:]
    vmem = pl.BlockSpec(memory_space=pltpu.VMEM)
    dtypes = [jnp.float32 if outs > 1 and n == 0 else jnp.bfloat16 for n in range(outs)]
    results = [((share * width // outs, width), t) for t in dtypes]
    scratch = [
        ((2 * width, count), jnp.bfloat16),
        ((2 * width, count), jnp.bfloat16),
        ((share // 2, 2 * width, width), jnp.float32),
    ]
    inputs = [(v.shape, v.dtype) for v in (turned, phi, own)]
    return pl.pallas_call(
        functools.partial(terms_kernel, share, chunk),
        out_shape=[jax.ShapeDtypeStruct(*result) for result in results],
        in_specs=[vmem] * 3,
        out_specs=[vmem] * outs,
        scratch_shapes=[pltpu.VMEM(*shape) for shape in scratch],
        compiler_params=pltpu.CompilerParams(vmem_limit_bytes=grant(results + scratch + inputs)),
        cost_estimate=pl.CostEstimate(
            flops=2 * share * width * width * count * 3, bytes_accessed=2**22, transcendentals=0
        ),
    )(turned, phi, own)


def place_kernel(plan, pieces, given, where_ref, *refs):
    rows, decks, line, block, runs = plan
    out_ref, wide, sems = refs[pieces + given :]
    step = math.gcd(line, LANES)
    copies = []
    for n, (piece, offsets, chunk, d) in enumerate(runs):
        done = n * line

        def widen(k, _):
            at = pl.multiple_of(k * step, step)
            wide[pl.ds(done + at, step), :] = refs[piece][pl.ds(d * line + at, step), :].astype(
                jnp.float32
            )
            return 0

        lax.fori_loop(0, line // step, widen, 0)
        start = (member(where_ref, rows, offsets) * CHUNKS + chunk) * block
        start = start + lax.rem(where_ref[3] - d + decks, decks) * line
        to = pl.ds(pl.multiple_of(start, line), line)
        copies.append(
            pltpu.make_async_copy(wide.at[done : done + line], out_ref.at[to], sems.at[n])
        )
        copies[-1].start()
    for copy in copies:
        copy.wait()


def put(where, result, total_rows, rows, decks, chosen):
    values = [value for _, _, value in chosen]
    block, width = values[0].shape
    line = block // decks
    runs = [
        (n, offsets, chunk, d) for n, (chunk, offsets, _) in enumerate(chosen) for d in range(decks)
    ]
    given = [] if result is None else [result]
    vmem, anywhere = (pl.BlockSpec(memory_space=m) for m in (pltpu.VMEM, pl.ANY))
    wide = ((len(runs) * line, width), jnp.float32)
    return pl.pallas_call(
        functools.partial(place_kernel, (rows, decks, line, block, runs), len(values), len(given)),
        out_shape=jax.ShapeDtypeStruct((total_rows, width), jnp.float32),
        in_specs=[pl.BlockSpec(memory_space=pltpu.SMEM)]
        + [vmem] * len(values)
        + [anywhere] * len(given),
        out_specs=anywhere,
        scratch_shapes=[pltpu.VMEM(*wide), pltpu.SemaphoreType.DMA((len(runs),))],
        input_output_aliases={1 + len(values): 0} if given else {},
        compiler_params=pltpu.CompilerParams(
            vmem_limit_bytes=grant([wide] + [(v.shape, v.dtype) for v in values], 2**21)
        ),
        cost_estimate=pl.CostEstimate(
            flops=0, bytes_accessed=6 * wide[0][0] * width, transcendentals=0
        ),
    )(where, *values, *given)


def edge_piece(cells, weight):
    layers, height, comps, across, width = cells.shape
    decks = lax.axis_size("deck")
    outer = jnp.where(lax.axis_index("side") == 1, cells[..., across - 2 :, :], cells[..., :2, :])
    joints = [(2 * d + 1, 2 * d + 2) for d in range(decks - 1)]
    outer = lax.ppermute(outer, SPAN, joints + [(j, i) for i, j in joints])
    outer = outer.transpose(0, 1, 3, 2, 4).reshape(layers, 2 * height, comps * width)
    columns = weight.transpose(0, 1, 2)
    parts = []
    for _ in range(WEIGHT_PARTS):
        part = lax.reduce_precision(columns, 8, 7)
        columns = columns - part
        parts.append(part.astype(jnp.bfloat16))
    tile = jnp.concatenate(parts, axis=2)
    total = pl.cdiv(2 * height + across, TILE) * TILE
    outer = jnp.pad(outer, ((0, 0), (0, total - across - 2 * height), (0, 0)))
    tile = jnp.pad(tile, ((0, 0), (0, 0), (0, comps * width - tile.shape[2])))
    return jnp.concatenate([outer, tile], axis=1)


def spread_small(piece):
    rows = lax.axis_size("row")
    got = {(0, 0): piece, (0, 1): rotate(piece, "side")}
    for r in range(1, rows):
        got[(r, 0)] = rotate(piece, "row", r)
        pairs = [(2 * i + s, 2 * ((i + r) % rows) + 1 - s) for i in range(rows) for s in range(2)]
        got[(r, 1)] = lax.ppermute(piece, DIAGONAL, pairs)
    out = {}
    for (r, s), value in got.items():
        out[(r, 0, s)] = value
        out[(r, 1, s)] = rotate(value, "core")
    return out


def sum_over_decks(terms, decks):
    if len(terms) > 1:
        parts = [terms[0]] + [rotate(terms[r], "deck", r) for r in range(1, decks)]
    else:
        width = terms[0].shape[1]
        parts = list(lax.all_to_all(terms[0].reshape(decks, -1, width), "deck", 0, 0))
    return sum(part.astype(jnp.float32) for part in parts).astype(jnp.bfloat16)


def shards(velocity_modes, cell_weight):
    width = velocity_modes.shape[-1]
    rows, decks = lax.axis_size("row"), lax.axis_size("deck")
    members = rows * 4
    share = width // members // CHUNKS
    where = jnp.stack([lax.axis_index(a) for a in ("row", "core", "side", "deck")]).astype(jnp.int32)
    outs = decks if share % (2 * decks) == 0 else 1

    cells = velocity_modes.transpose(0, 2, 3, 1, 4)
    blocks = spread_small(cells)
    edges = spread_small(edge_piece(cells, cell_weight))
    offsets = list(blocks)
    blocks, edges = ([d[o] for o in offsets] for d in (blocks, edges))
    slopes = plane_slopes(where, blocks, edges, offsets, share, rows, decks, outs)
    terms = [plane_terms(*slopes, n, share, outs) for n in range(CHUNKS)]

    def put_all(result, chosen):
        return put(where, result, width * width, rows, decks, chosen)

    result = None
    waiting = []
    for n in range(CHUNKS):
        mine = sum_over_decks(terms[n], decks)
        piece = jnp.concatenate([mine] + [rotate(mine, "deck", r) for r in range(1, decks)], axis=0)
        across = rotate(piece, "side")
        along = [rotate(piece, "row", r) for r in range(1, rows)]
        near = [(n, (0, 0, 0), piece), (n, (0, 0, 1), across)]
        near += [(n, (r, 0, 0), v) for r, v in enumerate(along, 1)]
        if n == 0:
            diagonal = [rotate(across, "row", r) for r in range(1, rows)]
        else:
            result = put_all(result, waiting.pop(0))
            along, result = lax.optimization_barrier((along, result))
            diagonal = [rotate(v, "side") for v in along]
        near += [(n, (r, 1, s), rotate(v, "core")) for _, (r, _, s), v in near]
        waiting.append(near)
        if n == CHUNKS - 1:
            result = put_all(result, waiting.pop(0))
            diagonal, result = lax.optimization_barrier((diagonal, result))
        far = [(n, (r, 0, 1), v) for r, v in enumerate(diagonal, 1)]
        far_core = [(n, (r, 1, 1), rotate(v, "core")) for r, v in enumerate(diagonal, 1)]
        if n == CHUNKS - 1:
            waiting[-1] += far
            waiting.append(far_core)
        else:
            waiting.append(far + far_core)
    for chosen in waiting:
        result = put_all(result, chosen)
    return result.reshape(width, width, width)


def solution(mesh):
    streams, spans = (mesh.shape[name] for name in ("stream", "span"))
    split = Mesh(mesh.devices.reshape(streams // 2, 2, spans // 2, 2), STREAM + SPAN)
    placed = (P(STREAM, SPAN, None, None, None), P(STREAM, SPAN, None))
    return jax.shard_map(shards, mesh=split, in_specs=placed, out_specs=P(), check_vma=False)
```

```python
import functools
import math

import jax
import jax.numpy as jnp
from jax import lax
from jax.experimental import pallas as pl
from jax.experimental.pallas import tpu as pltpu
from jax.sharding import Mesh, PartitionSpec as P

STREAM = ("row", "core")
SPAN = ("deck", "side")
DIAGONAL = ("row", "side")
WEIGHT_PARTS = 3
LANES = 128
TILE = 16
CHUNKS = 2
TURNED = (((1,), (1,)), ((), ()))


def rotate(value, axis, by=1):
    count = lax.axis_size(axis)
    return lax.ppermute(value, axis, [(i, (i + by) % count) for i in range(count)])


def member(where, rows, offsets):
    r, c, s = offsets
    row = lax.rem(where[0] - r + rows, rows)
    return (row * 2 + lax.rem(where[1] + c, 2)) * 2 + lax.rem(where[2] + s, 2)


def grant(shapes, slack=6 * 2**20):
    total = slack
    for shape, dtype in shapes:
        *outer, rows, columns = shape
        size = jnp.dtype(dtype).itemsize
        rows, columns = pl.cdiv(rows, TILE) * TILE, pl.cdiv(columns, LANES) * LANES
        total += math.prod(outer) * rows * columns * size
    return total


def slopes_kernel(sizes, offsets, where_ref, *refs):
    layers, height, across, width, share, rows, decks, outs = sizes
    members = len(offsets)
    blocks, edges = refs[:members], refs[members : 2 * members]
    turned, own, field, edge, *sources = refs[2 * members :]
    count = members * layers * height * across
    depth = members // 2 * layers
    piece = 4 * count // depth
    parts = count // piece

    field[:2] = jnp.zeros_like(field[:2])
    field[members + 2 :] = jnp.zeros_like(field[members + 2 :])
    for n in range(members):
        at = member(where_ref, rows, offsets[n])
        field[at + 2] = blocks[n][...].astype(jnp.float32)
        edge[at] = edges[n][...].astype(jnp.float32)

    index = lax.broadcasted_iota(jnp.int32, (across, width), 0)
    weight_row = edge.shape[2] - across
    row, column = (lax.broadcasted_iota(jnp.int32, (width, width), d) for d in range(2))
    eye = (row == column).astype(jnp.bfloat16)

    def stencil(x, b, source):
        def layer_at(step, side):
            at = x + step + layers
            return lax.div(at, layers) * 2 + side, lax.rem(at, layers)

        for side in range(2):
            here_at, layer = layer_at(0, side)
            at = here_at - 2
            tile = edge[at, layer, weight_row:, 0:width]
            weights = tile
            for part in range(1, WEIGHT_PARTS):
                weights = weights + pltpu.roll(tile, width - part * height, 1)
            beside = {step: layer_at(step, side) for step in (-2, -1, 1, 2)}
            found = []
            for z in range(height):
                weight = jnp.broadcast_to(weights[:, z : z + 1], (across, width))
                twelfth, half = weight * (1.0 / 12.0), weight * 0.5
                base = 2 * z // across * across
                here = field[here_at, layer, z, b]
                along = {step: field[m, l, z, b] for step, (m, l) in beside.items()}
                value_x = 8.0 * (along[1] - along[-1]) - (along[2] - along[-2])

                outer = edge[at, layer, base : base + across, b * width : (b + 1) * width]
                beyond = field[here_at + 1 - 2 * side, layer, z, b]
                if side == 0:
                    prev = pltpu.roll(outer, (across - 2 - (2 * z - base)) % across, 0)
                    after = beyond
                else:
                    prev = beyond
                    after = pltpu.roll(outer, (across - (2 * z - base)) % across, 0)
                near = pltpu.roll(jnp.where(index < 1, after, here), across - 1, 0)
                near = near - pltpu.roll(jnp.where(index >= across - 1, prev, here), 1, 0)
                far = pltpu.roll(jnp.where(index < 2, after, here), across - 2, 0)
                far = far - pltpu.roll(jnp.where(index >= across - 2, prev, here), 2, 0)
                value_y = 8.0 * near - far

                value_z = jnp.zeros_like(here)
                if z < height - 1:
                    value_z = field[here_at, layer, z + 1, b]
                if z > 0:
                    value_z = value_z - field[here_at, layer, z - 1, b]
                found.append((here, value_x * twelfth, value_y * twelfth, value_z * half))
                if len(found) * across == TILE:
                    start = ((at * layers + layer) * height + z + 1) * across - TILE
                    to = pl.ds(pl.multiple_of(start, TILE), TILE)
                    for q in range(4):
                        value = jnp.concatenate([f[q] for f in found], axis=0)
                        source[q, to, :] = value.astype(jnp.bfloat16)
                    found = []

    def turn(x, b, source):
        q, part = lax.div(x, parts), lax.rem(x, parts)
        at = pl.ds(pl.multiple_of(part * piece, piece), piece)
        value = lax.dot_general(eye, source[q, at, :], TURNED, preferred_element_type=jnp.float32)
        turned[q, b, :, at] = value.astype(jnp.bfloat16)

    for step in range(4):

        def one_layer(x, _):
            if step < 3:
                stencil(x, step, sources[step % 2])
            if step > 0:
                turn(x, step - 1, sources[(step - 1) % 2])
            return 0

        lax.fori_loop(0, depth, one_layer, 0)

    row, column = (
        lax.broadcasted_iota(jnp.int32, (CHUNKS * share * TILE, width), d) for d in range(2)
    )
    chunk = sum((row >= n * share * TILE).astype(jnp.int32) for n in range(1, CHUNKS))
    mode = lax.shift_right_logical(row, TILE.bit_length() - 1) - chunk * share
    mode = mode + (where_ref[3] * (share // decks) if outs > 1 else 0)
    mode = jnp.where(mode >= share, mode - share, mode)
    mode = mode + (member(where_ref, rows, (0, 0, 0)) * CHUNKS + chunk) * share
    pick = (column == mode).astype(jnp.bfloat16)
    for b in range(3):
        value = jnp.dot(pick, turned[0, b], preferred_element_type=jnp.float32)
        own[b] = value.astype(jnp.bfloat16)


def plane_slopes(where, blocks, edges, offsets, share, rows, decks, outs):
    layers, height, comps, across, width = blocks[0].shape
    members = len(blocks)
    count = members * layers * height * across
    sizes = (layers, height, across, width, share, rows, decks, outs)
    vmem = pl.BlockSpec(memory_space=pltpu.VMEM)
    results = [
        ((4, comps, width, count), jnp.bfloat16),
        ((comps, CHUNKS * share * TILE, count), jnp.bfloat16),
    ]
    scratch = [
        ((members + 4,) + blocks[0].shape, jnp.float32),
        ((members,) + edges[0].shape, jnp.float32),
        ((4, count, width), jnp.bfloat16),
        ((4, count, width), jnp.bfloat16),
    ]
    inputs = [(v.shape, v.dtype) for v in blocks + edges]
    return pl.pallas_call(
        functools.partial(slopes_kernel, sizes, offsets),
        out_shape=[jax.ShapeDtypeStruct(*result) for result in results],
        in_specs=[pl.BlockSpec(memory_space=pltpu.SMEM)] + [vmem] * (2 * members),
        out_specs=[vmem] * len(results),
        scratch_shapes=[pltpu.VMEM(*shape) for shape in scratch],
        compiler_params=pltpu.CompilerParams(vmem_limit_bytes=grant(results + scratch + inputs)),
        cost_estimate=pl.CostEstimate(
            flops=2 * 12 * count * width * width, bytes_accessed=2**22, transcendentals=0
        ),
    )(where, *blocks, *edges)


def terms_kernel(share, chunk, turned, own, *refs):
    *out_refs, even, odd = refs
    outs = len(out_refs)
    width, count = turned.shape[2:]
    first = chunk * share
    for pair in range(share // 2):
        quad = (even, odd)[pair % 2]
        for a in range(3):
            for start in range(0, count, LANES):
                lanes = slice(start, start + LANES)
                spread = [
                    [
                        own[b, (first + 2 * pair + h) * TILE : (first + 2 * pair + h + 1) * TILE, lanes]
                        for b in range(3)
                    ]
                    for h in range(2)
                ]
                for k in range(0, width, TILE):
                    slope = [turned[1 + a, b, k : k + TILE, lanes] for b in range(3)]
                    for h in range(2):
                        value = spread[h][0] * slope[0]
                        value = value + spread[h][1] * slope[1]
                        value = value + spread[h][2] * slope[2]
                        quad[a, h * width + k : h * width + k + TILE, lanes] = value
        total = sum(
            lax.dot_general(turned[0, a], quad[a], TURNED, preferred_element_type=jnp.float32)
            for a in range(3)
        )
        for h in range(2):
            start = (2 * pair + h) * width
            out_ref = out_refs[start * outs // (share * width)]
            start = start % (share * width // outs)
            out_ref[start : start + width, :] = total[:, h * width : (h + 1) * width].astype(
                out_ref.dtype
            )


def plane_terms(turned, own, chunk, share, outs):
    width, count = turned.shape[2:]
    vmem = pl.BlockSpec(memory_space=pltpu.VMEM)
    dtypes = [jnp.float32 if outs > 1 and n == 0 else jnp.bfloat16 for n in range(outs)]
    results = [((share * width // outs, width), t) for t in dtypes]
    second = 2 if share > 2 else 1
    scratch = [((3, 2 * width, count), jnp.bfloat16)] * second
    scratch += [((TILE, LANES), jnp.bfloat16)] * (2 - second)
    inputs = [(v.shape, v.dtype) for v in (turned, own)]
    return pl.pallas_call(
        functools.partial(terms_kernel, share, chunk),
        out_shape=[jax.ShapeDtypeStruct(*result) for result in results],
        in_specs=[vmem] * 2,
        out_specs=[vmem] * outs,
        scratch_shapes=[pltpu.VMEM(*shape) for shape in scratch],
        compiler_params=pltpu.CompilerParams(vmem_limit_bytes=grant(results + scratch + inputs)),
        cost_estimate=pl.CostEstimate(
            flops=2 * share * width * width * count * 3, bytes_accessed=2**22, transcendentals=0
        ),
    )(turned, own)


def place_kernel(plan, pieces, given, where_ref, *refs):
    rows, decks, line, block, runs = plan
    out_ref, wide, sems = refs[pieces + given :]
    step = math.gcd(line, LANES)
    copies = []
    for n, (piece, offsets, chunk, d) in enumerate(runs):
        done = n * line

        def widen(k, _):
            at = pl.multiple_of(k * step, step)
            wide[pl.ds(done + at, step), :] = refs[piece][pl.ds(d * line + at, step), :].astype(
                jnp.float32
            )
            return 0

        lax.fori_loop(0, line // step, widen, 0)
        start = (member(where_ref, rows, offsets) * CHUNKS + chunk) * block
        start = start + lax.rem(where_ref[3] - d + decks, decks) * line
        to = pl.ds(pl.multiple_of(start, line), line)
        copies.append(
            pltpu.make_async_copy(wide.at[done : done + line], out_ref.at[to], sems.at[n])
        )
        copies[-1].start()
    for copy in copies:
        copy.wait()


def put(where, result, total_rows, rows, decks, chosen):
    values = [value for _, _, value in chosen]
    block, width = values[0].shape
    line = block // decks
    runs = [
        (n, offsets, chunk, d) for n, (chunk, offsets, _) in enumerate(chosen) for d in range(decks)
    ]
    given = [] if result is None else [result]
    vmem, anywhere = (pl.BlockSpec(memory_space=m) for m in (pltpu.VMEM, pl.ANY))
    wide = ((len(runs) * line, width), jnp.float32)
    return pl.pallas_call(
        functools.partial(place_kernel, (rows, decks, line, block, runs), len(values), len(given)),
        out_shape=jax.ShapeDtypeStruct((total_rows, width), jnp.float32),
        in_specs=[pl.BlockSpec(memory_space=pltpu.SMEM)]
        + [vmem] * len(values)
        + [anywhere] * len(given),
        out_specs=anywhere,
        scratch_shapes=[pltpu.VMEM(*wide), pltpu.SemaphoreType.DMA((len(runs),))],
        input_output_aliases={1 + len(values): 0} if given else {},
        compiler_params=pltpu.CompilerParams(
            vmem_limit_bytes=grant([wide] + [(v.shape, v.dtype) for v in values], 2**21)
        ),
        cost_estimate=pl.CostEstimate(
            flops=0, bytes_accessed=6 * wide[0][0] * width, transcendentals=0
        ),
    )(where, *values, *given)


def outer_rows(cells):
    across = cells.shape[3]
    decks = lax.axis_size("deck")
    rows = jnp.where(lax.axis_index("side") == 1, cells[..., across - 2 :, :], cells[..., :2, :])
    joints = [(2 * d + 1, 2 * d + 2) for d in range(decks - 1)]
    return lax.ppermute(rows, SPAN, joints + [(j, i) for i, j in joints])


def edge_piece(outer, weight):
    layers, height, comps, _, width = outer.shape
    across = weight.shape[1]
    outer = outer.transpose(0, 1, 3, 2, 4).reshape(layers, 2 * height, comps * width)
    parts = []
    for _ in range(WEIGHT_PARTS):
        part = lax.reduce_precision(weight, 8, 7)
        weight = weight - part
        parts.append(part.astype(jnp.bfloat16))
    tile = jnp.concatenate(parts, axis=2)
    total = pl.cdiv(2 * height + across, TILE) * TILE
    outer = jnp.pad(outer, ((0, 0), (0, total - across - 2 * height), (0, 0)))
    tile = jnp.pad(tile, ((0, 0), (0, 0), (0, comps * width - tile.shape[2])))
    return jnp.concatenate([outer, tile], axis=1)


def spread_near(piece):
    rows = lax.axis_size("row")
    got = {(0, 0): piece, (0, 1): rotate(piece, "side")}
    for r in range(1, rows):
        got[(r, 0)] = rotate(piece, "row", r)
        pairs = [(2 * i + s, 2 * ((i + r) % rows) + 1 - s) for i in range(rows) for s in range(2)]
        got[(r, 1)] = lax.ppermute(piece, DIAGONAL, pairs)
    return got


def spread_cores(got):
    out = {}
    for (r, s), value in got.items():
        out[(r, 0, s)] = value
        out[(r, 1, s)] = rotate(value, "core")
    return out


def sum_over_decks(terms, decks):
    if len(terms) > 1:
        parts = [terms[0]] + [rotate(terms[r], "deck", r) for r in range(1, decks)]
    else:
        width = terms[0].shape[1]
        parts = list(lax.all_to_all(terms[0].reshape(decks, -1, width), "deck", 0, 0))
    return sum(part.astype(jnp.float32) for part in parts).astype(jnp.bfloat16)


def shards(velocity_modes, cell_weight):
    width = velocity_modes.shape[-1]
    rows, decks = lax.axis_size("row"), lax.axis_size("deck")
    members = rows * 4
    share = width // members // CHUNKS
    where = jnp.stack([lax.axis_index(a) for a in ("row", "core", "side", "deck")]).astype(jnp.int32)
    outs = decks if share % (2 * decks) == 0 else 1

    cells = velocity_modes.transpose(0, 2, 3, 1, 4)
    outer = outer_rows(cells)
    near = spread_near(cells)
    outer, near = lax.optimization_barrier((outer, near))
    near[(0, 0)] = cells
    blocks = spread_cores(near)
    edges = spread_cores(spread_near(edge_piece(outer, cell_weight)))
    offsets = list(blocks)
    blocks, edges = ([d[o] for o in offsets] for d in (blocks, edges))
    slopes = plane_slopes(where, blocks, edges, offsets, share, rows, decks, outs)
    terms = [plane_terms(*slopes, n, share, outs) for n in range(CHUNKS)]

    def put_all(result, chosen):
        return put(where, result, width * width, rows, decks, chosen)

    result = None
    waiting = []
    for n in range(CHUNKS):
        mine = sum_over_decks(terms[n], decks)
        piece = jnp.concatenate([mine] + [rotate(mine, "deck", r) for r in range(1, decks)], axis=0)
        across = rotate(piece, "side")
        along = [rotate(piece, "row", r) for r in range(1, rows)]
        near = [(n, (0, 0, 0), piece), (n, (0, 0, 1), across)]
        near += [(n, (r, 0, 0), v) for r, v in enumerate(along, 1)]
        if n == 0:
            diagonal = [rotate(across, "row", r) for r in range(1, rows)]
        else:
            result = put_all(result, waiting.pop(0))
            along, result = lax.optimization_barrier((along, result))
            diagonal = [rotate(v, "side") for v in along]
        near_core = [(n, (r, 1, s), rotate(v, "core")) for _, (r, _, s), v in near]
        if n == CHUNKS - 1:
            result = put_all(result, waiting.pop(0) + near)
            diagonal, result = lax.optimization_barrier((diagonal, result))
            waiting.append(near_core)
        else:
            waiting.append(near + near_core)
        far = [(n, (r, 0, 1), v) for r, v in enumerate(diagonal, 1)]
        far_core = [(n, (r, 1, 1), rotate(v, "core")) for r, v in enumerate(diagonal, 1)]
        if n == CHUNKS - 1:
            waiting[-1] += far
            waiting.append(far_core)
        else:
            waiting.append(far + far_core)
    for chosen in waiting:
        result = put_all(result, chosen)
    return result.reshape(width, width, width)


def solution(mesh):
    streams, spans = (mesh.shape[name] for name in ("stream", "span"))
    split = Mesh(mesh.devices.reshape(streams // 2, 2, spans // 2, 2), STREAM + SPAN)
    placed = (P(STREAM, SPAN, None, None, None), P(STREAM, SPAN, None))
    return jax.shard_map(shards, mesh=split, in_specs=placed, out_specs=P(), check_vma=False)
```

```python
import functools
import math

import jax
import jax.numpy as jnp
from jax import lax
from jax.experimental import pallas as pl
from jax.experimental.pallas import tpu as pltpu
from jax.sharding import Mesh, PartitionSpec as P

STREAM = ("row", "core")
SPAN = ("deck", "side")
DIAGONAL = ("row", "side")
WEIGHT_PARTS = 3
LANES = 128
TILE = 16
CHUNKS = 2
TURNED = (((1,), (1,)), ((), ()))


def rotate(value, axis, by=1):
    count = lax.axis_size(axis)
    return lax.ppermute(value, axis, [(i, (i + by) % count) for i in range(count)])


def member(where, rows, offsets):
    r, c, s = offsets
    row = lax.rem(where[0] - r + rows, rows)
    return (row * 2 + lax.rem(where[1] + c, 2)) * 2 + lax.rem(where[2] + s, 2)


def grant(shapes, slack=6 * 2**20):
    total = slack
    for shape, dtype in shapes:
        *outer, rows, columns = shape
        size = jnp.dtype(dtype).itemsize
        rows, columns = pl.cdiv(rows, TILE) * TILE, pl.cdiv(columns, LANES) * LANES
        total += math.prod(outer) * rows * columns * size
    return total


def slopes_kernel(sizes, offsets, where_ref, *refs):
    layers, height, across, width, rows = sizes
    members = len(offsets)
    blocks, edges = refs[:members], refs[members : 2 * members]
    turned, phi, field, edge, mine, sem, *sources = refs[2 * members :]
    count = members * layers * height * across
    depth = members // 2 * layers
    piece = 4 * count // depth
    parts = count // piece

    fetch = pltpu.make_async_copy(blocks[0], mine, sem)
    fetch.start()
    field[:2] = jnp.zeros_like(field[:2])
    field[members + 2 :] = jnp.zeros_like(field[members + 2 :])
    for n in range(members):
        at = member(where_ref, rows, offsets[n])
        edge[at] = edges[n][...].astype(jnp.float32)
        if n > 0:
            field[at + 2] = blocks[n][...].astype(jnp.float32)
    fetch.wait()
    field[member(where_ref, rows, offsets[0]) + 2] = mine[...].astype(jnp.float32)

    index = lax.broadcasted_iota(jnp.int32, (across, width), 0)
    weight_row = edge.shape[2] - across
    row, column = (lax.broadcasted_iota(jnp.int32, (2 * width, 2 * width), d) for d in range(2))
    eye = (row == column).astype(jnp.bfloat16)

    def stencil(x, b, source):
        def layer_at(step, side):
            at = x + step + layers
            return lax.div(at, layers) * 2 + side, lax.rem(at, layers)

        for side in range(2):
            here_at, layer = layer_at(0, side)
            at = here_at - 2
            tile = edge[at, layer, weight_row:, 0:width]
            weights = tile
            for part in range(1, WEIGHT_PARTS):
                weights = weights + pltpu.roll(tile, width - part * height, 1)
            beside = {step: layer_at(step, side) for step in (-2, -1, 1, 2)}
            found = []
            for z in range(height):
                weight = jnp.broadcast_to(weights[:, z : z + 1], (across, width))
                twelfth, half = weight * (1.0 / 12.0), weight * 0.5
                base = 2 * z // across * across
                here = field[here_at, layer, z, b]
                along = {step: field[m, l, z, b] for step, (m, l) in beside.items()}
                value_x = 8.0 * (along[1] - along[-1]) - (along[2] - along[-2])

                outer = edge[at, layer, base : base + across, b * width : (b + 1) * width]
                beyond = field[here_at + 1 - 2 * side, layer, z, b]
                if side == 0:
                    prev = pltpu.roll(outer, (across - 2 - (2 * z - base)) % across, 0)
                    after = beyond
                else:
                    prev = beyond
                    after = pltpu.roll(outer, (across - (2 * z - base)) % across, 0)
                near = pltpu.roll(jnp.where(index < 1, after, here), across - 1, 0)
                near = near - pltpu.roll(jnp.where(index >= across - 1, prev, here), 1, 0)
                far = pltpu.roll(jnp.where(index < 2, after, here), across - 2, 0)
                far = far - pltpu.roll(jnp.where(index >= across - 2, prev, here), 2, 0)
                value_y = 8.0 * near - far

                value_z = jnp.zeros_like(here)
                if z < height - 1:
                    value_z = field[here_at, layer, z + 1, b]
                if z > 0:
                    value_z = value_z - field[here_at, layer, z - 1, b]
                found.append((here, value_x * twelfth, value_y * twelfth, value_z * half))
                if len(found) * across == TILE:
                    start = ((at * layers + layer) * height + z + 1) * across - TILE
                    to = pl.ds(pl.multiple_of(start, TILE), TILE)
                    for q in range(4):
                        value = jnp.concatenate([f[q] for f in found], axis=0)
                        columns = slice(q % 2 * width, (q % 2 + 1) * width)
                        source[q // 2, to, columns] = value.astype(jnp.bfloat16)
                    found = []

    def turn(x, b, source):
        both, part = lax.div(x, parts), lax.rem(x, parts)
        at = pl.ds(pl.multiple_of(part * piece, piece), piece)
        value = lax.dot_general(eye, source[both, at, :], TURNED, preferred_element_type=jnp.float32)
        for n in range(2):
            turned[2 * both + n, b, :, at] = value[n * width : (n + 1) * width].astype(jnp.bfloat16)

        @pl.when(both == 0)
        def _():
            phi[b, :, at] = value[:width]

    for step in range(4):

        def two_layers(x, _):
            if step < 3:
                stencil(2 * x, step, sources[step % 2])
                stencil(2 * x + 1, step, sources[step % 2])
            if step > 0:
                turn(x, step - 1, sources[(step - 1) % 2])
            return 0

        lax.fori_loop(0, depth // 2, two_layers, 0)


def plane_slopes(where, blocks, edges, offsets, rows):
    layers, height, comps, across, width = blocks[0].shape
    members = len(blocks)
    count = members * layers * height * across
    sizes = (layers, height, across, width, rows)
    vmem, anywhere = (pl.BlockSpec(memory_space=m) for m in (pltpu.VMEM, pl.ANY))
    results = [
        ((4, comps, width, count), jnp.bfloat16),
        ((comps, width, count), jnp.float32),
    ]
    scratch = [
        ((members + 4,) + blocks[0].shape, jnp.float32),
        ((members,) + edges[0].shape, jnp.float32),
        (blocks[0].shape, blocks[0].dtype),
        ((2, count, 2 * width), jnp.bfloat16),
        ((2, count, 2 * width), jnp.bfloat16),
    ]
    inputs = [(v.shape, v.dtype) for v in blocks + edges]
    buffers = [pltpu.VMEM(*shape) for shape in scratch]
    return pl.pallas_call(
        functools.partial(slopes_kernel, sizes, offsets),
        out_shape=[jax.ShapeDtypeStruct(*result) for result in results],
        in_specs=[pl.BlockSpec(memory_space=pltpu.SMEM), anywhere] + [vmem] * (2 * members - 1),
        out_specs=[vmem] * len(results),
        scratch_shapes=buffers[:3] + [pltpu.SemaphoreType.DMA] + buffers[3:],
        compiler_params=pltpu.CompilerParams(vmem_limit_bytes=grant(results + scratch + inputs)),
        cost_estimate=pl.CostEstimate(
            flops=2 * 12 * count * width * width, bytes_accessed=2**22, transcendentals=0
        ),
    )(where, *blocks, *edges)


def terms_kernel(share, chunk, rows, decks, where_ref, turned, phi, *refs):
    out_refs = [ref for ref in refs if len(ref.shape) == 2]
    own, *quads = refs[len(out_refs) :]
    outs = len(out_refs)
    width, count = turned.shape[2:]
    base = (member(where_ref, rows, (0, 0, 0)) * CHUNKS + chunk) * share
    first = where_ref[3] * (share // decks) if outs > 1 else 0
    together = min(2, share // 2)
    for i in range(share):
        mode = base + lax.rem(i + first, share)
        for b in range(3):
            own[b, i] = jnp.broadcast_to(phi[b, pl.ds(mode, 1), :], (TILE, count))
    for group in range(share // 2 // together):
        modes = range(group * 2 * together, (group + 1) * 2 * together)
        held = [quads[(group * together + p) % len(quads)] for p in range(together)]
        for a in range(3):
            for start in range(0, count, LANES):
                lanes = slice(start, start + LANES)
                spread = [[own[b, mode, :, lanes] for b in range(3)] for mode in modes]
                for k in range(0, width, TILE):
                    slope = [
                        turned[1 + a, b, k : k + TILE, lanes].astype(jnp.float32) for b in range(3)
                    ]
                    for i, row in enumerate(spread):
                        value = row[0] * slope[0] + row[1] * slope[1] + row[2] * slope[2]
                        at = i % 2 * width + k
                        held[i // 2][a, at : at + TILE, lanes] = value.astype(jnp.bfloat16)
        for p in range(together):
            total = sum(
                lax.dot_general(
                    turned[0, a], held[p][a], TURNED, preferred_element_type=jnp.float32
                )
                for a in range(3)
            )
            for h in range(2):
                start = (2 * (group * together + p) + h) * width
                out_ref = out_refs[start * outs // (share * width)]
                start = start % (share * width // outs)
                out_ref[start : start + width, :] = total[:, h * width : (h + 1) * width].astype(
                    out_ref.dtype
                )


def plane_terms(where, turned, phi, chunk, share, rows, decks, outs):
    width, count = turned.shape[2:]
    vmem = pl.BlockSpec(memory_space=pltpu.VMEM)
    dtypes = [jnp.float32 if outs > 1 and n == 0 else jnp.bfloat16 for n in range(outs)]
    results = [((share * width // outs, width), t) for t in dtypes]
    scratch = [((3, share, TILE, count), jnp.float32)]
    scratch += [((3, 2 * width, count), jnp.bfloat16)] * min(4, share // 2)
    inputs = [(v.shape, v.dtype) for v in (turned, phi)]
    return pl.pallas_call(
        functools.partial(terms_kernel, share, chunk, rows, decks),
        out_shape=[jax.ShapeDtypeStruct(*result) for result in results],
        in_specs=[pl.BlockSpec(memory_space=pltpu.SMEM)] + [vmem] * 2,
        out_specs=[vmem] * outs,
        scratch_shapes=[pltpu.VMEM(*shape) for shape in scratch],
        compiler_params=pltpu.CompilerParams(vmem_limit_bytes=grant(results + scratch + inputs)),
        cost_estimate=pl.CostEstimate(
            flops=2 * share * width * width * count * 3, bytes_accessed=2**22, transcendentals=0
        ),
    )(where, turned, phi)


def place_kernel(plan, pieces, given, where_ref, *refs):
    rows, decks, line, block, runs = plan
    out_ref, wide, sems = refs[pieces + given :]
    step = math.gcd(line, LANES)
    copies = []
    for n, (piece, offsets, chunk, d) in enumerate(runs):
        done = n * line

        def widen(k, _):
            at = pl.multiple_of(k * step, step)
            wide[pl.ds(done + at, step), :] = refs[piece][pl.ds(d * line + at, step), :].astype(
                jnp.float32
            )
            return 0

        lax.fori_loop(0, line // step, widen, 0)
        start = (member(where_ref, rows, offsets) * CHUNKS + chunk) * block
        start = start + lax.rem(where_ref[3] - d + decks, decks) * line
        to = pl.ds(pl.multiple_of(start, line), line)
        copies.append(
            pltpu.make_async_copy(wide.at[done : done + line], out_ref.at[to], sems.at[n])
        )
        copies[-1].start()
    for copy in copies:
        copy.wait()


def put(where, result, total_rows, rows, decks, chosen):
    values = [value for _, _, value in chosen]
    block, width = values[0].shape
    line = block // decks
    runs = [
        (n, offsets, chunk, d) for n, (chunk, offsets, _) in enumerate(chosen) for d in range(decks)
    ]
    given = [] if result is None else [result]
    vmem, anywhere = (pl.BlockSpec(memory_space=m) for m in (pltpu.VMEM, pl.ANY))
    wide = ((len(runs) * line, width), jnp.float32)
    return pl.pallas_call(
        functools.partial(place_kernel, (rows, decks, line, block, runs), len(values), len(given)),
        out_shape=jax.ShapeDtypeStruct((total_rows, width), jnp.float32),
        in_specs=[pl.BlockSpec(memory_space=pltpu.SMEM)]
        + [vmem] * len(values)
        + [anywhere] * len(given),
        out_specs=anywhere,
        scratch_shapes=[pltpu.VMEM(*wide), pltpu.SemaphoreType.DMA((len(runs),))],
        input_output_aliases={1 + len(values): 0} if given else {},
        compiler_params=pltpu.CompilerParams(
            vmem_limit_bytes=grant([wide] + [(v.shape, v.dtype) for v in values], 2**21)
        ),
        cost_estimate=pl.CostEstimate(
            flops=0, bytes_accessed=6 * wide[0][0] * width, transcendentals=0
        ),
    )(where, *values, *given)


def outer_rows(cells):
    across = cells.shape[3]
    decks = lax.axis_size("deck")
    rows = jnp.where(lax.axis_index("side") == 1, cells[..., across - 2 :, :], cells[..., :2, :])
    joints = [(2 * d + 1, 2 * d + 2) for d in range(decks - 1)]
    return lax.ppermute(rows, SPAN, joints + [(j, i) for i, j in joints])


def edge_piece(outer, weight):
    layers, height, comps, _, width = outer.shape
    across = weight.shape[1]
    outer = outer.transpose(0, 1, 3, 2, 4).reshape(layers, 2 * height, comps * width)
    parts = []
    for _ in range(WEIGHT_PARTS):
        part = lax.reduce_precision(weight, 8, 7)
        weight = weight - part
        parts.append(part.astype(jnp.bfloat16))
    tile = jnp.concatenate(parts, axis=2)
    total = pl.cdiv(2 * height + across, TILE) * TILE
    outer = jnp.pad(outer, ((0, 0), (0, total - across - 2 * height), (0, 0)))
    tile = jnp.pad(tile, ((0, 0), (0, 0), (0, comps * width - tile.shape[2])))
    return jnp.concatenate([outer, tile], axis=1)


def spread_near(piece):
    rows = lax.axis_size("row")
    got = {(0, 0): piece, (0, 1): rotate(piece, "side")}
    for r in range(1, rows):
        got[(r, 0)] = rotate(piece, "row", r)
        pairs = [(2 * i + s, 2 * ((i + r) % rows) + 1 - s) for i in range(rows) for s in range(2)]
        got[(r, 1)] = lax.ppermute(piece, DIAGONAL, pairs)
    return got


def spread_cores(got):
    out = {}
    for (r, s), value in got.items():
        out[(r, 0, s)] = value
        out[(r, 1, s)] = rotate(value, "core")
    return out


def sum_over_decks(terms, decks):
    if len(terms) > 1:
        parts = [terms[0]] + [rotate(terms[r], "deck", r) for r in range(1, decks)]
    else:
        width = terms[0].shape[1]
        parts = list(lax.all_to_all(terms[0].reshape(decks, -1, width), "deck", 0, 0))
    return sum(part.astype(jnp.float32) for part in parts).astype(jnp.bfloat16)


def shards(velocity_modes, cell_weight):
    width = velocity_modes.shape[-1]
    rows, decks = lax.axis_size("row"), lax.axis_size("deck")
    members = rows * 4
    share = width // members // CHUNKS
    where = jnp.stack([lax.axis_index(a) for a in ("row", "core", "side", "deck")]).astype(jnp.int32)
    outs = decks if share % (2 * decks) == 0 else 1

    cells = velocity_modes.transpose(0, 2, 3, 1, 4)
    outer = outer_rows(cells)
    near = spread_near(cells)
    outer, near = lax.optimization_barrier((outer, near))
    near[(0, 0)] = cells
    blocks = spread_cores(near)
    edges = spread_cores(spread_near(edge_piece(outer, cell_weight)))
    offsets = list(blocks)
    blocks, edges = ([d[o] for o in offsets] for d in (blocks, edges))
    slopes = plane_slopes(where, blocks, edges, offsets, rows)
    terms = [plane_terms(where, *slopes, n, share, rows, decks, outs) for n in range(CHUNKS)]

    def put_all(result, chosen):
        return put(where, result, width * width, rows, decks, chosen)

    result = None
    waiting = []
    for n in range(CHUNKS):
        mine = sum_over_decks(terms[n], decks)
        piece = jnp.concatenate([mine] + [rotate(mine, "deck", r) for r in range(1, decks)], axis=0)
        got = spread_near(piece)
        near = [(n, (r, 0, s), v) for (r, s), v in got.items()]
        if n > 0:
            result = put_all(result, waiting.pop(0))
            near, result = lax.optimization_barrier(([v for _, _, v in near], result))
            near = [(n, (r, 0, s), v) for (r, s), v in zip(got, near)]
        waiting.append(near + [(n, (r, 1, s), rotate(v, "core")) for _, (r, _, s), v in near])
    *chosen, last = waiting.pop(0)
    result = put_all(result, chosen)
    result = put_all(result, [last])
    return result.reshape(width, width, width)


def solution(mesh):
    streams, spans = (mesh.shape[name] for name in ("stream", "span"))
    split = Mesh(mesh.devices.reshape(streams // 2, 2, spans // 2, 2), STREAM + SPAN)
    placed = (P(STREAM, SPAN, None, None, None), P(STREAM, SPAN, None))
    return jax.shard_map(shards, mesh=split, in_specs=placed, out_specs=P(), check_vma=False)
```

```python
import functools
import math

import jax
import jax.numpy as jnp
from jax import lax
from jax.experimental import pallas as pl
from jax.experimental.pallas import tpu as pltpu
from jax.sharding import Mesh, PartitionSpec as P

STREAM = ("row", "core")
SPAN = ("deck", "side")
DIAGONAL = ("row", "side")
WEIGHT_PARTS = 3
LANES = 128
TILE = 16
CHUNKS = 2
TURNED = (((1,), (1,)), ((), ()))


def rotate(value, axis, by=1):
    count = lax.axis_size(axis)
    return lax.ppermute(value, axis, [(i, (i + by) % count) for i in range(count)])


def member(where, rows, offsets):
    r, c, s = offsets
    row = lax.rem(where[0] - r + rows, rows)
    return (row * 2 + lax.rem(where[1] + c, 2)) * 2 + lax.rem(where[2] + s, 2)


def grant(shapes, slack=6 * 2**20):
    total = slack
    for shape, dtype in shapes:
        *outer, rows, columns = shape
        size = jnp.dtype(dtype).itemsize
        rows, columns = pl.cdiv(rows, TILE) * TILE, pl.cdiv(columns, LANES) * LANES
        total += math.prod(outer) * rows * columns * size
    return total


def slopes_kernel(sizes, offsets, where_ref, *refs):
    layers, height, across, width, rows = sizes
    members = len(offsets)
    blocks, edges = refs[:members], refs[members : members + 2]
    turned, phi, field, edge, *sources = refs[members + 2 :]
    count = members * layers * height * across
    depth = members // 2 * layers
    piece = 4 * count // depth
    parts = count // piece

    field[:2] = jnp.zeros_like(field[:2])
    field[members + 2 :] = jnp.zeros_like(field[members + 2 :])
    for n in range(members):
        field[member(where_ref, rows, offsets[n]) + 2] = blocks[n][...].astype(jnp.float32)
    for c in range(2):
        for r in range(rows):
            stream = lax.div(member(where_ref, rows, (r, c, 0)), 2)
            for h in range(2):
                upper = lax.rem(where_ref[2] + h, 2)
                edge[stream, upper] = edges[c][2 * r + h].astype(jnp.float32)

    index = lax.broadcasted_iota(jnp.int32, (across, width), 0)
    row, column = (lax.broadcasted_iota(jnp.int32, (2 * width, 2 * width), d) for d in range(2))
    eye = (row == column).astype(jnp.bfloat16)

    def stencil(x, b, source):
        def layer_at(step, side):
            at = x + step + layers
            return lax.div(at, layers) * 2 + side, lax.rem(at, layers)

        for side in range(2):
            here_at, layer = layer_at(0, side)
            at = here_at - 2
            stream = lax.div(at, 2)
            tile = field[here_at, layer, 3 * height]
            weights = tile
            for part in range(1, WEIGHT_PARTS):
                weights = weights + pltpu.roll(tile, width - part * height, 1)
            beside = {step: layer_at(step, side) for step in (-2, -1, 1, 2)}
            found = []
            for z in range(height):
                weight = jnp.broadcast_to(weights[:, z : z + 1], (across, width))
                twelfth, half = weight * (1.0 / 12.0), weight * 0.5
                base = 2 * z // across * across
                here = field[here_at, layer, 3 * z + b]
                along = {step: field[m, l, 3 * z + b] for step, (m, l) in beside.items()}
                value_x = 8.0 * (along[1] - along[-1]) - (along[2] - along[-2])

                columns = slice(b * width, (b + 1) * width)
                outer = edge[stream, side, layer, base : base + across, columns]
                beyond = field[here_at + 1 - 2 * side, layer, 3 * z + b]
                if side == 0:
                    prev = pltpu.roll(outer, (across - 2 - (2 * z - base)) % across, 0)
                    after = beyond
                else:
                    prev = beyond
                    after = pltpu.roll(outer, (across - (2 * z - base)) % across, 0)
                near = pltpu.roll(jnp.where(index < 1, after, here), across - 1, 0)
                near = near - pltpu.roll(jnp.where(index >= across - 1, prev, here), 1, 0)
                far = pltpu.roll(jnp.where(index < 2, after, here), across - 2, 0)
                far = far - pltpu.roll(jnp.where(index >= across - 2, prev, here), 2, 0)
                value_y = 8.0 * near - far

                value_z = jnp.zeros_like(here)
                if z < height - 1:
                    value_z = field[here_at, layer, 3 * (z + 1) + b]
                if z > 0:
                    value_z = value_z - field[here_at, layer, 3 * (z - 1) + b]
                found.append((here, value_x * twelfth, value_y * twelfth, value_z * half))
                if len(found) * across == TILE:
                    start = ((at * layers + layer) * height + z + 1) * across - TILE
                    to = pl.ds(pl.multiple_of(start, TILE), TILE)
                    for q in range(4):
                        value = jnp.concatenate([f[q] for f in found], axis=0)
                        columns = slice(q % 2 * width, (q % 2 + 1) * width)
                        source[q // 2, to, columns] = value.astype(jnp.bfloat16)
                    found = []

    def turn(x, b, source):
        both, part = lax.div(x, parts), lax.rem(x, parts)
        at = pl.ds(pl.multiple_of(part * piece, piece), piece)
        value = lax.dot_general(eye, source[both, at, :], TURNED, preferred_element_type=jnp.float32)
        for n in range(2):
            turned[2 * both + n, b, :, at] = value[n * width : (n + 1) * width].astype(jnp.bfloat16)

        @pl.when(both == 0)
        def _():
            phi[b, :, at] = value[:width]

    for step in range(4):

        def two_layers(x, _):
            if step < 3:
                stencil(2 * x, step, sources[step % 2])
                stencil(2 * x + 1, step, sources[step % 2])
            if step > 0:
                turn(x, step - 1, sources[(step - 1) % 2])
            return 0

        lax.fori_loop(0, depth // 2, two_layers, 0)


def plane_slopes(where, blocks, edges, offsets, rows, comps):
    layers, planes, across, width = blocks[0].shape
    height = planes // comps
    members = len(blocks)
    count = members * layers * height * across
    sizes = (layers, height, across, width, rows)
    vmem = pl.BlockSpec(memory_space=pltpu.VMEM)
    results = [
        ((4, comps, width, count), jnp.bfloat16),
        ((comps, width, count), jnp.float32),
    ]
    scratch = [
        ((members + 4,) + blocks[0].shape, jnp.float32),
        ((members // 2, 2) + edges[0].shape[1:], jnp.float32),
        ((2, count, 2 * width), jnp.bfloat16),
        ((2, count, 2 * width), jnp.bfloat16),
    ]
    inputs = [(v.shape, v.dtype) for v in blocks + edges]
    return pl.pallas_call(
        functools.partial(slopes_kernel, sizes, offsets),
        out_shape=[jax.ShapeDtypeStruct(*result) for result in results],
        in_specs=[pl.BlockSpec(memory_space=pltpu.SMEM)] + [vmem] * (members + 2),
        out_specs=[vmem] * len(results),
        scratch_shapes=[pltpu.VMEM(*shape) for shape in scratch],
        compiler_params=pltpu.CompilerParams(vmem_limit_bytes=grant(results + scratch + inputs)),
        cost_estimate=pl.CostEstimate(
            flops=2 * 12 * count * width * width, bytes_accessed=2**22, transcendentals=0
        ),
    )(where, *blocks, *edges)


def terms_kernel(share, chunk, rows, decks, where_ref, turned, phi, *refs):
    out_refs = [ref for ref in refs if len(ref.shape) == 2]
    own, *quads = refs[len(out_refs) :]
    outs = len(out_refs)
    width, count = turned.shape[2:]
    base = (member(where_ref, rows, (0, 0, 0)) * CHUNKS + chunk) * share
    first = where_ref[3] * (share // decks) if outs > 1 else 0
    together = min(4, share)
    for i in range(share):
        mode = base + lax.rem(i + first, share)
        for b in range(3):
            own[b, i] = jnp.broadcast_to(phi[b, pl.ds(mode, 1), :], (TILE, count))
    for group in range(share // together):
        modes = range(group * together, (group + 1) * together)
        quad = quads[group % len(quads)]
        for a in range(3):
            for start in range(0, count, LANES):
                lanes = slice(start, start + LANES)
                spread = [[own[b, mode, :, lanes] for b in range(3)] for mode in modes]
                for k in range(0, width, TILE):
                    slope = [
                        turned[1 + a, b, k : k + TILE, lanes].astype(jnp.float32) for b in range(3)
                    ]
                    for i, row in enumerate(spread):
                        value = row[0] * slope[0] + row[1] * slope[1] + row[2] * slope[2]
                        at = i * width + k
                        quad[a, at : at + TILE, lanes] = value.astype(jnp.bfloat16)
        total = sum(
            lax.dot_general(turned[0, a], quad[a], TURNED, preferred_element_type=jnp.float32)
            for a in range(3)
        )
        for i, mode in enumerate(modes):
            start = mode * width
            out_ref = out_refs[start * outs // (share * width)]
            start = start % (share * width // outs)
            out_ref[start : start + width, :] = total[:, i * width : (i + 1) * width].astype(
                out_ref.dtype
            )


def plane_terms(where, turned, phi, chunk, share, rows, decks, outs):
    width, count = turned.shape[2:]
    vmem = pl.BlockSpec(memory_space=pltpu.VMEM)
    dtypes = [jnp.float32 if outs > 1 and n == 0 else jnp.bfloat16 for n in range(outs)]
    results = [((share * width // outs, width), t) for t in dtypes]
    scratch = [((3, share, TILE, count), jnp.float32)]
    together = min(4, share)
    scratch += [((3, together * width, count), jnp.bfloat16)] * min(2, share // together)
    inputs = [(v.shape, v.dtype) for v in (turned, phi)]
    return pl.pallas_call(
        functools.partial(terms_kernel, share, chunk, rows, decks),
        out_shape=[jax.ShapeDtypeStruct(*result) for result in results],
        in_specs=[pl.BlockSpec(memory_space=pltpu.SMEM)] + [vmem] * 2,
        out_specs=[vmem] * outs,
        scratch_shapes=[pltpu.VMEM(*shape) for shape in scratch],
        compiler_params=pltpu.CompilerParams(vmem_limit_bytes=grant(results + scratch + inputs)),
        cost_estimate=pl.CostEstimate(
            flops=2 * share * width * width * count * 3, bytes_accessed=2**22, transcendentals=0
        ),
    )(where, turned, phi)


def place_kernel(plan, pieces, given, where_ref, *refs):
    rows, decks, line, block, runs = plan
    out_ref, wide, sems = refs[pieces + given :]
    step = math.gcd(line, LANES)
    copies = []
    for n, (piece, offsets, chunk, d) in enumerate(runs):
        done = n * line

        def widen(k, _):
            at = pl.multiple_of(k * step, step)
            wide[pl.ds(done + at, step), :] = refs[piece][pl.ds(d * line + at, step), :].astype(
                jnp.float32
            )
            return 0

        lax.fori_loop(0, line // step, widen, 0)
        start = (member(where_ref, rows, offsets) * CHUNKS + chunk) * block
        start = start + lax.rem(where_ref[3] - d + decks, decks) * line
        to = pl.ds(pl.multiple_of(start, line), line)
        copies.append(
            pltpu.make_async_copy(wide.at[done : done + line], out_ref.at[to], sems.at[n])
        )
        copies[-1].start()
    for copy in copies:
        copy.wait()


def put(where, result, total_rows, rows, decks, chosen):
    values = [value for _, _, value in chosen]
    block, width = values[0].shape
    line = block // decks
    runs = [
        (n, offsets, chunk, d) for n, (chunk, offsets, _) in enumerate(chosen) for d in range(decks)
    ]
    given = [] if result is None else [result]
    vmem, anywhere = (pl.BlockSpec(memory_space=m) for m in (pltpu.VMEM, pl.ANY))
    wide = ((len(runs) * line, width), jnp.float32)
    return pl.pallas_call(
        functools.partial(place_kernel, (rows, decks, line, block, runs), len(values), len(given)),
        out_shape=jax.ShapeDtypeStruct((total_rows, width), jnp.float32),
        in_specs=[pl.BlockSpec(memory_space=pltpu.SMEM)]
        + [vmem] * len(values)
        + [anywhere] * len(given),
        out_specs=anywhere,
        scratch_shapes=[pltpu.VMEM(*wide), pltpu.SemaphoreType.DMA((len(runs),))],
        input_output_aliases={1 + len(values): 0} if given else {},
        compiler_params=pltpu.CompilerParams(
            vmem_limit_bytes=grant([wide] + [(v.shape, v.dtype) for v in values], 2**21)
        ),
        cost_estimate=pl.CostEstimate(
            flops=0, bytes_accessed=6 * wide[0][0] * width, transcendentals=0
        ),
    )(where, *values, *given)


def raw_piece(cells, weight):
    layers, height, comps, across, width = cells.shape
    parts = []
    for _ in range(WEIGHT_PARTS):
        part = lax.reduce_precision(weight, 8, 7)
        weight = weight - part
        parts.append(part.astype(jnp.bfloat16))
    tile = jnp.concatenate(parts, axis=2)
    tile = jnp.pad(tile, ((0, 0), (0, 0), (0, width - tile.shape[2])))
    cells = cells.reshape(layers, height * comps, across, width)
    return jnp.concatenate([cells, tile[:, None]], axis=1)


def outer_rows(cells):
    layers, height, comps, across, width = cells.shape
    rows, decks = lax.axis_size("row"), lax.axis_size("deck")
    ends = jnp.where(lax.axis_index("side") == 1, cells[..., across - 2 :, :], cells[..., :2, :])
    ends = ends.transpose(0, 1, 3, 2, 4).reshape(layers, 2 * height, comps * width)
    total = pl.cdiv(2 * height, TILE) * TILE
    ends = jnp.pad(ends, ((0, 0), (0, total - 2 * height), (0, 0)))
    found = []
    for r in range(rows):
        for other in range(2):
            pairs = []
            for i in range(rows):
                to = (i + r) % rows
                for d in range(decks - 1):
                    low, high = 2 * (i * decks + d) + 1, 2 * (i * decks + d + 1)
                    pairs.append((low, 2 * (to * decks + d + 1) + other))
                    pairs.append((high, 2 * (to * decks + d) + 1 - other))
            found.append(lax.ppermute(ends, ("row",) + SPAN, pairs))
    return jnp.stack(found)


def spread_near(piece):
    rows = lax.axis_size("row")
    got = {(0, 0): piece, (0, 1): rotate(piece, "side")}
    for r in range(1, rows):
        got[(r, 0)] = rotate(piece, "row", r)
        pairs = [(2 * i + s, 2 * ((i + r) % rows) + 1 - s) for i in range(rows) for s in range(2)]
        got[(r, 1)] = lax.ppermute(piece, DIAGONAL, pairs)
    return got


def spread_cores(got):
    out = {}
    for (r, s), value in got.items():
        out[(r, 0, s)] = value
        out[(r, 1, s)] = rotate(value, "core")
    return out


def parts_over_decks(terms, decks):
    if len(terms) > 1:
        return [terms[0]] + [rotate(terms[r], "deck", r) for r in range(1, decks)]
    width = terms[0].shape[1]
    return list(lax.all_to_all(terms[0].reshape(decks, -1, width), "deck", 0, 0))


def shards(velocity_modes, cell_weight):
    width = velocity_modes.shape[-1]
    rows, decks = lax.axis_size("row"), lax.axis_size("deck")
    members = rows * 4
    share = width // members // CHUNKS
    where = jnp.stack([lax.axis_index(a) for a in ("row", "core", "side", "deck")]).astype(jnp.int32)
    outs = decks if share % (2 * decks) == 0 else 1

    cells = velocity_modes.transpose(0, 2, 3, 1, 4)
    blocks = spread_cores(spread_near(raw_piece(cells, cell_weight)))
    offsets = list(blocks)
    outer = outer_rows(cells)
    edges = [outer, rotate(outer, "core")]
    slopes = plane_slopes(where, list(blocks.values()), edges, offsets, rows, cells.shape[2])
    terms = [plane_terms(where, *slopes, n, share, rows, decks, outs) for n in range(CHUNKS)]

    def put_all(result, chosen):
        return put(where, result, width * width, rows, decks, chosen)

    parts = [parts_over_decks(t, decks) for t in terms]
    parts[0], parts[1][0] = lax.optimization_barrier((parts[0], parts[1][0]))
    pieces = []
    for n in range(CHUNKS):
        mine = sum(part.astype(jnp.float32) for part in parts[n]).astype(jnp.bfloat16)
        pieces.append(
            jnp.concatenate([mine] + [rotate(mine, "deck", r) for r in range(1, decks)], axis=0)
        )

    def to_core(chosen):
        return [(n, (r, 1, s), rotate(v, "core")) for n, (r, _, s), v in chosen]

    result = None
    near, far = [], []
    for n, piece in enumerate(pieces):
        across = rotate(piece, "side")
        along = [rotate(piece, "row", r) for r in range(1, rows)]
        near.append([piece, across] + along)
    for n in range(CHUNKS):
        if n > 0:
            near[n], result = lax.optimization_barrier((near[n], result))
        piece, across, *along = near[n]
        if n % 2 == 0:
            diagonal = [rotate(across, "row", r) for r in range(1, rows)]
        else:
            diagonal = [rotate(v, "side") for v in along]
        if n < CHUNKS - 1:
            near[n], near[n + 1][0] = lax.optimization_barrier((near[n], near[n + 1][0]))
        chosen = [(n, (0, 0, 0), near[n][0]), (n, (0, 0, 1), near[n][1])]
        chosen += [(n, (r, 0, 0), v) for r, v in enumerate(near[n][2:], 1)]
        cores = to_core(chosen)
        if n < CHUNKS - 1:
            result = put_all(result, chosen + cores)
            far = [(n, (r, 0, 1), v) for r, v in enumerate(diagonal, 1)]
            far += to_core(far)
        else:
            result = put_all(result, far + chosen)
            diagonal, result = lax.optimization_barrier((diagonal, result))
            far = [(n, (r, 0, 1), v) for r, v in enumerate(diagonal, 1)]
            result = put_all(result, cores + far)
            result = put_all(result, to_core(far))
    return result.reshape(width, width, width)


def solution(mesh):
    streams, spans = (mesh.shape[name] for name in ("stream", "span"))
    split = Mesh(mesh.devices.reshape(streams // 2, 2, spans // 2, 2), STREAM + SPAN)
    placed = (P(STREAM, SPAN, None, None, None), P(STREAM, SPAN, None))
    return jax.shard_map(shards, mesh=split, in_specs=placed, out_specs=P(), check_vma=False)
```

```python
import functools
import math

import jax
import jax.numpy as jnp
from jax import lax
from jax.experimental import pallas as pl
from jax.experimental.pallas import tpu as pltpu
from jax.sharding import Mesh, PartitionSpec as P

STREAM = ("row", "core")
SPAN = ("deck", "side")
DIAGONAL = ("row", "side")
WEIGHT_PARTS = 3
LANES = 128
TILE = 16
CHUNKS = 2
TURNED = (((1,), (1,)), ((), ()))


def rotate(value, axis, by=1):
    count = lax.axis_size(axis)
    return lax.ppermute(value, axis, [(i, (i + by) % count) for i in range(count)])


def member(where, rows, offsets):
    r, c, s = offsets
    row = lax.rem(where[0] - r + rows, rows)
    return (row * 2 + lax.rem(where[1] + c, 2)) * 2 + lax.rem(where[2] + s, 2)


def grant(shapes, slack=6 * 2**20):
    total = slack
    for shape, dtype in shapes:
        *outer, rows, columns = shape
        size = jnp.dtype(dtype).itemsize
        rows, columns = pl.cdiv(rows, TILE) * TILE, pl.cdiv(columns, LANES) * LANES
        total += math.prod(outer) * rows * columns * size
    return total


def slopes_kernel(sizes, offsets, where_ref, *refs):
    layers, height, across, width, rows = sizes
    members = len(offsets)
    blocks = refs[:members]
    turned, phi, field, *sources = refs[members:]
    count = members * layers * height * across
    depth = members // 2 * layers
    piece = 4 * count // depth
    parts = count // piece

    field[:2] = jnp.zeros_like(field[:2])
    field[members + 2 :] = jnp.zeros_like(field[members + 2 :])
    for n in range(members):
        field[member(where_ref, rows, offsets[n]) + 2] = blocks[n][...].astype(jnp.float32)
    index = lax.broadcasted_iota(jnp.int32, (across, width), 0)
    row, column = (lax.broadcasted_iota(jnp.int32, (2 * width, 2 * width), d) for d in range(2))
    eye = (row == column).astype(jnp.bfloat16)

    def stencil(x, b, source):
        def layer_at(step, side):
            at = x + step + layers
            return lax.div(at, layers) * 2 + side, lax.rem(at, layers)

        for side in range(2):
            here_at, layer = layer_at(0, side)
            at = here_at - 2
            tile = field[here_at, layer, 3 * height]
            weights = tile
            for part in range(1, WEIGHT_PARTS):
                weights = weights + pltpu.roll(tile, width - part * height, 1)
            beside = {step: layer_at(step, side) for step in (-2, -1, 1, 2)}
            found = []
            for z in range(height):
                weight = jnp.broadcast_to(weights[:, z : z + 1], (across, width))
                twelfth, half = weight * (1.0 / 12.0), weight * 0.5
                base = 2 * z // across * across
                here = field[here_at, layer, 3 * z + b]
                along = {step: field[m, l, 3 * z + b] for step, (m, l) in beside.items()}
                value_x = 8.0 * (along[1] - along[-1]) - (along[2] - along[-2])

                outer = field[here_at, layer, 3 * height + 1 + base // across * 3 + b]
                beyond = field[here_at + 1 - 2 * side, layer, 3 * z + b]
                if side == 0:
                    prev = pltpu.roll(outer, (across - 2 - (2 * z - base)) % across, 0)
                    after = beyond
                else:
                    prev = beyond
                    after = pltpu.roll(outer, (across - (2 * z - base)) % across, 0)
                near = pltpu.roll(jnp.where(index < 1, after, here), across - 1, 0)
                near = near - pltpu.roll(jnp.where(index >= across - 1, prev, here), 1, 0)
                far = pltpu.roll(jnp.where(index < 2, after, here), across - 2, 0)
                far = far - pltpu.roll(jnp.where(index >= across - 2, prev, here), 2, 0)
                value_y = 8.0 * near - far

                value_z = jnp.zeros_like(here)
                if z < height - 1:
                    value_z = field[here_at, layer, 3 * (z + 1) + b]
                if z > 0:
                    value_z = value_z - field[here_at, layer, 3 * (z - 1) + b]
                found.append((here, value_x * twelfth, value_y * twelfth, value_z * half))
                if len(found) * across == TILE:
                    start = ((at * layers + layer) * height + z + 1) * across - TILE
                    to = pl.ds(pl.multiple_of(start, TILE), TILE)
                    for q in range(4):
                        value = jnp.concatenate([f[q] for f in found], axis=0)
                        columns = slice(q % 2 * width, (q % 2 + 1) * width)
                        source[q // 2, to, columns] = value.astype(jnp.bfloat16)
                    found = []

    def turn(x, b, source):
        both, part = lax.div(x, parts), lax.rem(x, parts)
        at = pl.ds(pl.multiple_of(part * piece, piece), piece)
        value = lax.dot_general(eye, source[both, at, :], TURNED, preferred_element_type=jnp.float32)
        for n in range(2):
            turned[2 * both + n, b, :, at] = value[n * width : (n + 1) * width].astype(jnp.bfloat16)

        @pl.when(both == 0)
        def _():
            phi[b, :, at] = value[:width]

    for step in range(4):

        def two_layers(x, _):
            if step < 3:
                stencil(2 * x, step, sources[step % 2])
                stencil(2 * x + 1, step, sources[step % 2])
            if step > 0:
                turn(x, step - 1, sources[(step - 1) % 2])
            return 0

        lax.fori_loop(0, depth // 2, two_layers, 0)


def plane_slopes(where, blocks, offsets, rows, height, comps):
    layers, _, across, width = blocks[0].shape
    members = len(blocks)
    count = members * layers * height * across
    sizes = (layers, height, across, width, rows)
    vmem = pl.BlockSpec(memory_space=pltpu.VMEM)
    results = [
        ((4, comps, width, count), jnp.bfloat16),
        ((comps, width, count), jnp.float32),
    ]
    scratch = [
        ((members + 4,) + blocks[0].shape, jnp.float32),
        ((2, count, 2 * width), jnp.bfloat16),
        ((2, count, 2 * width), jnp.bfloat16),
    ]
    inputs = [(v.shape, v.dtype) for v in blocks]
    return pl.pallas_call(
        functools.partial(slopes_kernel, sizes, offsets),
        out_shape=[jax.ShapeDtypeStruct(*result) for result in results],
        in_specs=[pl.BlockSpec(memory_space=pltpu.SMEM)] + [vmem] * members,
        out_specs=[vmem] * len(results),
        scratch_shapes=[pltpu.VMEM(*shape) for shape in scratch],
        compiler_params=pltpu.CompilerParams(vmem_limit_bytes=grant(results + scratch + inputs)),
        cost_estimate=pl.CostEstimate(
            flops=2 * 12 * count * width * width, bytes_accessed=2**22, transcendentals=0
        ),
    )(where, *blocks)


def terms_kernel(share, chunk, rows, decks, where_ref, turned, phi, *refs):
    out_refs = [ref for ref in refs if len(ref.shape) == 2]
    own, *quads = refs[len(out_refs) :]
    outs = len(out_refs)
    width, count = turned.shape[2:]
    base = (member(where_ref, rows, (0, 0, 0)) * CHUNKS + chunk) * share
    first = where_ref[3] * (share // decks) if outs > 1 else 0
    together = min(4, share)
    for i in range(share):
        mode = base + lax.rem(i + first, share)
        for b in range(3):
            own[b, i] = jnp.broadcast_to(phi[b, pl.ds(mode, 1), :], (TILE, count))
    for group in range(share // together):
        modes = range(group * together, (group + 1) * together)
        quad = quads[group % len(quads)]
        for a in range(3):
            for start in range(0, count, LANES):
                lanes = slice(start, start + LANES)
                spread = [[own[b, mode, :, lanes] for b in range(3)] for mode in modes]
                for k in range(0, width, TILE):
                    slope = [
                        turned[1 + a, b, k : k + TILE, lanes].astype(jnp.float32) for b in range(3)
                    ]
                    for i, row in enumerate(spread):
                        value = row[0] * slope[0] + row[1] * slope[1] + row[2] * slope[2]
                        at = i * width + k
                        quad[a, at : at + TILE, lanes] = value.astype(jnp.bfloat16)
        total = sum(
            lax.dot_general(turned[0, a], quad[a], TURNED, preferred_element_type=jnp.float32)
            for a in range(3)
        )
        for i, mode in enumerate(modes):
            start = mode * width
            out_ref = out_refs[start * outs // (share * width)]
            start = start % (share * width // outs)
            out_ref[start : start + width, :] = total[:, i * width : (i + 1) * width].astype(
                out_ref.dtype
            )


def plane_terms(where, turned, phi, chunk, share, rows, decks, outs):
    width, count = turned.shape[2:]
    vmem = pl.BlockSpec(memory_space=pltpu.VMEM)
    dtypes = [jnp.float32 if outs > 1 and n == 0 else jnp.bfloat16 for n in range(outs)]
    results = [((share * width // outs, width), t) for t in dtypes]
    scratch = [((3, share, TILE, count), jnp.float32)]
    together = min(4, share)
    scratch += [((3, together * width, count), jnp.bfloat16)] * min(2, share // together)
    inputs = [(v.shape, v.dtype) for v in (turned, phi)]
    return pl.pallas_call(
        functools.partial(terms_kernel, share, chunk, rows, decks),
        out_shape=[jax.ShapeDtypeStruct(*result) for result in results],
        in_specs=[pl.BlockSpec(memory_space=pltpu.SMEM)] + [vmem] * 2,
        out_specs=[vmem] * outs,
        scratch_shapes=[pltpu.VMEM(*shape) for shape in scratch],
        compiler_params=pltpu.CompilerParams(vmem_limit_bytes=grant(results + scratch + inputs)),
        cost_estimate=pl.CostEstimate(
            flops=2 * share * width * width * count * 3, bytes_accessed=2**22, transcendentals=0
        ),
    )(where, turned, phi)


def place_kernel(plan, pieces, given, where_ref, *refs):
    rows, decks, line, runs = plan
    out_ref, wide, sems = refs[pieces + given :]
    step = math.gcd(line, LANES)
    copies = []
    for n, (piece, offsets, chunk, d, first) in enumerate(runs):
        done = n * line

        def widen(k, _):
            at = pl.multiple_of(k * step, step)
            wide[pl.ds(done + at, step), :] = refs[piece][pl.ds(first * line + at, step), :].astype(
                jnp.float32
            )
            return 0

        lax.fori_loop(0, line // step, widen, 0)
        start = (member(where_ref, rows, offsets) * CHUNKS + chunk) * decks * line
        start = start + lax.rem(where_ref[3] - d + decks, decks) * line
        to = pl.ds(pl.multiple_of(start, line), line)
        copies.append(
            pltpu.make_async_copy(wide.at[done : done + line], out_ref.at[to], sems.at[n])
        )
        copies[-1].start()
    for copy in copies:
        copy.wait()


def put(where, result, total_rows, rows, decks, chosen, line):
    values = [value for _, _, value in chosen]
    width = values[0].shape[1]
    runs = [
        (n, offsets, chunk, d, at)
        for n, (chunk, parts, _) in enumerate(chosen)
        for at, (offsets, d) in enumerate((o, d) for o, ds in parts for d in ds)
    ]
    given = [] if result is None else [result]
    vmem, anywhere = (pl.BlockSpec(memory_space=m) for m in (pltpu.VMEM, pl.ANY))
    wide = ((len(runs) * line, width), jnp.float32)
    return pl.pallas_call(
        functools.partial(place_kernel, (rows, decks, line, runs), len(values), len(given)),
        out_shape=jax.ShapeDtypeStruct((total_rows, width), jnp.float32),
        in_specs=[pl.BlockSpec(memory_space=pltpu.SMEM)]
        + [vmem] * len(values)
        + [anywhere] * len(given),
        out_specs=anywhere,
        scratch_shapes=[pltpu.VMEM(*wide), pltpu.SemaphoreType.DMA((len(runs),))],
        input_output_aliases={1 + len(values): 0} if given else {},
        compiler_params=pltpu.CompilerParams(
            vmem_limit_bytes=grant([wide] + [(v.shape, v.dtype) for v in values], 2**21)
        ),
        cost_estimate=pl.CostEstimate(
            flops=0, bytes_accessed=6 * wide[0][0] * width, transcendentals=0
        ),
    )(where, *values, *given)


def outer_rows(cells):
    across = cells.shape[3]
    decks = lax.axis_size("deck")
    ends = jnp.where(lax.axis_index("side") == 1, cells[..., across - 2 :, :], cells[..., :2, :])
    joints = [(2 * d + 1, 2 * d + 2) for d in range(decks - 1)]
    return lax.ppermute(ends, SPAN, joints + [(j, i) for i, j in joints])


def whole_piece(cells, outer, weight):
    layers, height, comps, across, width = cells.shape
    parts = []
    for _ in range(WEIGHT_PARTS):
        part = lax.reduce_precision(weight, 8, 7)
        weight = weight - part
        parts.append(part.astype(jnp.bfloat16))
    tile = jnp.concatenate(parts, axis=2)
    tile = jnp.pad(tile, ((0, 0), (0, 0), (0, width - tile.shape[2])))
    cells = cells.reshape(layers, height * comps, across, width)
    outer = outer.transpose(0, 1, 3, 2, 4).reshape(layers, 2 * height, comps, width)
    groups = pl.cdiv(2 * height, across)
    outer = jnp.pad(outer, ((0, 0), (0, groups * across - 2 * height), (0, 0), (0, 0)))
    outer = outer.reshape(layers, groups, across, comps, width).transpose(0, 1, 3, 2, 4)
    outer = outer.reshape(layers, groups * comps, across, width)
    return jnp.concatenate([cells, tile[:, None], outer], axis=1)


def spread_near(piece):
    rows = lax.axis_size("row")
    got = {(0, 0): piece, (0, 1): rotate(piece, "side")}
    for r in range(1, rows):
        got[(r, 0)] = rotate(piece, "row", r)
        pairs = [(2 * i + s, 2 * ((i + r) % rows) + 1 - s) for i in range(rows) for s in range(2)]
        got[(r, 1)] = lax.ppermute(piece, DIAGONAL, pairs)
    return got


def spread_cores(got):
    out = {}
    for (r, s), value in got.items():
        out[(r, 0, s)] = value
        out[(r, 1, s)] = rotate(value, "core")
    return out


def parts_over_decks(terms, decks):
    if len(terms) > 1:
        return [terms[0]] + [rotate(terms[r], "deck", r) for r in range(1, decks)]
    width = terms[0].shape[1]
    return list(lax.all_to_all(terms[0].reshape(decks, -1, width), "deck", 0, 0))


def shards(velocity_modes, cell_weight):
    width = velocity_modes.shape[-1]
    rows, decks = lax.axis_size("row"), lax.axis_size("deck")
    members = rows * 4
    share = width // members // CHUNKS
    where = jnp.stack([lax.axis_index(a) for a in ("row", "core", "side", "deck")]).astype(jnp.int32)
    outs = decks if share % (2 * decks) == 0 else 1

    cells = velocity_modes.transpose(0, 2, 3, 1, 4)
    blocks = spread_cores(spread_near(whole_piece(cells, outer_rows(cells), cell_weight)))
    offsets = list(blocks)
    height, comps = cells.shape[1:3]
    slopes = plane_slopes(where, list(blocks.values()), offsets, rows, height, comps)
    terms = [plane_terms(where, *slopes, n, share, rows, decks, outs) for n in range(CHUNKS)]

    line = share * width // decks
    every = range(decks)
    half = decks // 2

    def put_all(result, chosen):
        return put(where, result, width * width, rows, decks, chosen, line)

    parts = [parts_over_decks(t, decks) for t in terms]
    pieces = []
    for n in range(CHUNKS):
        mine = sum(part.astype(jnp.float32) for part in parts[n]).astype(jnp.bfloat16)
        pieces.append(
            jnp.concatenate([mine] + [rotate(mine, "deck", r) for r in range(1, decks)], axis=0)
        )

    def to_core(chosen):
        joined = rotate(jnp.concatenate([v for _, _, v in chosen], axis=0), "core")
        parts = [((r, 1, s), ds) for _, ps, _ in chosen for (r, _, s), ds in ps]
        return [(chosen[0][0], parts, joined)]

    result = None
    waiting = []
    for n, piece in enumerate(pieces):
        across = rotate(piece, "side")
        along = [rotate(piece, "row", r) for r in range(1, rows)]
        near = [(n, [((0, 0, 0), every)], piece), (n, [((0, 0, 1), every)], across)]
        near += [(n, [((r, 0, 0), every)], v) for r, v in enumerate(along, 1)]
        halves = [across[: half * line]] + [v[half * line :] for v in along]
        if waiting:
            result = put_all(result, waiting.pop(0))
            halves, result = lax.optimization_barrier((halves, result))
        far = [
            (n, [((r, 0, 1), every[:half])], rotate(halves[0], "row", r)) for r in range(1, rows)
        ]
        far += [
            (n, [((r, 0, 1), every[half:])], rotate(halves[r], "side")) for r in range(1, rows)
        ]
        if n < CHUNKS - 1:
            waiting += [near, far + to_core(near + far)]
        else:
            core = to_core(near)
            result = put_all(result, sum(waiting, []) + near)
            last, result = lax.optimization_barrier(([v for _, _, v in far], result))
            far = [(n, ps, v) for (_, ps, _), v in zip(far, last)]
            result = put_all(result, core + far)
            result = put_all(result, to_core(far))
    return result.reshape(width, width, width)


def solution(mesh):
    streams, spans = (mesh.shape[name] for name in ("stream", "span"))
    split = Mesh(mesh.devices.reshape(streams // 2, 2, spans // 2, 2), STREAM + SPAN)
    placed = (P(STREAM, SPAN, None, None, None), P(STREAM, SPAN, None))
    return jax.shard_map(shards, mesh=split, in_specs=placed, out_specs=P(), check_vma=False)
```

```python
import functools
import math

import jax
import jax.numpy as jnp
from jax import lax
from jax.experimental import pallas as pl
from jax.experimental.pallas import tpu as pltpu
from jax.sharding import Mesh, PartitionSpec as P

STREAM = ("row", "core")
SPAN = ("deck", "side")
DIAGONAL = ("row", "side")
WEIGHT_PARTS = 3
LANES = 128
TILE = 16
CHUNKS = 2
TURNED = (((1,), (1,)), ((), ()))


def rotate(value, axis, by=1):
    count = lax.axis_size(axis)
    return lax.ppermute(value, axis, [(i, (i + by) % count) for i in range(count)])


def member(where, rows, offsets):
    r, c, s = offsets
    row = lax.rem(where[0] - r + rows, rows)
    return (row * 2 + lax.rem(where[1] + c, 2)) * 2 + lax.rem(where[2] + s, 2)


def grant(shapes, slack=6 * 2**20):
    total = slack
    for shape, dtype in shapes:
        *outer, rows, columns = shape
        size = jnp.dtype(dtype).itemsize
        rows, columns = pl.cdiv(rows, TILE) * TILE, pl.cdiv(columns, LANES) * LANES
        total += math.prod(outer) * rows * columns * size
    return total


def slopes_kernel(sizes, offsets, where_ref, *refs):
    layers, height, across, width, rows = sizes
    members = len(offsets)
    blocks = refs[:members]
    turned, phi, field, *sources = refs[members:]
    count = members * layers * height * across
    depth = members // 2 * layers
    piece = 4 * count // depth
    parts = count // piece

    field[:2] = jnp.zeros_like(field[:2])
    field[members + 2 :] = jnp.zeros_like(field[members + 2 :])
    for n in range(members):
        field[member(where_ref, rows, offsets[n]) + 2] = blocks[n][...].astype(jnp.float32)
    index = lax.broadcasted_iota(jnp.int32, (across, width), 0)
    row, column = (lax.broadcasted_iota(jnp.int32, (2 * width, 2 * width), d) for d in range(2))
    eye = (row == column).astype(jnp.bfloat16)

    def stencil(x, b, source):
        def layer_at(step, side):
            at = x + step + layers
            return lax.div(at, layers) * 2 + side, lax.rem(at, layers)

        for side in range(2):
            here_at, layer = layer_at(0, side)
            at = here_at - 2
            tile = field[here_at, layer, 3 * height]
            weights = tile
            for part in range(1, WEIGHT_PARTS):
                weights = weights + pltpu.roll(tile, width - part * height, 1)
            beside = {step: layer_at(step, side) for step in (-2, -1, 1, 2)}
            found = []
            for z in range(height):
                weight = jnp.broadcast_to(weights[:, z : z + 1], (across, width))
                twelfth, half = weight * (1.0 / 12.0), weight * 0.5
                base = 2 * z // across * across
                here = field[here_at, layer, 3 * z + b]
                along = {step: field[m, l, 3 * z + b] for step, (m, l) in beside.items()}
                value_x = 8.0 * (along[1] - along[-1]) - (along[2] - along[-2])

                outer = field[here_at, layer, 3 * height + 1 + base // across * 3 + b]
                beyond = field[here_at + 1 - 2 * side, layer, 3 * z + b]
                if side == 0:
                    prev = pltpu.roll(outer, (across - 2 - (2 * z - base)) % across, 0)
                    after = beyond
                else:
                    prev = beyond
                    after = pltpu.roll(outer, (across - (2 * z - base)) % across, 0)
                near = pltpu.roll(jnp.where(index < 1, after, here), across - 1, 0)
                near = near - pltpu.roll(jnp.where(index >= across - 1, prev, here), 1, 0)
                far = pltpu.roll(jnp.where(index < 2, after, here), across - 2, 0)
                far = far - pltpu.roll(jnp.where(index >= across - 2, prev, here), 2, 0)
                value_y = 8.0 * near - far

                value_z = jnp.zeros_like(here)
                if z < height - 1:
                    value_z = field[here_at, layer, 3 * (z + 1) + b]
                if z > 0:
                    value_z = value_z - field[here_at, layer, 3 * (z - 1) + b]
                found.append((here, value_x * twelfth, value_y * twelfth, value_z * half))
                if len(found) * across == TILE:
                    start = ((at * layers + layer) * height + z + 1) * across - TILE
                    to = pl.ds(pl.multiple_of(start, TILE), TILE)
                    for q in range(4):
                        value = jnp.concatenate([f[q] for f in found], axis=0)
                        columns = slice(q % 2 * width, (q % 2 + 1) * width)
                        source[q // 2, to, columns] = value.astype(jnp.bfloat16)
                    found = []

    def turn(x, b, source):
        both, part = lax.div(x, parts), lax.rem(x, parts)
        at = pl.ds(pl.multiple_of(part * piece, piece), piece)
        value = lax.dot_general(eye, source[both, at, :], TURNED, preferred_element_type=jnp.float32)
        for n in range(2):
            turned[2 * both + n, b, :, at] = value[n * width : (n + 1) * width].astype(jnp.bfloat16)

        @pl.when(both == 0)
        def _():
            phi[b, :, at] = value[:width]

    for step in range(4):

        def two_layers(x, _):
            if step < 3:
                stencil(2 * x, step, sources[step % 2])
                stencil(2 * x + 1, step, sources[step % 2])
            if step > 0:
                turn(x, step - 1, sources[(step - 1) % 2])
            return 0

        lax.fori_loop(0, depth // 2, two_layers, 0)


def plane_slopes(where, blocks, offsets, rows, height, comps):
    layers, _, across, width = blocks[0].shape
    members = len(blocks)
    count = members * layers * height * across
    sizes = (layers, height, across, width, rows)
    vmem = pl.BlockSpec(memory_space=pltpu.VMEM)
    results = [
        ((4, comps, width, count), jnp.bfloat16),
        ((comps, width, count), jnp.float32),
    ]
    scratch = [
        ((members + 4,) + blocks[0].shape, jnp.float32),
        ((2, count, 2 * width), jnp.bfloat16),
        ((2, count, 2 * width), jnp.bfloat16),
    ]
    inputs = [(v.shape, v.dtype) for v in blocks]
    return pl.pallas_call(
        functools.partial(slopes_kernel, sizes, offsets),
        out_shape=[jax.ShapeDtypeStruct(*result) for result in results],
        in_specs=[pl.BlockSpec(memory_space=pltpu.SMEM)] + [vmem] * members,
        out_specs=[vmem] * len(results),
        scratch_shapes=[pltpu.VMEM(*shape) for shape in scratch],
        compiler_params=pltpu.CompilerParams(vmem_limit_bytes=grant(results + scratch + inputs)),
        cost_estimate=pl.CostEstimate(
            flops=2 * 12 * count * width * width, bytes_accessed=2**22, transcendentals=0
        ),
    )(where, *blocks)


def terms_kernel(share, chunk, rows, decks, where_ref, turned, phi, *refs):
    *out_refs, own, even, odd = refs
    quads = (even, odd)
    outs = len(out_refs)
    width, count = turned.shape[2:]
    base = (member(where_ref, rows, (0, 0, 0)) * CHUNKS + chunk) * share
    first = where_ref[3] * (share // decks) if outs > 1 else 0
    together = min(4, share)
    for i in range(share):
        mode = base + lax.rem(i + first, share)
        for b in range(3):
            own[b, i] = jnp.broadcast_to(phi[b, pl.ds(mode, 1), :], (TILE, count))
    units = [(group, a) for group in range(share // together) for a in range(3)]
    totals = {}
    for turn in range(len(units) + 1):
        if turn < len(units):
            group, a = units[turn]
            quad = quads[turn % 2]
            for start in range(0, count, LANES):
                lanes = slice(start, start + LANES)
                spread = [
                    [own[b, group * together + i, :, lanes] for b in range(3)]
                    for i in range(together)
                ]
                for k in range(0, width, TILE):
                    slope = [
                        turned[1 + a, b, k : k + TILE, lanes].astype(jnp.float32) for b in range(3)
                    ]
                    for i, row in enumerate(spread):
                        value = row[0] * slope[0] + row[1] * slope[1] + row[2] * slope[2]
                        at = i * width + k
                        quad[at : at + TILE, lanes] = value.astype(jnp.bfloat16)
        if turn > 0:
            group, a = units[turn - 1]
            value = lax.dot_general(
                turned[0, a], quads[(turn - 1) % 2][...], TURNED, preferred_element_type=jnp.float32
            )
            totals[group] = totals[group] + value if a else value
    for group, total in totals.items():
        for i in range(together):
            start = (group * together + i) * width
            out_ref = out_refs[start * outs // (share * width)]
            start = start % (share * width // outs)
            out_ref[start : start + width, :] = total[:, i * width : (i + 1) * width].astype(
                out_ref.dtype
            )


def plane_terms(where, turned, phi, chunk, share, rows, decks, outs):
    width, count = turned.shape[2:]
    vmem = pl.BlockSpec(memory_space=pltpu.VMEM)
    dtypes = [jnp.float32 if outs > 1 and n == 0 else jnp.bfloat16 for n in range(outs)]
    results = [((share * width // outs, width), t) for t in dtypes]
    scratch = [((3, share, TILE, count), jnp.float32)]
    together = min(4, share)
    scratch += [((together * width, count), jnp.bfloat16)] * 2
    inputs = [(v.shape, v.dtype) for v in (turned, phi)]
    return pl.pallas_call(
        functools.partial(terms_kernel, share, chunk, rows, decks),
        out_shape=[jax.ShapeDtypeStruct(*result) for result in results],
        in_specs=[pl.BlockSpec(memory_space=pltpu.SMEM)] + [vmem] * 2,
        out_specs=[vmem] * outs,
        scratch_shapes=[pltpu.VMEM(*shape) for shape in scratch],
        compiler_params=pltpu.CompilerParams(vmem_limit_bytes=grant(results + scratch + inputs)),
        cost_estimate=pl.CostEstimate(
            flops=2 * share * width * width * count * 3, bytes_accessed=2**22, transcendentals=0
        ),
    )(where, turned, phi)


def place_kernel(plan, pieces, given, where_ref, *refs):
    rows, decks, line, runs = plan
    out_ref, wide, sems = refs[pieces + given :]
    step = math.gcd(line, LANES)
    copies = []
    for n, (piece, offsets, chunk, d, first) in enumerate(runs):
        done = n * line

        def widen(k, _):
            at = pl.multiple_of(k * step, step)
            wide[pl.ds(done + at, step), :] = refs[piece][pl.ds(first * line + at, step), :].astype(
                jnp.float32
            )
            return 0

        lax.fori_loop(0, line // step, widen, 0)
        start = (member(where_ref, rows, offsets) * CHUNKS + chunk) * decks * line
        start = start + lax.rem(where_ref[3] - d + decks, decks) * line
        to = pl.ds(pl.multiple_of(start, line), line)
        copies.append(
            pltpu.make_async_copy(wide.at[done : done + line], out_ref.at[to], sems.at[n])
        )
        copies[-1].start()
    for copy in copies:
        copy.wait()


def put(where, result, total_rows, rows, decks, chosen, line):
    values = [value for _, _, value in chosen]
    width = values[0].shape[1]
    runs = [
        (n, offsets, chunk, d, at)
        for n, (chunk, parts, _) in enumerate(chosen)
        for at, (offsets, d) in enumerate((o, d) for o, ds in parts for d in ds)
    ]
    given = [] if result is None else [result]
    vmem, anywhere = (pl.BlockSpec(memory_space=m) for m in (pltpu.VMEM, pl.ANY))
    wide = ((len(runs) * line, width), jnp.float32)
    return pl.pallas_call(
        functools.partial(place_kernel, (rows, decks, line, runs), len(values), len(given)),
        out_shape=jax.ShapeDtypeStruct((total_rows, width), jnp.float32),
        in_specs=[pl.BlockSpec(memory_space=pltpu.SMEM)]
        + [vmem] * len(values)
        + [anywhere] * len(given),
        out_specs=anywhere,
        scratch_shapes=[pltpu.VMEM(*wide), pltpu.SemaphoreType.DMA((len(runs),))],
        input_output_aliases={1 + len(values): 0} if given else {},
        compiler_params=pltpu.CompilerParams(
            vmem_limit_bytes=grant([wide] + [(v.shape, v.dtype) for v in values], 2**21)
        ),
        cost_estimate=pl.CostEstimate(
            flops=0, bytes_accessed=6 * wide[0][0] * width, transcendentals=0
        ),
    )(where, *values, *given)


def outer_rows(cells):
    across = cells.shape[3]
    decks = lax.axis_size("deck")
    ends = jnp.where(lax.axis_index("side") == 1, cells[..., across - 2 :, :], cells[..., :2, :])
    joints = [(2 * d + 1, 2 * d + 2) for d in range(decks - 1)]
    return lax.ppermute(ends, SPAN, joints + [(j, i) for i, j in joints])


def whole_piece(cells, outer, weight):
    layers, height, comps, across, width = cells.shape
    parts = []
    for _ in range(WEIGHT_PARTS):
        part = lax.reduce_precision(weight, 8, 7)
        weight = weight - part
        parts.append(part.astype(jnp.bfloat16))
    tile = jnp.concatenate(parts, axis=2)
    tile = jnp.pad(tile, ((0, 0), (0, 0), (0, width - tile.shape[2])))
    cells = cells.reshape(layers, height * comps, across, width)
    outer = outer.transpose(0, 1, 3, 2, 4).reshape(layers, 2 * height, comps, width)
    groups = pl.cdiv(2 * height, across)
    outer = jnp.pad(outer, ((0, 0), (0, groups * across - 2 * height), (0, 0), (0, 0)))
    outer = outer.reshape(layers, groups, across, comps, width).transpose(0, 1, 3, 2, 4)
    outer = outer.reshape(layers, groups * comps, across, width)
    return jnp.concatenate([cells, tile[:, None], outer], axis=1)


def spread_near(piece):
    rows = lax.axis_size("row")
    got = {(0, 0): piece, (0, 1): rotate(piece, "side")}
    for r in range(1, rows):
        got[(r, 0)] = rotate(piece, "row", r)
        pairs = [(2 * i + s, 2 * ((i + r) % rows) + 1 - s) for i in range(rows) for s in range(2)]
        got[(r, 1)] = lax.ppermute(piece, DIAGONAL, pairs)
    return got


def spread_cores(got):
    out = {}
    for (r, s), value in got.items():
        out[(r, 0, s)] = value
        out[(r, 1, s)] = rotate(value, "core")
    return out


def parts_over_decks(terms, decks):
    if len(terms) > 1:
        return [terms[0]] + [rotate(terms[r], "deck", r) for r in range(1, decks)]
    width = terms[0].shape[1]
    return list(lax.all_to_all(terms[0].reshape(decks, -1, width), "deck", 0, 0))


def shards(velocity_modes, cell_weight):
    width = velocity_modes.shape[-1]
    rows, decks = lax.axis_size("row"), lax.axis_size("deck")
    members = rows * 4
    share = width // members // CHUNKS
    where = jnp.stack([lax.axis_index(a) for a in ("row", "core", "side", "deck")]).astype(jnp.int32)
    outs = decks if share % (2 * decks) == 0 else 1

    cells = velocity_modes.transpose(0, 2, 3, 1, 4)
    blocks = spread_cores(spread_near(whole_piece(cells, outer_rows(cells), cell_weight)))
    offsets = list(blocks)
    height, comps = cells.shape[1:3]
    slopes = plane_slopes(where, list(blocks.values()), offsets, rows, height, comps)
    terms = [
        list(plane_terms(where, *slopes, n, share, rows, decks, outs)) for n in range(CHUNKS)
    ]

    line = share * width // decks
    every = range(decks)
    half = decks // 2

    def put_all(result, chosen):
        return put(where, result, width * width, rows, decks, chosen, line)

    pieces = []
    for n in range(CHUNKS):
        parts = parts_over_decks(terms[n], decks)
        if n < CHUNKS - 1:
            parts, terms[n + 1][0] = lax.optimization_barrier((parts, terms[n + 1][0]))
        mine = sum(part.astype(jnp.float32) for part in parts).astype(jnp.bfloat16)
        if n < CHUNKS - 1:
            mine, later = lax.optimization_barrier((mine, terms[n + 1]))
            terms[n + 1] = list(later)
        pieces.append(
            jnp.concatenate([mine] + [rotate(mine, "deck", r) for r in range(1, decks)], axis=0)
        )

    def join(chosen):
        return chosen[0][0], sum((ps for _, ps, _ in chosen), []), jnp.concatenate(
            [v for _, _, v in chosen], axis=0
        )

    def to_core(n, parts, value):
        return n, [((r, 1, s), ds) for (r, _, s), ds in parts], rotate(value, "core")

    result = None
    waiting = []
    for n, piece in enumerate(pieces):
        across = rotate(piece, "side")
        along = [rotate(piece, "row", r) for r in range(1, rows)]
        near = [(n, [((0, 0, 0), every)], piece), (n, [((0, 0, 1), every)], across)]
        near += [(n, [((r, 0, 0), every)], v) for r, v in enumerate(along, 1)]
        halves = [across[: half * line]] + [v[half * line :] for v in along]
        if n > 0:
            result = put_all(result, waiting)
            halves, result = lax.optimization_barrier((halves, result))
        far = [
            (n, [((r, 0, 1), every[:half])], rotate(halves[0], "row", r)) for r in range(1, rows)
        ]
        far += [
            (n, [((r, 0, 1), every[half:])], rotate(halves[r], "side")) for r in range(1, rows)
        ]
        if n < CHUNKS - 1:
            waiting = near
            held = [(far, join(near + far))]
        else:
            first, second = join(near), []
            for values, (m, parts, joined) in held:
                joined, halves = lax.optimization_barrier((joined, halves))
                second += values + [to_core(m, parts, joined)]
            core = to_core(*first)
            result = put_all(result, second + near)
            last, result = lax.optimization_barrier(([v for _, _, v in far], result))
            far = [(n, ps, v) for (_, ps, _), v in zip(far, last)]
            result = put_all(result, [core] + far)
            result = put_all(result, [to_core(*join(far))])
    return result.reshape(width, width, width)


def solution(mesh):
    streams, spans = (mesh.shape[name] for name in ("stream", "span"))
    split = Mesh(mesh.devices.reshape(streams // 2, 2, spans // 2, 2), STREAM + SPAN)
    placed = (P(STREAM, SPAN, None, None, None), P(STREAM, SPAN, None))
    return jax.shard_map(shards, mesh=split, in_specs=placed, out_specs=P(), check_vma=False)
```

```python
import functools
import math

import jax
import jax.numpy as jnp
from jax import lax
from jax.experimental import pallas as pl
from jax.experimental.pallas import tpu as pltpu
from jax.sharding import Mesh, PartitionSpec as P

STREAM = ("row", "core")
SPAN = ("deck", "side")
DIAGONAL = ("row", "side")
WEIGHT_PARTS = 3
LANES = 128
TILE = 16
CHUNKS = 2
TURNED = (((1,), (1,)), ((), ()))


def rotate(value, axis, by=1):
    count = lax.axis_size(axis)
    return lax.ppermute(value, axis, [(i, (i + by) % count) for i in range(count)])


def member(where, rows, offsets):
    r, c, s = offsets
    row = lax.rem(where[0] - r + rows, rows)
    return (row * 2 + lax.rem(where[1] + c, 2)) * 2 + lax.rem(where[2] + s, 2)


def grant(shapes, slack=6 * 2**20):
    total = slack
    for shape, dtype in shapes:
        *outer, rows, columns = shape
        size = jnp.dtype(dtype).itemsize
        rows, columns = pl.cdiv(rows, TILE) * TILE, pl.cdiv(columns, LANES) * LANES
        total += math.prod(outer) * rows * columns * size
    return total


def slopes_kernel(sizes, offsets, where_ref, *refs):
    layers, height, across, width, rows = sizes
    members = len(offsets)
    blocks = refs[:members]
    turned, phi, field, *sources = refs[members:]
    count = members * layers * height * across
    depth = members // 2 * layers
    piece = 4 * count // depth
    parts = count // piece

    field[:2] = jnp.zeros_like(field[:2])
    field[members + 2 :] = jnp.zeros_like(field[members + 2 :])
    for n in range(members):
        field[member(where_ref, rows, offsets[n]) + 2] = blocks[n][...].astype(jnp.float32)
    index = lax.broadcasted_iota(jnp.int32, (across, width), 0)
    row, column = (lax.broadcasted_iota(jnp.int32, (2 * width, 2 * width), d) for d in range(2))
    eye = (row == column).astype(jnp.bfloat16)

    def stencil(x, b, source):
        def layer_at(step, side):
            at = x + step + layers
            return lax.div(at, layers) * 2 + side, lax.rem(at, layers)

        for side in range(2):
            here_at, layer = layer_at(0, side)
            at = here_at - 2
            tile = field[here_at, layer, 3 * height]
            weights = tile
            for part in range(1, WEIGHT_PARTS):
                weights = weights + pltpu.roll(tile, width - part * height, 1)
            beside = {step: layer_at(step, side) for step in (-2, -1, 1, 2)}
            found = []
            for z in range(height):
                weight = jnp.broadcast_to(weights[:, z : z + 1], (across, width))
                twelfth, half = weight * (1.0 / 12.0), weight * 0.5
                base = 2 * z // across * across
                here = field[here_at, layer, 3 * z + b]
                along = {step: field[m, l, 3 * z + b] for step, (m, l) in beside.items()}
                value_x = 8.0 * (along[1] - along[-1]) - (along[2] - along[-2])

                outer = field[here_at, layer, 3 * height + 1 + base // across * 3 + b]
                beyond = field[here_at + 1 - 2 * side, layer, 3 * z + b]
                if side == 0:
                    prev = pltpu.roll(outer, (across - 2 - (2 * z - base)) % across, 0)
                    after = beyond
                else:
                    prev = beyond
                    after = pltpu.roll(outer, (across - (2 * z - base)) % across, 0)
                near = pltpu.roll(jnp.where(index < 1, after, here), across - 1, 0)
                near = near - pltpu.roll(jnp.where(index >= across - 1, prev, here), 1, 0)
                far = pltpu.roll(jnp.where(index < 2, after, here), across - 2, 0)
                far = far - pltpu.roll(jnp.where(index >= across - 2, prev, here), 2, 0)
                value_y = 8.0 * near - far

                value_z = jnp.zeros_like(here)
                if z < height - 1:
                    value_z = field[here_at, layer, 3 * (z + 1) + b]
                if z > 0:
                    value_z = value_z - field[here_at, layer, 3 * (z - 1) + b]
                found.append((here, value_x * twelfth, value_y * twelfth, value_z * half))
                if len(found) * across == TILE:
                    start = ((at * layers + layer) * height + z + 1) * across - TILE
                    to = pl.ds(pl.multiple_of(start, TILE), TILE)
                    for q in range(4):
                        value = jnp.concatenate([f[q] for f in found], axis=0)
                        columns = slice(q % 2 * width, (q % 2 + 1) * width)
                        source[q // 2, to, columns] = value.astype(jnp.bfloat16)
                    found = []

    def turn(x, b, source):
        both, part = lax.div(x, parts), lax.rem(x, parts)
        at = pl.ds(pl.multiple_of(part * piece, piece), piece)
        value = lax.dot_general(eye, source[both, at, :], TURNED, preferred_element_type=jnp.float32)
        for n in range(2):
            turned[2 * both + n, b, :, at] = value[n * width : (n + 1) * width].astype(jnp.bfloat16)

        @pl.when(both == 0)
        def _():
            phi[b, :, at] = value[:width]

    for step in range(4):

        def two_layers(x, _):
            if step < 3:
                stencil(2 * x, step, sources[step % 2])
                stencil(2 * x + 1, step, sources[step % 2])
            if step > 0:
                turn(x, step - 1, sources[(step - 1) % 2])
            return 0

        lax.fori_loop(0, depth // 2, two_layers, 0)


def plane_slopes(where, blocks, offsets, rows, height, comps):
    layers, _, across, width = blocks[0].shape
    members = len(blocks)
    count = members * layers * height * across
    sizes = (layers, height, across, width, rows)
    vmem = pl.BlockSpec(memory_space=pltpu.VMEM)
    results = [
        ((4, comps, width, count), jnp.bfloat16),
        ((comps, width, count), jnp.float32),
    ]
    scratch = [
        ((members + 4,) + blocks[0].shape, jnp.float32),
        ((2, count, 2 * width), jnp.bfloat16),
        ((2, count, 2 * width), jnp.bfloat16),
    ]
    inputs = [(v.shape, v.dtype) for v in blocks]
    return pl.pallas_call(
        functools.partial(slopes_kernel, sizes, offsets),
        out_shape=[jax.ShapeDtypeStruct(*result) for result in results],
        in_specs=[pl.BlockSpec(memory_space=pltpu.SMEM)] + [vmem] * members,
        out_specs=[vmem] * len(results),
        scratch_shapes=[pltpu.VMEM(*shape) for shape in scratch],
        compiler_params=pltpu.CompilerParams(vmem_limit_bytes=grant(results + scratch + inputs)),
        cost_estimate=pl.CostEstimate(
            flops=2 * 12 * count * width * width, bytes_accessed=2**22, transcendentals=0
        ),
    )(where, *blocks)


def terms_kernel(share, chunk, rows, decks, where_ref, turned, phi, *refs):
    out_refs = [ref for ref in refs if len(ref.shape) == 2]
    own, *quads = refs[len(out_refs) :]
    outs = len(out_refs)
    width, count = turned.shape[2:]
    base = (member(where_ref, rows, (0, 0, 0)) * CHUNKS + chunk) * share
    first = where_ref[3] * (share // decks) if outs > 1 else 0
    together = min(4, share)
    for i in range(share):
        mode = base + lax.rem(i + first, share)
        for b in range(3):
            own[b, i] = jnp.broadcast_to(phi[b, pl.ds(mode, 1), :], (TILE, count))
    for group in range(share // together):
        modes = range(group * together, (group + 1) * together)
        quad = quads[group % len(quads)]
        for a in range(3):
            for start in range(0, count, LANES):
                lanes = slice(start, start + LANES)
                spread = [[own[b, mode, :, lanes] for b in range(3)] for mode in modes]
                for k in range(0, width, TILE):
                    slope = [
                        turned[1 + a, b, k : k + TILE, lanes].astype(jnp.float32) for b in range(3)
                    ]
                    for i, row in enumerate(spread):
                        value = row[0] * slope[0] + row[1] * slope[1] + row[2] * slope[2]
                        at = i * width + k
                        quad[a, at : at + TILE, lanes] = value.astype(jnp.bfloat16)
        total = sum(
            lax.dot_general(turned[0, a], quad[a], TURNED, preferred_element_type=jnp.float32)
            for a in range(3)
        )
        for i, mode in enumerate(modes):
            start = mode * width
            out_ref = out_refs[start * outs // (share * width)]
            start = start % (share * width // outs)
            out_ref[start : start + width, :] = total[:, i * width : (i + 1) * width].astype(
                out_ref.dtype
            )


def plane_terms(where, turned, phi, chunk, share, rows, decks, outs):
    width, count = turned.shape[2:]
    vmem = pl.BlockSpec(memory_space=pltpu.VMEM)
    dtypes = [jnp.float32 if outs > 1 and n == 0 else jnp.bfloat16 for n in range(outs)]
    results = [((share * width // outs, width), t) for t in dtypes]
    scratch = [((3, share, TILE, count), jnp.float32)]
    together = min(4, share)
    scratch += [((3, together * width, count), jnp.bfloat16)] * min(2, share // together)
    inputs = [(v.shape, v.dtype) for v in (turned, phi)]
    return pl.pallas_call(
        functools.partial(terms_kernel, share, chunk, rows, decks),
        out_shape=[jax.ShapeDtypeStruct(*result) for result in results],
        in_specs=[pl.BlockSpec(memory_space=pltpu.SMEM)] + [vmem] * 2,
        out_specs=[vmem] * outs,
        scratch_shapes=[pltpu.VMEM(*shape) for shape in scratch],
        compiler_params=pltpu.CompilerParams(vmem_limit_bytes=grant(results + scratch + inputs)),
        cost_estimate=pl.CostEstimate(
            flops=2 * share * width * width * count * 3, bytes_accessed=2**22, transcendentals=0
        ),
    )(where, turned, phi)


def place_kernel(plan, pieces, given, where_ref, *refs):
    rows, decks, line, runs = plan
    out_ref, wide, sems = refs[pieces + given :]
    step = math.gcd(line, LANES)
    copies = []
    for n, (piece, offsets, chunk, d, first) in enumerate(runs):
        done = n * line

        def widen(k, _):
            at = pl.multiple_of(k * step, step)
            wide[pl.ds(done + at, step), :] = refs[piece][pl.ds(first * line + at, step), :].astype(
                jnp.float32
            )
            return 0

        lax.fori_loop(0, line // step, widen, 0)
        start = (member(where_ref, rows, offsets) * CHUNKS + chunk) * decks * line
        start = start + lax.rem(where_ref[3] - d + decks, decks) * line
        to = pl.ds(pl.multiple_of(start, line), line)
        copies.append(
            pltpu.make_async_copy(wide.at[done : done + line], out_ref.at[to], sems.at[n])
        )
        copies[-1].start()
    for copy in copies:
        copy.wait()


def put(where, result, total_rows, rows, decks, chosen, line):
    values = [value for _, value in chosen]
    width = values[0].shape[1]
    runs = [
        (n, offsets, chunk, d, at)
        for n, (parts, _) in enumerate(chosen)
        for at, (chunk, offsets, d) in enumerate((c, o, d) for c, o, ds in parts for d in ds)
    ]
    given = [] if result is None else [result]
    vmem, anywhere = (pl.BlockSpec(memory_space=m) for m in (pltpu.VMEM, pl.ANY))
    wide = ((len(runs) * line, width), jnp.float32)
    return pl.pallas_call(
        functools.partial(place_kernel, (rows, decks, line, runs), len(values), len(given)),
        out_shape=jax.ShapeDtypeStruct((total_rows, width), jnp.float32),
        in_specs=[pl.BlockSpec(memory_space=pltpu.SMEM)]
        + [vmem] * len(values)
        + [anywhere] * len(given),
        out_specs=anywhere,
        scratch_shapes=[pltpu.VMEM(*wide), pltpu.SemaphoreType.DMA((len(runs),))],
        input_output_aliases={1 + len(values): 0} if given else {},
        compiler_params=pltpu.CompilerParams(
            vmem_limit_bytes=grant([wide] + [(v.shape, v.dtype) for v in values], 2**21)
        ),
        cost_estimate=pl.CostEstimate(
            flops=0, bytes_accessed=6 * wide[0][0] * width, transcendentals=0
        ),
    )(where, *values, *given)


def outer_rows(cells):
    across = cells.shape[3]
    decks = lax.axis_size("deck")
    ends = jnp.where(lax.axis_index("side") == 1, cells[..., across - 2 :, :], cells[..., :2, :])
    joints = [(2 * d + 1, 2 * d + 2) for d in range(decks - 1)]
    return lax.ppermute(ends, SPAN, joints + [(j, i) for i, j in joints])


def whole_piece(cells, outer, weight):
    layers, height, comps, across, width = cells.shape
    parts = []
    for _ in range(WEIGHT_PARTS):
        part = lax.reduce_precision(weight, 8, 7)
        weight = weight - part
        parts.append(part.astype(jnp.bfloat16))
    tile = jnp.concatenate(parts, axis=2)
    tile = jnp.pad(tile, ((0, 0), (0, 0), (0, width - tile.shape[2])))
    cells = cells.reshape(layers, height * comps, across, width)
    outer = outer.transpose(0, 1, 3, 2, 4).reshape(layers, 2 * height, comps, width)
    groups = pl.cdiv(2 * height, across)
    outer = jnp.pad(outer, ((0, 0), (0, groups * across - 2 * height), (0, 0), (0, 0)))
    outer = outer.reshape(layers, groups, across, comps, width).transpose(0, 1, 3, 2, 4)
    outer = outer.reshape(layers, groups * comps, across, width)
    return jnp.concatenate([cells, tile[:, None], outer], axis=1)


def spread_near(piece):
    rows = lax.axis_size("row")
    got = {(0, 0): piece, (0, 1): rotate(piece, "side")}
    for r in range(1, rows):
        got[(r, 0)] = rotate(piece, "row", r)
        pairs = [(2 * i + s, 2 * ((i + r) % rows) + 1 - s) for i in range(rows) for s in range(2)]
        got[(r, 1)] = lax.ppermute(piece, DIAGONAL, pairs)
    return got


def spread_cores(got):
    out = {}
    for (r, s), value in got.items():
        out[(r, 0, s)] = value
        out[(r, 1, s)] = rotate(value, "core")
    return out


def parts_over_decks(terms, decks):
    if len(terms) > 1:
        return [terms[0]] + [rotate(terms[r], "deck", r) for r in range(1, decks)]
    width = terms[0].shape[1]
    return list(lax.all_to_all(terms[0].reshape(decks, -1, width), "deck", 0, 0))


def shards(velocity_modes, cell_weight):
    width = velocity_modes.shape[-1]
    rows, decks = lax.axis_size("row"), lax.axis_size("deck")
    members = rows * 4
    share = width // members // CHUNKS
    where = jnp.stack([lax.axis_index(a) for a in ("row", "core", "side", "deck")]).astype(jnp.int32)
    outs = decks if share % (2 * decks) == 0 else 1

    cells = velocity_modes.transpose(0, 2, 3, 1, 4)
    blocks = spread_cores(spread_near(whole_piece(cells, outer_rows(cells), cell_weight)))
    offsets = list(blocks)
    height, comps = cells.shape[1:3]
    slopes = plane_slopes(where, list(blocks.values()), offsets, rows, height, comps)
    terms = [
        list(plane_terms(where, *slopes, n, share, rows, decks, outs)) for n in range(CHUNKS)
    ]

    line = share * width // decks
    every = range(decks)
    half = decks // 2

    def put_all(result, chosen):
        return put(where, result, width * width, rows, decks, chosen, line)

    pieces = []
    for n in range(CHUNKS):
        parts = parts_over_decks(terms[n], decks)
        if n < CHUNKS - 1:
            parts, terms[n + 1][0] = lax.optimization_barrier((parts, terms[n + 1][0]))
        mine = sum(part.astype(jnp.float32) for part in parts).astype(jnp.bfloat16)
        if n < CHUNKS - 1:
            mine, later = lax.optimization_barrier((mine, terms[n + 1]))
            terms[n + 1] = list(later)
        pieces.append(
            jnp.concatenate([mine] + [rotate(mine, "deck", r) for r in range(1, decks)], axis=0)
        )

    def to_core(groups):
        chosen = sum(groups, [])
        joined = rotate(jnp.concatenate([v for _, _, v in chosen], axis=0), "core")
        runs = [(n, (r, 1, s), ds) for n, ps, _ in chosen for (r, _, s), ds in ps]
        return [(runs, joined)]

    def flat(*groups):
        return [([(n, o, ds) for o, ds in ps], v) for g in groups for n, ps, v in g]

    result = None
    held, core = [], []
    for n, piece in enumerate(pieces):
        across = rotate(piece, "side")
        along = [rotate(piece, "row", r) for r in range(1, rows)]
        near = [(n, [((0, 0, 0), every)], piece), (n, [((0, 0, 1), every)], across)]
        near += [(n, [((r, 0, 0), every)], v) for r, v in enumerate(along, 1)]
        halves = [across[: half * line]] + [v[half * line :] for v in along]
        if n > 0:
            result = put_all(result, flat(held[0]) + core)
        far = [
            (n, [((r, 0, 1), every[:half])], rotate(halves[0], "row", r)) for r in range(1, rows)
        ]
        far += [
            (n, [((r, 0, 1), every[half:])], rotate(halves[r], "side")) for r in range(1, rows)
        ]
        if n < CHUNKS - 1:
            core = to_core([near])
            held = [near, far]
        else:
            core = to_core([held[1], near])
            result = put_all(result, flat(held[1], near))
            values, result = lax.optimization_barrier(([v for _, _, v in far], result))
            far = [(n, ps, v) for (_, ps, _), v in zip(far, values)]
            last = to_core([far])
            result = put_all(result, core + flat(far))
            result = put_all(result, last)
    return result.reshape(width, width, width)


def solution(mesh):
    streams, spans = (mesh.shape[name] for name in ("stream", "span"))
    split = Mesh(mesh.devices.reshape(streams // 2, 2, spans // 2, 2), STREAM + SPAN)
    placed = (P(STREAM, SPAN, None, None, None), P(STREAM, SPAN, None))
    return jax.shard_map(shards, mesh=split, in_specs=placed, out_specs=P(), check_vma=False)
```

```python
import functools
import math

import jax
import jax.numpy as jnp
from jax import lax
from jax.experimental import pallas as pl
from jax.experimental.pallas import tpu as pltpu
from jax.sharding import Mesh, PartitionSpec as P

STREAM = ("row", "core")
SPAN = ("deck", "side")
DIAGONAL = ("row", "side")
WEIGHT_PARTS = 3
LANES = 128
TILE = 16
CHUNKS = 2
TURNED = (((1,), (1,)), ((), ()))


def rotate(value, axis, by=1):
    count = lax.axis_size(axis)
    return lax.ppermute(value, axis, [(i, (i + by) % count) for i in range(count)])


def member(where, rows, offsets):
    r, c, s = offsets
    row = lax.rem(where[0] - r + rows, rows)
    return (row * 2 + lax.rem(where[1] + c, 2)) * 2 + lax.rem(where[2] + s, 2)


def grant(shapes, slack=6 * 2**20):
    total = slack
    for shape, dtype in shapes:
        *outer, rows, columns = shape
        size = jnp.dtype(dtype).itemsize
        rows, columns = pl.cdiv(rows, TILE) * TILE, pl.cdiv(columns, LANES) * LANES
        total += math.prod(outer) * rows * columns * size
    return total


def slopes_kernel(sizes, offsets, where_ref, *refs):
    layers, height, across, width, rows = sizes
    members = len(offsets)
    blocks = refs[:members]
    turned, phi, field, *sources = refs[members:]
    count = members * layers * height * across
    depth = members // 2 * layers
    piece = 4 * count // depth
    parts = count // piece

    field[:2] = jnp.zeros_like(field[:2])
    field[members + 2 :] = jnp.zeros_like(field[members + 2 :])
    for n in range(members):
        field[member(where_ref, rows, offsets[n]) + 2] = blocks[n][...].astype(jnp.float32)
    index = lax.broadcasted_iota(jnp.int32, (across, width), 0)
    row, column = (lax.broadcasted_iota(jnp.int32, (2 * width, 2 * width), d) for d in range(2))
    eye = (row == column).astype(jnp.bfloat16)

    def stencil(x, b, source):
        def layer_at(step, side):
            at = x + step + layers
            return lax.div(at, layers) * 2 + side, lax.rem(at, layers)

        for side in range(2):
            here_at, layer = layer_at(0, side)
            at = here_at - 2
            tile = field[here_at, layer, 3 * height]
            weights = tile
            for part in range(1, WEIGHT_PARTS):
                weights = weights + pltpu.roll(tile, width - part * height, 1)
            beside = {step: layer_at(step, side) for step in (-2, -1, 1, 2)}
            found = []
            for z in range(height):
                weight = jnp.broadcast_to(weights[:, z : z + 1], (across, width))
                twelfth, half = weight * (1.0 / 12.0), weight * 0.5
                base = 2 * z // across * across
                here = field[here_at, layer, 3 * z + b]
                along = {step: field[m, l, 3 * z + b] for step, (m, l) in beside.items()}
                value_x = 8.0 * (along[1] - along[-1]) - (along[2] - along[-2])

                outer = field[here_at, layer, 3 * height + 1 + base // across * 3 + b]
                beyond = field[here_at + 1 - 2 * side, layer, 3 * z + b]
                if side == 0:
                    prev = pltpu.roll(outer, (across - 2 - (2 * z - base)) % across, 0)
                    after = beyond
                else:
                    prev = beyond
                    after = pltpu.roll(outer, (across - (2 * z - base)) % across, 0)
                near = pltpu.roll(jnp.where(index < 1, after, here), across - 1, 0)
                near = near - pltpu.roll(jnp.where(index >= across - 1, prev, here), 1, 0)
                far = pltpu.roll(jnp.where(index < 2, after, here), across - 2, 0)
                far = far - pltpu.roll(jnp.where(index >= across - 2, prev, here), 2, 0)
                value_y = 8.0 * near - far

                value_z = jnp.zeros_like(here)
                if z < height - 1:
                    value_z = field[here_at, layer, 3 * (z + 1) + b]
                if z > 0:
                    value_z = value_z - field[here_at, layer, 3 * (z - 1) + b]
                found.append((here, value_x * twelfth, value_y * twelfth, value_z * half))
                if len(found) * across == TILE:
                    start = ((at * layers + layer) * height + z + 1) * across - TILE
                    to = pl.ds(pl.multiple_of(start, TILE), TILE)
                    for q in range(4):
                        value = jnp.concatenate([f[q] for f in found], axis=0)
                        columns = slice(q % 2 * width, (q % 2 + 1) * width)
                        source[q // 2, to, columns] = value.astype(jnp.bfloat16)
                    found = []

    def turn(x, b, source):
        both, part = lax.div(x, parts), lax.rem(x, parts)
        at = pl.ds(pl.multiple_of(part * piece, piece), piece)
        value = lax.dot_general(eye, source[both, at, :], TURNED, preferred_element_type=jnp.float32)
        for n in range(2):
            turned[2 * both + n, b, :, at] = value[n * width : (n + 1) * width].astype(jnp.bfloat16)

        @pl.when(both == 0)
        def _():
            phi[b, :, at] = value[:width]

    for step in range(4):

        def two_layers(x, _):
            if step < 3:
                stencil(2 * x, step, sources[step % 2])
                stencil(2 * x + 1, step, sources[step % 2])
            if step > 0:
                turn(x, step - 1, sources[(step - 1) % 2])
            return 0

        lax.fori_loop(0, depth // 2, two_layers, 0)


def plane_slopes(where, blocks, offsets, rows, height, comps):
    layers, _, across, width = blocks[0].shape
    members = len(blocks)
    count = members * layers * height * across
    sizes = (layers, height, across, width, rows)
    vmem = pl.BlockSpec(memory_space=pltpu.VMEM)
    results = [
        ((4, comps, width, count), jnp.bfloat16),
        ((comps, width, count), jnp.float32),
    ]
    scratch = [
        ((members + 4,) + blocks[0].shape, jnp.float32),
        ((2, count, 2 * width), jnp.bfloat16),
        ((2, count, 2 * width), jnp.bfloat16),
    ]
    inputs = [(v.shape, v.dtype) for v in blocks]
    return pl.pallas_call(
        functools.partial(slopes_kernel, sizes, offsets),
        out_shape=[jax.ShapeDtypeStruct(*result) for result in results],
        in_specs=[pl.BlockSpec(memory_space=pltpu.SMEM)] + [vmem] * members,
        out_specs=[vmem] * len(results),
        scratch_shapes=[pltpu.VMEM(*shape) for shape in scratch],
        compiler_params=pltpu.CompilerParams(vmem_limit_bytes=grant(results + scratch + inputs)),
        cost_estimate=pl.CostEstimate(
            flops=2 * 12 * count * width * width, bytes_accessed=2**22, transcendentals=0
        ),
    )(where, *blocks)


def terms_kernel(share, chunk, rows, decks, where_ref, turned, phi, *refs):
    out_refs = [ref for ref in refs if len(ref.shape) == 2]
    own, *quads = refs[len(out_refs) :]
    outs = len(out_refs)
    width, count = turned.shape[2:]
    base = (member(where_ref, rows, (0, 0, 0)) * CHUNKS + chunk) * share
    first = where_ref[3] * (share // decks) if outs > 1 else 0
    together = min(4, share)
    for i in range(share):
        mode = base + lax.rem(i + first, share)
        for b in range(3):
            own[b, i] = jnp.broadcast_to(phi[b, pl.ds(mode, 1), :], (TILE, count))
    for group in range(share // together):
        modes = range(group * together, (group + 1) * together)
        quad = quads[group % len(quads)]
        for a in range(3):
            for start in range(0, count, LANES):
                lanes = slice(start, start + LANES)
                spread = [[own[b, mode, :, lanes] for b in range(3)] for mode in modes]
                for k in range(0, width, TILE):
                    slope = [
                        turned[1 + a, b, k : k + TILE, lanes].astype(jnp.float32) for b in range(3)
                    ]
                    for i, row in enumerate(spread):
                        value = row[0] * slope[0] + row[1] * slope[1] + row[2] * slope[2]
                        at = i * width + k
                        quad[a, at : at + TILE, lanes] = value.astype(jnp.bfloat16)
        total = sum(
            lax.dot_general(turned[0, a], quad[a], TURNED, preferred_element_type=jnp.float32)
            for a in range(3)
        )
        for i, mode in enumerate(modes):
            start = mode * width
            out_ref = out_refs[start * outs // (share * width)]
            start = start % (share * width // outs)
            out_ref[start : start + width, :] = total[:, i * width : (i + 1) * width].astype(
                out_ref.dtype
            )


def plane_terms(where, turned, phi, chunk, share, rows, decks, outs):
    width, count = turned.shape[2:]
    vmem = pl.BlockSpec(memory_space=pltpu.VMEM)
    dtypes = [jnp.float32 if outs > 1 and n == 0 else jnp.bfloat16 for n in range(outs)]
    results = [((share * width // outs, width), t) for t in dtypes]
    scratch = [((3, share, TILE, count), jnp.float32)]
    together = min(4, share)
    scratch += [((3, together * width, count), jnp.bfloat16)] * min(2, share // together)
    inputs = [(v.shape, v.dtype) for v in (turned, phi)]
    return pl.pallas_call(
        functools.partial(terms_kernel, share, chunk, rows, decks),
        out_shape=[jax.ShapeDtypeStruct(*result) for result in results],
        in_specs=[pl.BlockSpec(memory_space=pltpu.SMEM)] + [vmem] * 2,
        out_specs=[vmem] * outs,
        scratch_shapes=[pltpu.VMEM(*shape) for shape in scratch],
        compiler_params=pltpu.CompilerParams(vmem_limit_bytes=grant(results + scratch + inputs)),
        cost_estimate=pl.CostEstimate(
            flops=2 * share * width * width * count * 3, bytes_accessed=2**22, transcendentals=0
        ),
    )(where, turned, phi)


def place_kernel(plan, pieces, given, where_ref, *refs):
    rows, decks, line, runs = plan
    out_ref, wide, sems = refs[pieces + given :]
    step = math.gcd(line, LANES)
    copies = []
    for n, (piece, offsets, chunk, d, first) in enumerate(runs):
        done = n * line

        def widen(k, _):
            at = pl.multiple_of(k * step, step)
            wide[pl.ds(done + at, step), :] = refs[piece][pl.ds(first * line + at, step), :].astype(
                jnp.float32
            )
            return 0

        lax.fori_loop(0, line // step, widen, 0)
        start = (member(where_ref, rows, offsets) * CHUNKS + chunk) * decks * line
        start = start + lax.rem(where_ref[3] - d + decks, decks) * line
        to = pl.ds(pl.multiple_of(start, line), line)
        copies.append(
            pltpu.make_async_copy(wide.at[done : done + line], out_ref.at[to], sems.at[n])
        )
        copies[-1].start()
    for copy in copies:
        copy.wait()


def put(where, result, total_rows, rows, decks, chosen, line):
    values = [value for _, _, value in chosen]
    width = values[0].shape[1]
    runs = [
        (n, offsets, chunk, d, at)
        for n, (chunk, parts, _) in enumerate(chosen)
        for at, (offsets, d) in enumerate((o, d) for o, ds in parts for d in ds)
    ]
    given = [] if result is None else [result]
    vmem, anywhere = (pl.BlockSpec(memory_space=m) for m in (pltpu.VMEM, pl.ANY))
    wide = ((len(runs) * line, width), jnp.float32)
    return pl.pallas_call(
        functools.partial(place_kernel, (rows, decks, line, runs), len(values), len(given)),
        out_shape=jax.ShapeDtypeStruct((total_rows, width), jnp.float32),
        in_specs=[pl.BlockSpec(memory_space=pltpu.SMEM)]
        + [vmem] * len(values)
        + [anywhere] * len(given),
        out_specs=anywhere,
        scratch_shapes=[pltpu.VMEM(*wide), pltpu.SemaphoreType.DMA((len(runs),))],
        input_output_aliases={1 + len(values): 0} if given else {},
        compiler_params=pltpu.CompilerParams(
            vmem_limit_bytes=grant([wide] + [(v.shape, v.dtype) for v in values], 2**21)
        ),
        cost_estimate=pl.CostEstimate(
            flops=0, bytes_accessed=6 * wide[0][0] * width, transcendentals=0
        ),
    )(where, *values, *given)


def outer_rows(cells):
    across = cells.shape[3]
    decks = lax.axis_size("deck")
    ends = jnp.where(lax.axis_index("side") == 1, cells[..., across - 2 :, :], cells[..., :2, :])
    joints = [(2 * d + 1, 2 * d + 2) for d in range(decks - 1)]
    return lax.ppermute(ends, SPAN, joints + [(j, i) for i, j in joints])


def whole_piece(cells, outer, weight):
    layers, height, comps, across, width = cells.shape
    parts = []
    for _ in range(WEIGHT_PARTS):
        part = lax.reduce_precision(weight, 8, 7)
        weight = weight - part
        parts.append(part.astype(jnp.bfloat16))
    tile = jnp.concatenate(parts, axis=2)
    tile = jnp.pad(tile, ((0, 0), (0, 0), (0, width - tile.shape[2])))
    cells = cells.reshape(layers, height * comps, across, width)
    outer = outer.transpose(0, 1, 3, 2, 4).reshape(layers, 2 * height, comps, width)
    groups = pl.cdiv(2 * height, across)
    outer = jnp.pad(outer, ((0, 0), (0, groups * across - 2 * height), (0, 0), (0, 0)))
    outer = outer.reshape(layers, groups, across, comps, width).transpose(0, 1, 3, 2, 4)
    outer = outer.reshape(layers, groups * comps, across, width)
    return jnp.concatenate([cells, tile[:, None], outer], axis=1)


def spread_near(piece):
    rows = lax.axis_size("row")
    got = {(0, 0): piece, (0, 1): rotate(piece, "side")}
    for r in range(1, rows):
        got[(r, 0)] = rotate(piece, "row", r)
        pairs = [(2 * i + s, 2 * ((i + r) % rows) + 1 - s) for i in range(rows) for s in range(2)]
        got[(r, 1)] = lax.ppermute(piece, DIAGONAL, pairs)
    return got


def spread_cores(got):
    out = {}
    for (r, s), value in got.items():
        out[(r, 0, s)] = value
        out[(r, 1, s)] = rotate(value, "core")
    return out


def parts_over_decks(terms, decks):
    if len(terms) > 1:
        return [terms[0]] + [rotate(terms[r], "deck", r) for r in range(1, decks)]
    width = terms[0].shape[1]
    return list(lax.all_to_all(terms[0].reshape(decks, -1, width), "deck", 0, 0))


def shards(velocity_modes, cell_weight):
    width = velocity_modes.shape[-1]
    rows, decks = lax.axis_size("row"), lax.axis_size("deck")
    members = rows * 4
    share = width // members // CHUNKS
    where = jnp.stack([lax.axis_index(a) for a in ("row", "core", "side", "deck")]).astype(jnp.int32)
    outs = decks if share % (2 * decks) == 0 else 1

    cells = velocity_modes.transpose(0, 2, 3, 1, 4)
    blocks = spread_cores(spread_near(whole_piece(cells, outer_rows(cells), cell_weight)))
    offsets = list(blocks)
    height, comps = cells.shape[1:3]
    slopes = plane_slopes(where, list(blocks.values()), offsets, rows, height, comps)
    terms = [
        list(plane_terms(where, *slopes, n, share, rows, decks, outs)) for n in range(CHUNKS)
    ]

    line = share * width // decks
    every = range(decks)
    half = decks // 2

    def put_all(result, chosen):
        return put(where, result, width * width, rows, decks, chosen, line)

    pieces = []
    for n in range(CHUNKS):
        parts = parts_over_decks(terms[n], decks)
        if n < CHUNKS - 1:
            parts, terms[n + 1][0] = lax.optimization_barrier((parts, terms[n + 1][0]))
        mine = sum(part.astype(jnp.float32) for part in parts).astype(jnp.bfloat16)
        if n < CHUNKS - 1:
            mine, later = lax.optimization_barrier((mine, terms[n + 1]))
            terms[n + 1] = list(later)
        pieces.append(
            jnp.concatenate([mine] + [rotate(mine, "deck", r) for r in range(1, decks)], axis=0)
        )

    def join(chosen):
        return chosen[0][0], sum((ps for _, ps, _ in chosen), []), jnp.concatenate(
            [v for _, _, v in chosen], axis=0
        )

    def to_core(n, parts, value):
        return n, [((r, 1, s), ds) for (r, _, s), ds in parts], rotate(value, "core")

    result = None
    waiting = []
    for n, piece in enumerate(pieces):
        across = rotate(piece, "side")
        along = [rotate(piece, "row", r) for r in range(1, rows)]
        near = [(n, [((0, 0, 0), every)], piece), (n, [((0, 0, 1), every)], across)]
        near += [(n, [((r, 0, 0), every)], v) for r, v in enumerate(along, 1)]
        halves = [across[: half * line]] + [v[half * line :] for v in along]
        if n > 0:
            result = put_all(result, waiting)
            halves, result = lax.optimization_barrier((halves, result))
        far = [
            (n, [((r, 0, 1), every[:half])], rotate(halves[0], "row", r)) for r in range(1, rows)
        ]
        far += [
            (n, [((r, 0, 1), every[half:])], rotate(halves[r], "side")) for r in range(1, rows)
        ]
        if n < CHUNKS - 1:
            waiting = near
            held = [(far, join(near + far))]
        else:
            first, second = join(near), []
            for values, (m, parts, joined) in held:
                joined, halves = lax.optimization_barrier((joined, halves))
                second += values + [to_core(m, parts, joined)]
            core = to_core(*first)
            result = put_all(result, second + near)
            last, result = lax.optimization_barrier(([v for _, _, v in far], result))
            far = [(n, ps, v) for (_, ps, _), v in zip(far, last)]
            result = put_all(result, [core] + far)
            result = put_all(result, [to_core(*join(far))])
    return result.reshape(width, width, width)


def solution(mesh):
    streams, spans = (mesh.shape[name] for name in ("stream", "span"))
    split = Mesh(mesh.devices.reshape(streams // 2, 2, spans // 2, 2), STREAM + SPAN)
    placed = (P(STREAM, SPAN, None, None, None), P(STREAM, SPAN, None))
    return jax.shard_map(shards, mesh=split, in_specs=placed, out_specs=P(), check_vma=False)
```

```python
import functools
import math

import jax
import jax.numpy as jnp
from jax import lax
from jax.experimental import pallas as pl
from jax.experimental.pallas import tpu as pltpu
from jax.sharding import Mesh, PartitionSpec as P

STREAM = ("row", "core")
SPAN = ("deck", "side")
DIAGONAL = ("row", "side")
WEIGHT_PARTS = 3
LANES = 128
TILE = 16
CHUNKS = 2
TURNED = (((1,), (1,)), ((), ()))


def rotate(value, axis, by=1):
    count = lax.axis_size(axis)
    return lax.ppermute(value, axis, [(i, (i + by) % count) for i in range(count)])


def swap(value, by):
    count = lax.axis_size("deck")
    assert count & (count - 1) == 0
    return lax.ppermute(value, "deck", [(i, i ^ by) for i in range(count)])


def member(where, rows, offsets):
    r, c, s = offsets
    row = lax.rem(where[0] - r + rows, rows)
    return (row * 2 + lax.rem(where[1] + c, 2)) * 2 + lax.rem(where[2] + s, 2)


def grant(shapes, slack=6 * 2**20):
    total = slack
    for shape, dtype in shapes:
        *outer, rows, columns = shape
        size = jnp.dtype(dtype).itemsize
        rows, columns = pl.cdiv(rows, TILE) * TILE, pl.cdiv(columns, LANES) * LANES
        total += math.prod(outer) * rows * columns * size
    return total


def slopes_kernel(sizes, offsets, where_ref, *refs):
    layers, height, across, width, rows = sizes
    members = len(offsets)
    blocks = refs[:members]
    turned, phi, field, *sources = refs[members:]
    count = members * layers * height * across
    depth = members // 2 * layers
    piece = 4 * count // depth
    parts = count // piece

    field[:2] = jnp.zeros_like(field[:2])
    field[members + 2 :] = jnp.zeros_like(field[members + 2 :])
    for n in range(members):
        field[member(where_ref, rows, offsets[n]) + 2] = blocks[n][...].astype(jnp.float32)
    index = lax.broadcasted_iota(jnp.int32, (across, width), 0)
    row, column = (lax.broadcasted_iota(jnp.int32, (2 * width, 2 * width), d) for d in range(2))
    eye = (row == column).astype(jnp.bfloat16)

    def stencil(x, b, source):
        def layer_at(step, side):
            at = x + step + layers
            return lax.div(at, layers) * 2 + side, lax.rem(at, layers)

        for side in range(2):
            here_at, layer = layer_at(0, side)
            at = here_at - 2
            tile = field[here_at, layer, 3 * height]
            weights = tile
            for part in range(1, WEIGHT_PARTS):
                weights = weights + pltpu.roll(tile, width - part * height, 1)
            beside = {step: layer_at(step, side) for step in (-2, -1, 1, 2)}
            found = []
            for z in range(height):
                weight = jnp.broadcast_to(weights[:, z : z + 1], (across, width))
                twelfth, half = weight * (1.0 / 12.0), weight * 0.5
                base = 2 * z // across * across
                here = field[here_at, layer, 3 * z + b]
                along = {step: field[m, l, 3 * z + b] for step, (m, l) in beside.items()}
                value_x = 8.0 * (along[1] - along[-1]) - (along[2] - along[-2])

                outer = field[here_at, layer, 3 * height + 1 + base // across * 3 + b]
                beyond = field[here_at + 1 - 2 * side, layer, 3 * z + b]
                if side == 0:
                    prev = pltpu.roll(outer, (across - 2 - (2 * z - base)) % across, 0)
                    after = beyond
                else:
                    prev = beyond
                    after = pltpu.roll(outer, (across - (2 * z - base)) % across, 0)
                near = pltpu.roll(jnp.where(index < 1, after, here), across - 1, 0)
                near = near - pltpu.roll(jnp.where(index >= across - 1, prev, here), 1, 0)
                far = pltpu.roll(jnp.where(index < 2, after, here), across - 2, 0)
                far = far - pltpu.roll(jnp.where(index >= across - 2, prev, here), 2, 0)
                value_y = 8.0 * near - far

                value_z = jnp.zeros_like(here)
                if z < height - 1:
                    value_z = field[here_at, layer, 3 * (z + 1) + b]
                if z > 0:
                    value_z = value_z - field[here_at, layer, 3 * (z - 1) + b]
                found.append((here, value_x * twelfth, value_y * twelfth, value_z * half))
                if len(found) * across == TILE:
                    start = ((at * layers + layer) * height + z + 1) * across - TILE
                    to = pl.ds(pl.multiple_of(start, TILE), TILE)
                    for q in range(4):
                        value = jnp.concatenate([f[q] for f in found], axis=0)
                        columns = slice(q % 2 * width, (q % 2 + 1) * width)
                        source[q // 2, to, columns] = value.astype(jnp.bfloat16)
                    found = []

    def turn(x, b, source):
        both, part = lax.div(x, parts), lax.rem(x, parts)
        at = pl.ds(pl.multiple_of(part * piece, piece), piece)
        value = lax.dot_general(eye, source[both, at, :], TURNED, preferred_element_type=jnp.float32)
        for n in range(2):
            turned[2 * both + n, b, :, at] = value[n * width : (n + 1) * width].astype(jnp.bfloat16)

        @pl.when(both == 0)
        def _():
            phi[b, :, at] = value[:width]

    for step in range(4):

        def two_layers(x, _):
            if step < 3:
                stencil(2 * x, step, sources[step % 2])
                stencil(2 * x + 1, step, sources[step % 2])
            if step > 0:
                turn(x, step - 1, sources[(step - 1) % 2])
            return 0

        lax.fori_loop(0, depth // 2, two_layers, 0)


def plane_slopes(where, blocks, offsets, rows, height, comps):
    layers, _, across, width = blocks[0].shape
    members = len(blocks)
    count = members * layers * height * across
    sizes = (layers, height, across, width, rows)
    vmem = pl.BlockSpec(memory_space=pltpu.VMEM)
    results = [
        ((4, comps, width, count), jnp.bfloat16),
        ((comps, width, count), jnp.float32),
    ]
    scratch = [
        ((members + 4,) + blocks[0].shape, jnp.float32),
        ((2, count, 2 * width), jnp.bfloat16),
        ((2, count, 2 * width), jnp.bfloat16),
    ]
    inputs = [(v.shape, v.dtype) for v in blocks]
    return pl.pallas_call(
        functools.partial(slopes_kernel, sizes, offsets),
        out_shape=[jax.ShapeDtypeStruct(*result) for result in results],
        in_specs=[pl.BlockSpec(memory_space=pltpu.SMEM)] + [vmem] * members,
        out_specs=[vmem] * len(results),
        scratch_shapes=[pltpu.VMEM(*shape) for shape in scratch],
        compiler_params=pltpu.CompilerParams(vmem_limit_bytes=grant(results + scratch + inputs)),
        cost_estimate=pl.CostEstimate(
            flops=2 * 12 * count * width * width, bytes_accessed=2**22, transcendentals=0
        ),
    )(where, *blocks)


def terms_kernel(share, chunk, rows, decks, where_ref, turned, phi, *refs):
    out_refs = [ref for ref in refs if len(ref.shape) == 2]
    own, *quads = refs[len(out_refs) :]
    outs = len(out_refs)
    width, count = turned.shape[2:]
    base = (member(where_ref, rows, (0, 0, 0)) * CHUNKS + chunk) * share
    each = share // decks if outs > 1 else share
    together = min(4, share)
    for i in range(share):
        mode = base + i
        if outs > 1:
            mode = base + lax.bitwise_xor(where_ref[3], i // each) * each + i % each
        for b in range(3):
            own[b, i] = jnp.broadcast_to(phi[b, pl.ds(mode, 1), :], (TILE, count))
    for group in range(share // together):
        modes = range(group * together, (group + 1) * together)
        quad = quads[group % len(quads)]
        for a in range(3):
            for start in range(0, count, LANES):
                lanes = slice(start, start + LANES)
                spread = [[own[b, mode, :, lanes] for b in range(3)] for mode in modes]
                for k in range(0, width, TILE):
                    slope = [
                        turned[1 + a, b, k : k + TILE, lanes].astype(jnp.float32) for b in range(3)
                    ]
                    for i, row in enumerate(spread):
                        value = row[0] * slope[0] + row[1] * slope[1] + row[2] * slope[2]
                        at = i * width + k
                        quad[a, at : at + TILE, lanes] = value.astype(jnp.bfloat16)
        total = sum(
            lax.dot_general(turned[0, a], quad[a], TURNED, preferred_element_type=jnp.float32)
            for a in range(3)
        )
        for i, mode in enumerate(modes):
            start = mode * width
            out_ref = out_refs[start * outs // (share * width)]
            start = start % (share * width // outs)
            out_ref[start : start + width, :] = total[:, i * width : (i + 1) * width].astype(
                out_ref.dtype
            )


def plane_terms(where, turned, phi, chunk, share, rows, decks, outs):
    width, count = turned.shape[2:]
    vmem = pl.BlockSpec(memory_space=pltpu.VMEM)
    dtypes = [jnp.float32 if outs > 1 and n == 0 else jnp.bfloat16 for n in range(outs)]
    results = [((share * width // outs, width), t) for t in dtypes]
    scratch = [((3, share, TILE, count), jnp.float32)]
    together = min(4, share)
    scratch += [((3, together * width, count), jnp.bfloat16)] * min(2, share // together)
    inputs = [(v.shape, v.dtype) for v in (turned, phi)]
    return pl.pallas_call(
        functools.partial(terms_kernel, share, chunk, rows, decks),
        out_shape=[jax.ShapeDtypeStruct(*result) for result in results],
        in_specs=[pl.BlockSpec(memory_space=pltpu.SMEM)] + [vmem] * 2,
        out_specs=[vmem] * outs,
        scratch_shapes=[pltpu.VMEM(*shape) for shape in scratch],
        compiler_params=pltpu.CompilerParams(vmem_limit_bytes=grant(results + scratch + inputs)),
        cost_estimate=pl.CostEstimate(
            flops=2 * share * width * width * count * 3, bytes_accessed=2**22, transcendentals=0
        ),
    )(where, turned, phi)


def place_kernel(plan, pieces, given, where_ref, *refs):
    rows, decks, line, runs = plan
    out_ref, wide, sems = refs[pieces + given :]
    step = math.gcd(line, LANES)
    copies = []
    for n, (piece, offsets, chunk, d, first) in enumerate(runs):
        done = n * line

        def widen(k, _):
            at = pl.multiple_of(k * step, step)
            wide[pl.ds(done + at, step), :] = refs[piece][pl.ds(first * line + at, step), :].astype(
                jnp.float32
            )
            return 0

        lax.fori_loop(0, line // step, widen, 0)
        start = (member(where_ref, rows, offsets) * CHUNKS + chunk) * decks * line
        start = start + lax.bitwise_xor(where_ref[3], d) * line
        to = pl.ds(pl.multiple_of(start, line), line)
        copies.append(
            pltpu.make_async_copy(wide.at[done : done + line], out_ref.at[to], sems.at[n])
        )
        copies[-1].start()
    for copy in copies:
        copy.wait()


def put(where, result, total_rows, rows, decks, chosen, line):
    values = [value for _, _, value in chosen]
    width = values[0].shape[1]
    runs = [
        (n, offsets, chunk, d, at)
        for n, (chunk, parts, _) in enumerate(chosen)
        for at, (offsets, d) in enumerate((o, d) for o, ds in parts for d in ds)
    ]
    given = [] if result is None else [result]
    vmem, anywhere = (pl.BlockSpec(memory_space=m) for m in (pltpu.VMEM, pl.ANY))
    wide = ((len(runs) * line, width), jnp.float32)
    return pl.pallas_call(
        functools.partial(place_kernel, (rows, decks, line, runs), len(values), len(given)),
        out_shape=jax.ShapeDtypeStruct((total_rows, width), jnp.float32),
        in_specs=[pl.BlockSpec(memory_space=pltpu.SMEM)]
        + [vmem] * len(values)
        + [anywhere] * len(given),
        out_specs=anywhere,
        scratch_shapes=[pltpu.VMEM(*wide), pltpu.SemaphoreType.DMA((len(runs),))],
        input_output_aliases={1 + len(values): 0} if given else {},
        compiler_params=pltpu.CompilerParams(
            vmem_limit_bytes=grant([wide] + [(v.shape, v.dtype) for v in values], 2**21)
        ),
        cost_estimate=pl.CostEstimate(
            flops=0, bytes_accessed=6 * wide[0][0] * width, transcendentals=0
        ),
    )(where, *values, *given)


def outer_rows(cells):
    across = cells.shape[3]
    decks = lax.axis_size("deck")
    ends = jnp.where(lax.axis_index("side") == 1, cells[..., across - 2 :, :], cells[..., :2, :])
    joints = [(2 * d + 1, 2 * d + 2) for d in range(decks - 1)]
    return lax.ppermute(ends, SPAN, joints + [(j, i) for i, j in joints])


def whole_piece(cells, outer, weight):
    layers, height, comps, across, width = cells.shape
    parts = []
    for _ in range(WEIGHT_PARTS):
        part = lax.reduce_precision(weight, 8, 7)
        weight = weight - part
        parts.append(part.astype(jnp.bfloat16))
    tile = jnp.concatenate(parts, axis=2)
    tile = jnp.pad(tile, ((0, 0), (0, 0), (0, width - tile.shape[2])))
    cells = cells.reshape(layers, height * comps, across, width)
    outer = outer.transpose(0, 1, 3, 2, 4).reshape(layers, 2 * height, comps, width)
    groups = pl.cdiv(2 * height, across)
    outer = jnp.pad(outer, ((0, 0), (0, groups * across - 2 * height), (0, 0), (0, 0)))
    outer = outer.reshape(layers, groups, across, comps, width).transpose(0, 1, 3, 2, 4)
    outer = outer.reshape(layers, groups * comps, across, width)
    return jnp.concatenate([cells, tile[:, None], outer], axis=1)


def spread_near(piece):
    rows = lax.axis_size("row")
    got = {(0, 0): piece, (0, 1): rotate(piece, "side")}
    for r in range(1, rows):
        got[(r, 0)] = rotate(piece, "row", r)
        pairs = [(2 * i + s, 2 * ((i + r) % rows) + 1 - s) for i in range(rows) for s in range(2)]
        got[(r, 1)] = lax.ppermute(piece, DIAGONAL, pairs)
    return got


def spread_cores(got):
    out = {}
    for (r, s), value in got.items():
        out[(r, 0, s)] = value
        out[(r, 1, s)] = rotate(value, "core")
    return out


def parts_over_decks(terms, decks):
    if len(terms) > 1:
        return [terms[0]] + [swap(terms[r], r) for r in range(1, decks)]
    width = terms[0].shape[1]
    return list(lax.all_to_all(terms[0].reshape(decks, -1, width), "deck", 0, 0))


def shards(velocity_modes, cell_weight):
    width = velocity_modes.shape[-1]
    rows, decks = lax.axis_size("row"), lax.axis_size("deck")
    members = rows * 4
    share = width // members // CHUNKS
    where = jnp.stack([lax.axis_index(a) for a in ("row", "core", "side", "deck")]).astype(jnp.int32)
    outs = decks if share % (2 * decks) == 0 else 1

    cells = velocity_modes.transpose(0, 2, 3, 1, 4)
    blocks = spread_cores(spread_near(whole_piece(cells, outer_rows(cells), cell_weight)))
    offsets = list(blocks)
    height, comps = cells.shape[1:3]
    slopes = plane_slopes(where, list(blocks.values()), offsets, rows, height, comps)
    terms = [
        list(plane_terms(where, *slopes, n, share, rows, decks, outs)) for n in range(CHUNKS)
    ]

    line = share * width // decks
    every = range(decks)
    half = decks // 2

    def put_all(result, chosen):
        return put(where, result, width * width, rows, decks, chosen, line)

    pieces = []
    for n in range(CHUNKS):
        parts = parts_over_decks(terms[n], decks)
        if n < CHUNKS - 1:
            parts, terms[n + 1][0] = lax.optimization_barrier((parts, terms[n + 1][0]))
        mine = sum(part.astype(jnp.float32) for part in parts).astype(jnp.bfloat16)
        if n < CHUNKS - 1:
            mine, later = lax.optimization_barrier((mine, terms[n + 1]))
            terms[n + 1] = list(later)
        pieces.append(
            jnp.concatenate([mine] + [swap(mine, r) for r in range(1, decks)], axis=0)
        )

    def join(chosen):
        return chosen[0][0], sum((ps for _, ps, _ in chosen), []), jnp.concatenate(
            [v for _, _, v in chosen], axis=0
        )

    def to_core(n, parts, value):
        return n, [((r, 1, s), ds) for (r, _, s), ds in parts], rotate(value, "core")

    result = None
    waiting = []
    for n, piece in enumerate(pieces):
        across = rotate(piece, "side")
        along = [rotate(piece, "row", r) for r in range(1, rows)]
        near = [(n, [((0, 0, 0), every)], piece), (n, [((0, 0, 1), every)], across)]
        near += [(n, [((r, 0, 0), every)], v) for r, v in enumerate(along, 1)]
        halves = [across[: half * line]] + [v[half * line :] for v in along]
        if n > 0:
            result = put_all(result, waiting)
            halves, result = lax.optimization_barrier((halves, result))
        far = [
            (n, [((r, 0, 1), every[:half])], rotate(halves[0], "row", r)) for r in range(1, rows)
        ]
        far += [
            (n, [((r, 0, 1), every[half:])], rotate(halves[r], "side")) for r in range(1, rows)
        ]
        if n < CHUNKS - 1:
            waiting = near
            held = [(far, join(near + far))]
        else:
            first, second = join(near), []
            for values, (m, parts, joined) in held:
                joined, halves = lax.optimization_barrier((joined, halves))
                second += values + [to_core(m, parts, joined)]
            core = to_core(*first)
            result = put_all(result, second + near)
            last, result = lax.optimization_barrier(([v for _, _, v in far], result))
            far = [(n, ps, v) for (_, ps, _), v in zip(far, last)]
            result = put_all(result, [core] + far)
            result = put_all(result, [to_core(*join(far))])
    return result.reshape(width, width, width)


def solution(mesh):
    streams, spans = (mesh.shape[name] for name in ("stream", "span"))
    split = Mesh(mesh.devices.reshape(streams // 2, 2, spans // 2, 2), STREAM + SPAN)
    placed = (P(STREAM, SPAN, None, None, None), P(STREAM, SPAN, None))
    return jax.shard_map(shards, mesh=split, in_specs=placed, out_specs=P(), check_vma=False)
```

```python
import functools
import math

import jax
import jax.numpy as jnp
from jax import lax
from jax.experimental import pallas as pl
from jax.experimental.pallas import tpu as pltpu
from jax.sharding import Mesh, PartitionSpec as P

STREAM = ("row", "core")
SPAN = ("deck", "side")
DIAGONAL = ("row", "side")
WEIGHT_PARTS = 3
LANES = 128
TILE = 16
CHUNKS = 2
TURNED = (((1,), (1,)), ((), ()))


def rotate(value, axis, by=1):
    count = lax.axis_size(axis)
    return lax.ppermute(value, axis, [(i, (i + by) % count) for i in range(count)])


def swap(value, by):
    count = lax.axis_size("deck")
    assert count & (count - 1) == 0
    return lax.ppermute(value, "deck", [(i, i ^ by) for i in range(count)])


def member(where, rows, offsets):
    r, c, s = offsets
    row = lax.rem(where[0] - r + rows, rows)
    return (row * 2 + lax.rem(where[1] + c, 2)) * 2 + lax.rem(where[2] + s, 2)


def grant(shapes, slack=6 * 2**20):
    total = slack
    for shape, dtype in shapes:
        *outer, rows, columns = shape
        size = jnp.dtype(dtype).itemsize
        rows, columns = pl.cdiv(rows, TILE) * TILE, pl.cdiv(columns, LANES) * LANES
        total += math.prod(outer) * rows * columns * size
    return total


def slopes_kernel(sizes, offsets, where_ref, *refs):
    layers, height, across, width, rows = sizes
    members = len(offsets)
    blocks = refs[:members]
    turned, phi, field, *sources = refs[members:]
    count = members * layers * height * across
    depth = members // 2 * layers
    piece = 4 * count // depth
    parts = count // piece

    field[:2] = jnp.zeros_like(field[:2])
    field[members + 2 :] = jnp.zeros_like(field[members + 2 :])
    for n in range(members):
        field[member(where_ref, rows, offsets[n]) + 2] = blocks[n][...].astype(jnp.float32)
    index = lax.broadcasted_iota(jnp.int32, (across, width), 0)
    row, column = (lax.broadcasted_iota(jnp.int32, (2 * width, 2 * width), d) for d in range(2))
    eye = (row == column).astype(jnp.bfloat16)

    def stencil(x, b, source):
        def layer_at(step, side):
            at = x + step + layers
            return lax.div(at, layers) * 2 + side, lax.rem(at, layers)

        for side in range(2):
            here_at, layer = layer_at(0, side)
            at = here_at - 2
            tile = field[here_at, layer, 3 * height]
            weights = tile
            for part in range(1, WEIGHT_PARTS):
                weights = weights + pltpu.roll(tile, width - part * height, 1)
            beside = {step: layer_at(step, side) for step in (-2, -1, 1, 2)}
            found = []
            for z in range(height):
                weight = jnp.broadcast_to(weights[:, z : z + 1], (across, width))
                twelfth, half = weight * (1.0 / 12.0), weight * 0.5
                base = 2 * z // across * across
                here = field[here_at, layer, 3 * z + b]
                along = {step: field[m, l, 3 * z + b] for step, (m, l) in beside.items()}
                value_x = 8.0 * (along[1] - along[-1]) - (along[2] - along[-2])

                outer = field[here_at, layer, 3 * height + 1 + base // across * 3 + b]
                beyond = field[here_at + 1 - 2 * side, layer, 3 * z + b]
                if side == 0:
                    prev = pltpu.roll(outer, (across - 2 - (2 * z - base)) % across, 0)
                    after = beyond
                else:
                    prev = beyond
                    after = pltpu.roll(outer, (across - (2 * z - base)) % across, 0)
                near = pltpu.roll(jnp.where(index < 1, after, here), across - 1, 0)
                near = near - pltpu.roll(jnp.where(index >= across - 1, prev, here), 1, 0)
                far = pltpu.roll(jnp.where(index < 2, after, here), across - 2, 0)
                far = far - pltpu.roll(jnp.where(index >= across - 2, prev, here), 2, 0)
                value_y = 8.0 * near - far

                value_z = jnp.zeros_like(here)
                if z < height - 1:
                    value_z = field[here_at, layer, 3 * (z + 1) + b]
                if z > 0:
                    value_z = value_z - field[here_at, layer, 3 * (z - 1) + b]
                found.append((here, value_x * twelfth, value_y * twelfth, value_z * half))
                if len(found) * across == TILE:
                    start = ((at * layers + layer) * height + z + 1) * across - TILE
                    to = pl.ds(pl.multiple_of(start, TILE), TILE)
                    for q in range(4):
                        value = jnp.concatenate([f[q] for f in found], axis=0)
                        columns = slice(q % 2 * width, (q % 2 + 1) * width)
                        source[q // 2, to, columns] = value.astype(jnp.bfloat16)
                    found = []

    def turn(x, b, source):
        both, part = lax.div(x, parts), lax.rem(x, parts)
        at = pl.ds(pl.multiple_of(part * piece, piece), piece)
        value = lax.dot_general(eye, source[both, at, :], TURNED, preferred_element_type=jnp.float32)
        for n in range(2):
            turned[2 * both + n, b, :, at] = value[n * width : (n + 1) * width].astype(jnp.bfloat16)

        @pl.when(both == 0)
        def _():
            phi[b, :, at] = value[:width]

    for step in range(4):

        def two_layers(x, _):
            if step < 3:
                stencil(2 * x, step, sources[step % 2])
                stencil(2 * x + 1, step, sources[step % 2])
            if step > 0:
                turn(x, step - 1, sources[(step - 1) % 2])
            return 0

        lax.fori_loop(0, depth // 2, two_layers, 0)


def plane_slopes(where, blocks, offsets, rows, height, comps):
    layers, _, across, width = blocks[0].shape
    members = len(blocks)
    count = members * layers * height * across
    sizes = (layers, height, across, width, rows)
    vmem = pl.BlockSpec(memory_space=pltpu.VMEM)
    results = [
        ((4, comps, width, count), jnp.bfloat16),
        ((comps, width, count), jnp.float32),
    ]
    scratch = [
        ((members + 4,) + blocks[0].shape, jnp.float32),
        ((2, count, 2 * width), jnp.bfloat16),
        ((2, count, 2 * width), jnp.bfloat16),
    ]
    inputs = [(v.shape, v.dtype) for v in blocks]
    return pl.pallas_call(
        functools.partial(slopes_kernel, sizes, offsets),
        out_shape=[jax.ShapeDtypeStruct(*result) for result in results],
        in_specs=[pl.BlockSpec(memory_space=pltpu.SMEM)] + [vmem] * members,
        out_specs=[vmem] * len(results),
        scratch_shapes=[pltpu.VMEM(*shape) for shape in scratch],
        compiler_params=pltpu.CompilerParams(vmem_limit_bytes=grant(results + scratch + inputs)),
        cost_estimate=pl.CostEstimate(
            flops=2 * 12 * count * width * width, bytes_accessed=2**22, transcendentals=0
        ),
    )(where, *blocks)


def terms_kernel(share, chunk, rows, decks, where_ref, turned, phi, *refs):
    out_refs = [ref for ref in refs if len(ref.shape) == 2]
    own, *quads = refs[len(out_refs) :]
    outs = len(out_refs)
    width, count = turned.shape[2:]
    base = (member(where_ref, rows, (0, 0, 0)) * CHUNKS + chunk) * share
    each = share // decks if outs > 1 else share
    together = min(4, share)
    for i in range(share):
        mode = base + i
        if outs > 1:
            mode = base + lax.bitwise_xor(where_ref[3], i // each) * each + i % each
        for b in range(3):
            own[b, i] = jnp.broadcast_to(phi[b, pl.ds(mode, 1), :], (TILE, count))
    for group in range(share // together):
        modes = range(group * together, (group + 1) * together)
        quad = quads[group % len(quads)]
        for a in range(3):
            for start in range(0, count, LANES):
                lanes = slice(start, start + LANES)
                spread = [[own[b, mode, :, lanes] for b in range(3)] for mode in modes]
                for k in range(0, width, TILE):
                    slope = [
                        turned[1 + a, b, k : k + TILE, lanes].astype(jnp.float32) for b in range(3)
                    ]
                    for i, row in enumerate(spread):
                        value = row[0] * slope[0] + row[1] * slope[1] + row[2] * slope[2]
                        at = i * width + k
                        quad[a, at : at + TILE, lanes] = value.astype(jnp.bfloat16)
        total = sum(
            lax.dot_general(turned[0, a], quad[a], TURNED, preferred_element_type=jnp.float32)
            for a in range(3)
        )
        for i, mode in enumerate(modes):
            start = mode * width
            out_ref = out_refs[start * outs // (share * width)]
            start = start % (share * width // outs)
            out_ref[start : start + width, :] = total[:, i * width : (i + 1) * width].astype(
                out_ref.dtype
            )


def plane_terms(where, turned, phi, chunk, share, rows, decks, outs):
    width, count = turned.shape[2:]
    vmem = pl.BlockSpec(memory_space=pltpu.VMEM)
    dtypes = [jnp.float32 if outs > 1 and n == 0 else jnp.bfloat16 for n in range(outs)]
    results = [((share * width // outs, width), t) for t in dtypes]
    scratch = [((3, share, TILE, count), jnp.float32)]
    together = min(4, share)
    scratch += [((3, together * width, count), jnp.bfloat16)] * min(2, share // together)
    inputs = [(v.shape, v.dtype) for v in (turned, phi)]
    return pl.pallas_call(
        functools.partial(terms_kernel, share, chunk, rows, decks),
        out_shape=[jax.ShapeDtypeStruct(*result) for result in results],
        in_specs=[pl.BlockSpec(memory_space=pltpu.SMEM)] + [vmem] * 2,
        out_specs=[vmem] * outs,
        scratch_shapes=[pltpu.VMEM(*shape) for shape in scratch],
        compiler_params=pltpu.CompilerParams(vmem_limit_bytes=grant(results + scratch + inputs)),
        cost_estimate=pl.CostEstimate(
            flops=2 * share * width * width * count * 3, bytes_accessed=2**22, transcendentals=0
        ),
    )(where, turned, phi)


def place_kernel(plan, pieces, given, where_ref, *refs):
    rows, decks, line, runs = plan
    out_ref, wide, sems = refs[pieces + given :]
    step = math.gcd(line, LANES)
    copies = []
    for n, (piece, offsets, chunk, d, first) in enumerate(runs):
        done = n * line

        def widen(k, _):
            at = pl.multiple_of(k * step, step)
            wide[pl.ds(done + at, step), :] = refs[piece][pl.ds(first * line + at, step), :].astype(
                jnp.float32
            )
            return 0

        lax.fori_loop(0, line // step, widen, 0)
        start = (member(where_ref, rows, offsets) * CHUNKS + chunk) * decks * line
        start = start + lax.bitwise_xor(where_ref[3], d) * line
        to = pl.ds(pl.multiple_of(start, line), line)
        copies.append(
            pltpu.make_async_copy(wide.at[done : done + line], out_ref.at[to], sems.at[n])
        )
        copies[-1].start()
    for copy in copies:
        copy.wait()


def put(where, result, total_rows, rows, decks, chosen, line):
    values = [value for _, _, value in chosen]
    width = values[0].shape[1]
    runs = [
        (n, offsets, chunk, d, at)
        for n, (chunk, parts, _) in enumerate(chosen)
        for at, (offsets, d) in enumerate((o, d) for o, ds in parts for d in ds)
    ]
    given = [] if result is None else [result]
    vmem, anywhere = (pl.BlockSpec(memory_space=m) for m in (pltpu.VMEM, pl.ANY))
    wide = ((len(runs) * line, width), jnp.float32)
    return pl.pallas_call(
        functools.partial(place_kernel, (rows, decks, line, runs), len(values), len(given)),
        out_shape=jax.ShapeDtypeStruct((total_rows, width), jnp.float32),
        in_specs=[pl.BlockSpec(memory_space=pltpu.SMEM)]
        + [vmem] * len(values)
        + [anywhere] * len(given),
        out_specs=anywhere,
        scratch_shapes=[pltpu.VMEM(*wide), pltpu.SemaphoreType.DMA((len(runs),))],
        input_output_aliases={1 + len(values): 0} if given else {},
        compiler_params=pltpu.CompilerParams(
            vmem_limit_bytes=grant([wide] + [(v.shape, v.dtype) for v in values], 2**21)
        ),
        cost_estimate=pl.CostEstimate(
            flops=0, bytes_accessed=6 * wide[0][0] * width, transcendentals=0
        ),
    )(where, *values, *given)


def outer_rows(cells):
    across = cells.shape[3]
    decks = lax.axis_size("deck")
    ends = jnp.where(lax.axis_index("side") == 1, cells[..., across - 2 :, :], cells[..., :2, :])
    joints = [(2 * d + 1, 2 * d + 2) for d in range(decks - 1)]
    return lax.ppermute(ends, SPAN, joints + [(j, i) for i, j in joints])


def whole_piece(cells, outer, weight):
    layers, height, comps, across, width = cells.shape
    parts = []
    for _ in range(WEIGHT_PARTS):
        part = lax.reduce_precision(weight, 8, 7)
        weight = weight - part
        parts.append(part.astype(jnp.bfloat16))
    tile = jnp.concatenate(parts, axis=2)
    tile = jnp.pad(tile, ((0, 0), (0, 0), (0, width - tile.shape[2])))
    cells = cells.reshape(layers, height * comps, across, width)
    outer = outer.transpose(0, 1, 3, 2, 4).reshape(layers, 2 * height, comps, width)
    groups = pl.cdiv(2 * height, across)
    outer = jnp.pad(outer, ((0, 0), (0, groups * across - 2 * height), (0, 0), (0, 0)))
    outer = outer.reshape(layers, groups, across, comps, width).transpose(0, 1, 3, 2, 4)
    outer = outer.reshape(layers, groups * comps, across, width)
    return jnp.concatenate([cells, tile[:, None], outer], axis=1)


def spread_near(piece):
    rows = lax.axis_size("row")
    got = {(0, 0): piece, (0, 1): rotate(piece, "side")}
    for r in range(1, rows):
        got[(r, 0)] = rotate(piece, "row", r)
        pairs = [(2 * i + s, 2 * ((i + r) % rows) + 1 - s) for i in range(rows) for s in range(2)]
        got[(r, 1)] = lax.ppermute(piece, DIAGONAL, pairs)
    return got


def spread_cores(got):
    out = {}
    for (r, s), value in got.items():
        out[(r, 0, s)] = value
        out[(r, 1, s)] = rotate(value, "core")
    return out


def parts_over_decks(terms, decks):
    if len(terms) > 1:
        return [terms[0]] + [swap(terms[r], r) for r in range(1, decks)]
    width = terms[0].shape[1]
    return list(lax.all_to_all(terms[0].reshape(decks, -1, width), "deck", 0, 0))


def shards(velocity_modes, cell_weight):
    width = velocity_modes.shape[-1]
    rows, decks = lax.axis_size("row"), lax.axis_size("deck")
    members = rows * 4
    share = width // members // CHUNKS
    where = jnp.stack([lax.axis_index(a) for a in ("row", "core", "side", "deck")]).astype(jnp.int32)
    outs = decks if share % (2 * decks) == 0 else 1

    cells = velocity_modes.transpose(0, 2, 3, 1, 4)
    blocks = spread_cores(spread_near(whole_piece(cells, outer_rows(cells), cell_weight)))
    offsets = list(blocks)
    height, comps = cells.shape[1:3]
    slopes = plane_slopes(where, list(blocks.values()), offsets, rows, height, comps)
    terms = [
        list(plane_terms(where, *slopes, n, share, rows, decks, outs)) for n in range(CHUNKS)
    ]

    line = share * width // decks
    every = range(decks)
    half = decks // 2

    def put_all(result, chosen):
        return put(where, result, width * width, rows, decks, chosen, line)

    pieces = []
    for n in range(CHUNKS):
        parts = parts_over_decks(terms[n], decks)
        if n < CHUNKS - 1:
            parts, terms[n + 1][0] = lax.optimization_barrier((parts, terms[n + 1][0]))
        mine = sum(part.astype(jnp.float32) for part in parts).astype(jnp.bfloat16)
        if n < CHUNKS - 1:
            mine, later = lax.optimization_barrier((mine, terms[n + 1]))
            terms[n + 1] = list(later)
        pieces.append([mine] + [swap(mine, r) for r in range(1, decks)])

    def join(chosen):
        return chosen[0][0], sum((ps for _, ps, _ in chosen), []), jnp.concatenate(
            [v for _, _, v in chosen], axis=0
        )

    def to_core(n, parts, value):
        return n, [((r, 1, s), ds) for (r, _, s), ds in parts], rotate(value, "core")

    result = None
    waiting = []
    for n, runs in enumerate(pieces):
        piece = jnp.concatenate(runs, axis=0)
        across = rotate(piece, "side")
        along = [rotate(piece, "row", r) for r in range(1, rows)]
        near = [(n, [((0, 0, 0), every)], piece), (n, [((0, 0, 1), every)], across)]
        near += [(n, [((r, 0, 0), every)], v) for r, v in enumerate(along, 1)]
        halves = [across[: half * line]] + [v[half * line :] for v in along]
        if n < CHUNKS - 1:
            halves, pieces[n + 1][0] = lax.optimization_barrier((halves, pieces[n + 1][0]))
        if n > 0:
            result = put_all(result, waiting)
            halves, result = lax.optimization_barrier((halves, result))
        far = [
            (n, [((r, 0, 1), every[:half])], rotate(halves[0], "row", r)) for r in range(1, rows)
        ]
        far += [
            (n, [((r, 0, 1), every[half:])], rotate(halves[r], "side")) for r in range(1, rows)
        ]
        if n < CHUNKS - 1:
            waiting = near
            held = [(far, join(near + far))]
        else:
            first, second = join(near), []
            for values, (m, parts, joined) in held:
                joined, halves = lax.optimization_barrier((joined, halves))
                second += values + [to_core(m, parts, joined)]
            core = to_core(*first)
            result = put_all(result, second + near)
            last, result = lax.optimization_barrier(([v for _, _, v in far], result))
            far = [(n, ps, v) for (_, ps, _), v in zip(far, last)]
            result = put_all(result, [core] + far)
            result = put_all(result, [to_core(*join(far))])
    return result.reshape(width, width, width)


def solution(mesh):
    streams, spans = (mesh.shape[name] for name in ("stream", "span"))
    split = Mesh(mesh.devices.reshape(streams // 2, 2, spans // 2, 2), STREAM + SPAN)
    placed = (P(STREAM, SPAN, None, None, None), P(STREAM, SPAN, None))
    return jax.shard_map(shards, mesh=split, in_specs=placed, out_specs=P(), check_vma=False)
```
